512 devices in a mesh: strip: 128 (over z, x, core), col: 4 (over y).
Axes of the slice: x: 4, y: 4, z: 16, core: 2. Of those that a mesh axis runs over, the one named last changes fastest.
Arguments:
- positions: float32 [3, 1024, 1024], P(None, 'strip', 'col'), may hold values from -1.8 to 1.8
- target: float32 [3, 1024, 1024], P(None, 'strip', 'col'), may hold values from -1.8 to 1.8
- inertia: float32 [1024, 1024], P('strip', 'col'), may hold values from 1 to 4
- stiffness: float32 [3, 1024, 1024], P(None, 'strip', 'col'), may hold values from 0.5 to 2
- pin_columns: int32 [64], replicated, may hold values from 0 to 1023
- inverses: bfloat16 [512, 512, 512], P('strip'), may hold values from -0.05 to 0.55
Outputs:
- displaced: float32 [3, 1024, 1024], P(None, 'strip', 'col')
The draws below stay inside these ranges and needn't reach their ends.
Inputs may be any that keep to these rules, and one draw needn't show every extreme that they name: `pin_columns`: a column may appear more than once.
All inputs are finite; a program needn't handle non-finite values.
Results may differ from the reference program's by a relative error of at most 0.0003.
Values sent between devices are 32-bit elements; how exact they have to be, the bound alone decides.
No kernel may reach another device: no remote copies, remote signals or barrier semaphores. Data moves between devices by JAX's collectives and lax.ppermute only.
A program may use at most 128 MiB of HBM per device.

```python
import math
import jax
import jax.numpy as jnp
from jax import lax

COL_DEV = 256
SROWS = 2
ITERS = 2
PINS = 64
NR = 1024
NC = 1024
STRIPS = 512
N_COL = 4


def spring_field(key):
    keyed = jax.random.fold_in(key, 999983)
    field = jnp.exp(jax.random.uniform(keyed, (3, NR, NC), jnp.float32, math.log(0.5), math.log(2.0)))
    field = jnp.clip(field, 0.5, 2.0)
    carry_key = jax.random.fold_in(key, 999979)
    carry_rows = jax.random.uniform(carry_key, (NR // SROWS, NC), jnp.float32, 1.98, 2.0)
    return field.at[1, SROWS - 1::SROWS, :].set(carry_rows)


def draw_stiffness(key, part):
    return spring_field(key)


def draw_inverses(key, part):
    block_size = SROWS * COL_DEV
    strip_gain = 0.985
    carry_weights = spring_field(key)[1, SROWS - 1::SROWS, :]
    weight_means = jnp.mean(carry_weights, axis=1)
    places = jnp.arange(COL_DEV, dtype=jnp.float32)
    kernel = jnp.exp(-jnp.abs(places[:, None] - places[None, :]) / 8.0)
    kernel = kernel / jnp.sum(kernel, axis=1, keepdims=True)
    beside = jnp.eye(SROWS, k=1, dtype=jnp.float32) + jnp.eye(SROWS, k=-1, dtype=jnp.float32)
    own = 0.08 * jnp.eye(SROWS, dtype=jnp.float32)
    own_part = jnp.kron(own, kernel)
    beside_part = jnp.kron(beside, jnp.eye(COL_DEV, dtype=jnp.float32))

    def one_block(number):
        keyed = jax.random.fold_in(key, number)
        key_diag, key_jitter = jax.random.split(keyed)
        carried = strip_gain / weight_means[number]
        structure = own_part + carried * beside_part
        diagonal = jax.random.uniform(key_diag, (block_size,), jnp.float32, 0.05, 0.1)
        jitter = jnp.clip(jax.random.normal(key_jitter, (block_size, block_size), jnp.float32), -4.0, 4.0)
        jitter = jitter * (0.05 / block_size ** 0.5)
        return (structure + jnp.diag(diagonal) + jitter).astype(jnp.bfloat16)
    return lax.map(one_block, jnp.arange(STRIPS))


def place_ends(values, own_key, least, largest):
    longest = values.shape.index(max(values.shape))
    spots = []
    for shift in (0, 1):
        where = [jax.random.randint(jax.random.fold_in(own_key, axis), (), 0, length) for axis, length in enumerate(values.shape)]
        where[longest] = (where[longest] + shift) % values.shape[longest]
        spots.append(tuple(where))
    return values.at[spots[0]].set(least).at[spots[1]].set(largest)


def shard_levels(key, dims, cuts, smallest, high):
    loudness = 1.0
    for dim, parts in cuts:
        draws = jax.random.uniform(jax.random.fold_in(jax.random.fold_in(key, 6), dim), (parts,), jnp.float32, smallest / len(cuts), high / len(cuts))
        loudness = loudness * jnp.repeat(jnp.exp(draws), dims[dim] // parts).reshape((-1,) + (1,) * (len(dims) - 1 - dim))
    return loudness


def centred(key, extent, width, bound, cuts=(), kind=jnp.bfloat16):
    values = jax.random.normal(key, extent, jnp.float32) * width
    if len(cuts) > 0:
        values = shard_levels(key, extent, cuts, -0.22, 0.18) * values
    return jnp.clip(values, min=-bound, max=bound).astype(kind)


def setup_inputs(seed: int = 0) -> dict:
    seeds = jax.random.split(jax.random.key(seed), 7)
    positions = centred(seeds[0], (3, NR, NC), 0.3, 1.8, ((1, 128), (2, 4)), jnp.float32)
    target = centred(seeds[1], (3, NR, NC), 0.3, 1.8, ((1, 128), (2, 4)), jnp.float32)
    inertia = jnp.clip(jnp.exp(math.log(4.0) - 1.3862944 * jax.random.uniform(seeds[2], (NR, NC), jnp.float32) ** shard_levels(seeds[2], (NR, NC), ((0, 128), (1, 4)), -0.2, 0.2)), 1.0, 4.0)
    stiffness = draw_stiffness(jax.random.fold_in(seeds[6], 71), 0)
    pin_columns = place_ends(jax.random.randint(seeds[4], (PINS,), 0, NC), jax.random.fold_in(seeds[4], 1), 0, NC - 1).astype(jnp.int32)
    inverses = draw_inverses(jax.random.fold_in(seeds[6], 71), 0)
    return {"positions": positions, "target": target, "inertia": inertia, "stiffness": stiffness, "pin_columns": pin_columns, "inverses": inverses}


pin_stiffness = 20.0
highest = lax.Precision.HIGHEST

def times_transposed(rows_in, matrix):
    return lax.dot_general(rows_in, matrix, (((rows_in.ndim - 1,), (1,)), ((), ())), precision=highest, preferred_element_type=jnp.float32)

def axis_vector(offset, direction):
    entries = [0.0, 0.0, 0.0]
    entries[direction] = float(offset)
    return jnp.array(entries, jnp.float32).reshape(3, 1, 1)

def edge_force(top_side, low_side, weight, rest_vec, rest_len):
    spacing = rest_vec + low_side - top_side
    length = jnp.sqrt(lax.optimization_barrier(jnp.sum(spacing * spacing, axis=0, keepdims=True)))
    projected = rest_len * spacing / jnp.maximum(length, 0.5 * rest_len)
    return weight[None] * (projected - rest_vec)

def spring_forces(displaced, stiffness):
    summed = jnp.zeros_like(displaced)
    for offset, channel in ((1, 0), (2, 2)):
        pulling = edge_force(displaced[:, :, :-offset], displaced[:, :, offset:], stiffness[channel][:, :-offset], axis_vector(offset, 0), float(offset))
        summed = summed.at[:, :, :-offset].add(-pulling)
        summed = summed.at[:, :, offset:].add(pulling)
    pulling = edge_force(displaced[:, :-1, :], displaced[:, 1:, :], stiffness[1][:-1, :], axis_vector(1, 1), 1.0)
    summed = summed.at[:, :-1, :].add(-pulling)
    return summed.at[:, 1:, :].add(pulling)

def block_coupling(displaced, stiffness):
    coupled = jnp.zeros_like(displaced)
    for offset, channel in ((1, 0), (2, 2)):
        left_cols = jnp.arange(NC - offset, dtype=jnp.int32)
        crossing = (left_cols + offset) // COL_DEV != left_cols // COL_DEV
        cross_weight = jnp.where(crossing[None, :], stiffness[channel][:, :-offset], 0.0)
        coupled = coupled.at[:, :, :-offset].add(cross_weight[None] * displaced[:, :, offset:])
        coupled = coupled.at[:, :, offset:].add(cross_weight[None] * displaced[:, :, :-offset])
    row_ids = jnp.arange(NR - 1, dtype=jnp.int32)
    down_weight = jnp.where((row_ids % SROWS == SROWS - 1)[:, None], stiffness[1][:-1], 0.0)
    return coupled.at[:, :-1, :].add(down_weight[None] * displaced[:, 1:, :])

def gauss_seidel(rhs_field, stiffness, inverses):
    last_start = (SROWS - 1) * COL_DEV
    rhs_blocks = rhs_field.reshape(3, STRIPS, SROWS, N_COL, COL_DEV).transpose(1, 3, 0, 2, 4)
    rhs_blocks = rhs_blocks.reshape(STRIPS, N_COL, 3, SROWS * COL_DEV)
    weights_last = stiffness[1][SROWS - 1::SROWS].at[-1].set(0.0).reshape(STRIPS, N_COL, 1, COL_DEV)

    def advance(carried, inputs):
        rhs_strip, inverse, weight_row = inputs
        placed = jnp.pad(carried, ((0, 0), (0, 0), (0, last_start)))
        solved = times_transposed(rhs_strip + placed, inverse.astype(jnp.float32))
        return (weight_row * solved[:, :, last_start:], solved)
    start = jnp.zeros((N_COL, 3, COL_DEV), jnp.float32)
    unused, solved_all = lax.scan(advance, start, (rhs_blocks, inverses, weights_last))
    solved_all = solved_all.reshape(STRIPS, N_COL, 3, SROWS, COL_DEV).transpose(2, 0, 3, 1, 4)
    return solved_all.reshape(3, NR, NC)

def reference(positions, target, inertia, stiffness, pin_columns, inverses):
    pinned = jnp.any(pin_columns[:, None] == jnp.arange(NC, dtype=jnp.int32)[None, :], axis=0)
    pinned_row = jnp.where(pinned[None, :], positions[:, 0, :], 0.0)
    anchor = jnp.zeros_like(positions).at[:, 0, :].set(pinned_row)
    inertial = inertia[None] * target + pin_stiffness * anchor
    displaced = positions
    for sweep_number in range(ITERS):
        rhs_field = inertial + spring_forces(displaced, stiffness) + block_coupling(displaced, stiffness)
        displaced = gauss_seidel(rhs_field, stiffness, inverses)
    return displaced
```

```python
import jax
import jax.numpy as jnp
from jax import lax
from jax.experimental import pallas as pl
from jax.experimental.pallas import tpu as pltpu
from jax.sharding import Mesh
from jax.sharding import PartitionSpec as P

F32 = jnp.float32
BF16 = jnp.bfloat16
STRIP = ("zh", "zl", "x", "c")
ZAX = ("zh", "zl")
PLANE = ("x", "c")
SIDES = ("c", "y")
CB = 256
PIN = 20.0
VMEM_LIMIT = 14 * 1024 * 1024


def dot(a, b):
    return lax.dot_general(a, b, (((1,), (0,)), ((), ())), preferred_element_type=F32)


def dot_t(a, b):
    return lax.dot_general(a, b, (((1,), (1,)), ((), ())), preferred_element_type=F32)


def pair(value):
    high = value.astype(BF16)
    low = (value - high.astype(F32)).astype(BF16)
    return high, low


def mm(a, b):
    return dot(a[0], b[0]) + (dot(a[0], b[1]) + dot(a[1], b[0]))


def eye():
    rows = lax.broadcasted_iota(jnp.int32, (CB, CB), 0)
    cols = lax.broadcasted_iota(jnp.int32, (CB, CB), 1)
    return jnp.where(rows == cols, 1.0, 0.0).astype(F32)


def stacked(value):
    high = value.astype(BF16)
    low = value - high.astype(F32)
    return jnp.concatenate([high.astype(F32), low], axis=0).astype(BF16)


def halves_sum(value):
    half = value.shape[0] // 2
    return value[:half] + value[half:]


def put_vector(vec_ref, slot, value):
    high = value.astype(BF16).astype(F32)
    vec_ref[0:3, slot * CB : (slot + 1) * CB] = high
    vec_ref[8:11, slot * CB : (slot + 1) * CB] = value - high


def apply_map(vec, high, low):
    return halves_sum(dot(vec, high) + dot(vec, low))


def call(kernel, outs, args, specs=None, scratch=(), flops=10**7, size=10**6, grid=None):
    vmem = pl.BlockSpec(memory_space=pltpu.VMEM)
    in_specs = [vmem] * len(args) if specs is None else [vmem if s is None else s for s in specs]
    many = isinstance(outs, (list, tuple))
    out_specs = [vmem] * len(outs) if many else vmem
    extra = {} if grid is None else {"grid": grid}
    return pl.pallas_call(
        kernel,
        out_shape=outs,
        in_specs=in_specs,
        out_specs=out_specs,
        scratch_shapes=list(scratch),
        compiler_params=pltpu.CompilerParams(vmem_limit_bytes=VMEM_LIMIT),
        cost_estimate=pl.CostEstimate(flops=flops, bytes_accessed=size, transcendentals=0),
        **extra,
    )(*args)


def sds(shape, dtype=F32):
    return jax.ShapeDtypeStruct(shape, dtype)


def local_map_kernel(inv_ref, stiff_ref, out_ref):
    first = dot_t(eye().astype(BF16), inv_ref[0]) * stiff_ref[1, 1:2, :]
    for k in range(1, 4):
        high, low = pair(first)
        first = (dot_t(high, inv_ref[k]) + dot_t(low, inv_ref[k])) * stiff_ref[
            1, 2 * k + 1 : 2 * k + 2, :
        ]
    out_ref[...] = first


def chip_map_kernel(both_ref, out_ref):
    product = mm(pair(both_ref[0]), pair(both_ref[1]))
    for k in range(4):
        out_ref[k] = product


def plane_product_kernel(chips_ref, *rest):
    out_ref = rest[-1]
    left = mm(pair(chips_ref[0]), pair(chips_ref[1]))
    right = mm(pair(chips_ref[2]), pair(chips_ref[3]))
    out_ref[...] = mm(pair(left), pair(right))


def low_bit():
    return lax.rem(lax.axis_index("zl"), 2)


def high_bit():
    return lax.div(lax.axis_index("zl"), 2)


def two_planes_kernel(own_ref, other_ref, *rest):
    out_ref = rest[-1]
    right = low_bit() == 1
    left_map = jnp.where(right, other_ref[...], own_ref[...])
    right_map = jnp.where(right, own_ref[...], other_ref[...])
    out_ref[...] = mm(pair(left_map), pair(right_map))


def four_planes_kernel(own_ref, other_ref, *rest):
    out_ref = rest[-1]
    right = high_bit() == 1
    start = pl.multiple_of(lax.axis_index("c") * 128, 128)
    own, other = own_ref[pl.ds(start, 128), :], other_ref[pl.ds(start, 128), :]
    left_map = jnp.where(right, other, own)
    right_map = jnp.where(right, own_ref[...], other_ref[...])
    out_ref[...] = mm(pair(left_map), pair(right_map))


def plane_maps_kernel(chips_ref, cores_ref, after_ref, wh_ref, wl_ref, eh_ref, el_ref, suf_ref, cur_ref):
    x = lax.axis_index("x")
    core = lax.axis_index("c")
    one = eye()
    chips = [pair(chips_ref[k]) for k in range(4)]

    def store(slot, col, value):
        high, low = pair(value)
        wh_ref[slot * CB : (slot + 1) * CB, col * CB : (col + 1) * CB] = high
        wl_ref[slot * CB : (slot + 1) * CB, col * CB : (col + 1) * CB] = low

    suffix = one
    suf_ref[3] = suffix
    store(3, 0, suffix)
    for k in (2, 1, 0):
        if k == 2:
            suffix = chips_ref[3]
        else:
            suffix = mm(chips[k + 1], pair(suffix))
        suf_ref[k] = suffix
        store(k, 0, suffix)
    store(4, 0, mm(pair(cores_ref[1]), pair(suf_ref[x])))
    store(4, 1, jnp.where(core == 1, one, 0.0))
    cur_ref[...] = jnp.where(core == 1, cores_ref[0], one)
    for k in (3, 2, 1, 0):

        @pl.when(k < x)
        def _():
            current = cur_ref[...]
            store(k, 1, current)
            cur_ref[...] = mm(chips[k], pair(current))

        @pl.when(k >= x)
        def _():
            store(k, 1, jnp.zeros((CB, CB), F32))

    high, low = pair(cur_ref[...])
    eh_ref[...] = high
    el_ref[...] = low


def group_maps_kernel(one_ref, two_ref, after_ref, out_ref, s_ref, e_ref):
    one = eye()
    sibling = one_ref[...]
    two = pair(two_ref[...])
    send = jnp.where(low_bit() == 0, sibling, one)
    take = jnp.where(low_bit() == 1, sibling, one)
    for k, value in ((0, send), (4, take)):
        parts = pair(value)
        out_ref[k] = parts[0]
        out_ref[k + 1] = parts[1]
    send = jnp.where(high_bit() == 0, mm(pair(send), two), send)
    take = jnp.where(high_bit() == 1, mm(two, pair(take)), take)
    for k, value in ((2, send), (6, take)):
        parts = pair(value)
        out_ref[k] = parts[0]
        out_ref[k + 1] = parts[1]
    s_ref[...] = send
    e_ref[...] = take


def joint_map(far_ref, s_ref, e_ref, out_ref):
    zh = lax.axis_index("zh")
    far = jnp.concatenate([far_ref[0], far_ref[1]], axis=0)
    left = jnp.where(zh == 0, s_ref[...], far)
    right = jnp.where(zh == 0, far, e_ref[...])
    joint = pair(mm(pair(left), pair(right)))
    out_ref[0] = joint[0]
    out_ref[1] = joint[1]


def edge_tiles(comps, weights):
    lane = lax.broadcasted_iota(jnp.int32, (8, 128), 1)
    right = jnp.zeros((8, 128), F32)
    left = jnp.zeros((8, 128), F32)
    for k, value in enumerate(comps + weights):
        mask = (lane == 2 * k) | (lane == 2 * k + 1)
        right = jnp.where(mask, pltpu.roll(value[:, 128:], (2 * k - 126) % 128, 1), right)
        if k < 3:
            left = jnp.where(mask, pltpu.roll(value[:, :128], 2 * k, 1), left)
    return left, right


def put_rows(out_ref, index, rows):
    for k in range(len(rows)):
        for h in range(2):
            spot = (slice(2 * k + h, 2 * k + h + 1), slice(None))
            out_ref[index + spot] = rows[k][:, 128 * h : 128 * (h + 1)]


def halo_kernel(u_ref, stiff_ref, after_ref, left_ref, right_ref, near_ref, cross_ref):
    core = lax.axis_index("c")
    comps = [u_ref[k] for k in range(3)]
    left, right = edge_tiles(comps, [stiff_ref[0], stiff_ref[2]])
    left_ref[...] = left
    right_ref[...] = right
    rows = comps + [stiff_ref[1]]
    put_rows(near_ref, (), [jnp.where(core == 0, r[7:8], r[0:1]) for r in rows])
    put_rows(cross_ref, (), [jnp.where(core == 0, r[0:1], r[7:8]) for r in rows])


def write_halos(comps, side_ref, row_ref):
    core = lax.axis_index("c")
    y = lax.axis_index("y")
    left, right = edge_tiles(comps, [])
    for j in range(8):
        side_ref[j] = jnp.zeros((8, 128), F32)
    side_ref[core * 4 + lax.rem(y + 1, 4)] = right
    side_ref[core * 4 + lax.rem(y + 3, 4)] = left
    rows = [c[0:1] for c in comps] + [jnp.zeros((1, CB), F32)]
    put_rows(side_ref, ((1 - core) * 4 + y,), rows)
    put_rows(row_ref, (), rows)


def row_of(tile, k):
    return jnp.concatenate([tile[2 * k : 2 * k + 1], tile[2 * k + 1 : 2 * k + 2]], axis=1)


def springs(ends, others, weight, rest, length):
    gaps = [o - e for o, e in zip(others, ends)]
    gaps = [g + r if r != 0.0 else g for g, r in zip(gaps, rest)]
    norm = jnp.sqrt(gaps[0] * gaps[0] + gaps[1] * gaps[1] + gaps[2] * gaps[2])
    factor = length / jnp.maximum(norm, 0.5 * length)
    return [weight * (g * factor - r if r != 0.0 else g * factor) for g, r in zip(gaps, rest)]


def solve_right_side(
    comps, inertial, from_left, from_right, below_rows, above_rows, above_weight, h_ext, b_ext,
    vertical, stiff_ref, inv_ref, base_ref,
):
    row = lax.broadcasted_iota(jnp.int32, (8, CB), 0)
    lane = lax.broadcasted_iota(jnp.int32, (8, 512), 1)
    wide = []
    for k in range(3):
        head = pltpu.roll(from_left, 126 - 2 * k, 1)
        tail = pltpu.roll(from_right, (-2 * k) % 128, 1) if k else from_right
        wide.append(jnp.concatenate([head, comps[k], tail], axis=1))
    total = [jnp.zeros((8, 512), F32)] * 3
    for offset, weight in ((1, h_ext), (2, b_ext)):
        shifted = [pltpu.roll(w, 512 - offset, 1) for w in wide]
        rest = (float(offset), 0.0, 0.0)
        pulls = springs(wide, shifted, weight, rest, float(offset))
        crossing = ((lane >= 128 - offset) & (lane < 128)) | (
            (lane >= 384 - offset) & (lane < 384)
        )
        across = jnp.where(crossing, weight, 0.0)
        for k in range(3):
            here = across * shifted[k] - pulls[k]
            there = across * wide[k] + pulls[k]
            total[k] = total[k] + here + pltpu.roll(there, offset, 1)
    lower = [
        jnp.where(row == 7, below_rows[k], pltpu.roll(comps[k], 7, 0)) for k in range(3)
    ]
    down = springs(comps, lower, vertical, (0.0, 1.0, 0.0), 1.0)
    upper = springs(
        above_rows, [c[0:1] for c in comps], above_weight, (0.0, 1.0, 0.0), 1.0
    )
    below_weight = jnp.where(lax.rem(row, 2) == 1, vertical, 0.0)
    rhs = []
    for k in range(3):
        received = jnp.where(row == 0, upper[k], pltpu.roll(down[k], 1, 0))
        rhs.append(
            inertial[k] + total[k][:, 128:384] + received - down[k] + below_weight * lower[k]
        )
    first = jnp.concatenate(rhs + [jnp.zeros((8, CB), F32)], axis=0)
    second = jnp.concatenate(
        [pltpu.roll(r, 7, 0) for r in rhs] + [jnp.zeros((8, CB), F32)], axis=0
    )
    wide_rhs = stacked(jnp.concatenate([first, second], axis=1))
    base = [jnp.zeros((8, CB), F32)] * 3
    for k in range(4):
        solved = halves_sum(dot_t(wide_rhs, inv_ref[k]))
        for j in range(3):
            part = solved[8 * j : 8 * j + 8]
            base[j] = jnp.where(
                row == 2 * k,
                part[:, :CB],
                jnp.where(row == 2 * k + 1, pltpu.roll(part[:, CB:], 1, 0), base[j]),
            )
    for j in range(3):
        base_ref[j] = base[j]
    weights = stiff_ref[1]
    last = base
    for k in range(1, 4):
        carried = jnp.concatenate(
            [weights * last[j] for j in range(3)] + [jnp.zeros((8, CB), F32)], axis=0
        )
        moved = halves_sum(dot_t(stacked(carried), inv_ref[k, CB:, :CB]))
        last = [
            jnp.where(row == 2 * k + 1, base[j] + pltpu.roll(moved[8 * j : 8 * j + 8], 2, 0), last[j])
            for j in range(3)
        ]
    rows = [(weights * last[j])[7:8] for j in range(3)]
    return jnp.concatenate(rows + [jnp.zeros((5, CB), F32)], axis=0)


def write_offsets(offset, chip_ref, msg_ref):
    core = lax.axis_index("c")
    x = lax.axis_index("x")
    chip = pair(chip_ref[1])
    onward = apply_map(stacked(offset), chip[0], chip[1])[0:3]
    raw = offset[0:3]
    onward = jnp.where(core == 0, onward, raw)
    for j in range(8):
        msg_ref[j] = jnp.where(x == j // 2, raw, onward)


def offsets_kernel(offset_ref, chip_ref, after_ref, msg_ref):
    write_offsets(offset_ref[...], chip_ref, msg_ref)


def first_side_kernel(
    u_ref, target_ref, inertia_ref, stiff_ref, pin_ref, left_ref, right_ref, near_ref, cross_ref,
    inv_ref, after_ref, base_ref, offset_ref, inertial_ref, ext_ref, above_ref,
):
    core = lax.axis_index("c")
    y = lax.axis_index("y")
    strip = (lax.axis_index("zh") * 4 + lax.axis_index("zl")) * 8 + lax.axis_index("x") * 2 + core
    comps = [u_ref[k] for k in range(3)]
    row = lax.broadcasted_iota(jnp.int32, (8, CB), 0)
    column = lax.broadcasted_iota(jnp.int32, (8, CB), 1) + y * CB
    hit = column < 0
    for k in range(pin_ref.shape[0]):
        hit = hit | (column == pin_ref[k])
    pinned = hit & (row == 0) & (strip == 0)
    inertial = []
    for k in range(3):
        value = inertia_ref[...] * target_ref[k] + PIN * jnp.where(pinned, comps[k], 0.0)
        inertial.append(value)
        inertial_ref[k] = value
    lane = lax.broadcasted_iota(jnp.int32, (8, 512), 1)
    from_left = left_ref[...]
    extended = []
    for k, channel, offset in ((3, 0, 1), (4, 2, 2)):
        head = pltpu.roll(from_left, 126 - 2 * k, 1)
        weight = jnp.concatenate([head, stiff_ref[channel], jnp.zeros((8, 128), F32)], axis=1)
        low = jnp.where(y == 0, 128, 128 - offset)
        high = jnp.where(y == 3, 384 - offset, 384)
        weight = jnp.where((lane >= low) & (lane < high), weight, 0.0)
        extended.append(weight)
        ext_ref[k - 3] = weight
    above = jnp.where(core == 0, cross_ref[...], near_ref[...])
    below = jnp.where(core == 0, near_ref[...], cross_ref[...])
    above_weight = jnp.where(strip == 0, 0.0, row_of(above, 3))
    above_ref[...] = jnp.broadcast_to(above_weight, (8, CB))
    vertical = jnp.where((row == 7) & (strip == 127), 0.0, stiff_ref[1])
    offset_ref[...] = solve_right_side(
        comps, inertial, from_left, right_ref[...], [row_of(below, k) for k in range(3)],
        [row_of(above, k) for k in range(3)], above_weight, extended[0], extended[1], vertical,
        stiff_ref, inv_ref, base_ref,
    )


def second_side_kernel(
    u_ref, stiff_ref, side_ref, row_ref, inv_ref, chip_ref, inertial_ref, ext_ref, above_ref,
    base_ref, msg_ref,
):
    core = lax.axis_index("c")
    y = lax.axis_index("y")
    strip = (lax.axis_index("zh") * 4 + lax.axis_index("zl")) * 8 + lax.axis_index("x") * 2 + core
    comps = [u_ref[k] for k in range(3)]
    row = lax.broadcasted_iota(jnp.int32, (8, CB), 0)
    partner = side_ref[(1 - core) * 4 + y]
    below = jnp.where(core == 0, partner, row_ref[...])
    above_weight = above_ref[0:1, :]
    divisor = jnp.where(strip == 0, 1.0, above_weight)
    above_rows = [u_ref[3, k : k + 1, :] / divisor for k in range(3)]
    vertical = jnp.where((row == 7) & (strip == 127), 0.0, stiff_ref[1])
    from_left = side_ref[core * 4 + lax.rem(y + 3, 4)]
    from_right = side_ref[core * 4 + lax.rem(y + 1, 4)]
    offset = solve_right_side(
        comps, [inertial_ref[k] for k in range(3)], from_left, from_right,
        [row_of(below, k) for k in range(3)], above_rows, above_weight, ext_ref[0], ext_ref[1],
        vertical, stiff_ref, inv_ref, base_ref,
    )
    write_offsets(offset, chip_ref, msg_ref)


def plane_vectors(got_ref, wh_ref, wl_ref, vec_ref):
    x = lax.axis_index("x")
    vec_ref[...] = jnp.zeros(vec_ref.shape, F32)
    for k in range(4):
        own = got_ref[2 * k + 1]
        put_vector(vec_ref, k, jnp.where(x == k, own, own + got_ref[2 * k]))
    put_vector(vec_ref, 4, got_ref[2 * x])
    return apply_map(vec_ref[...].astype(BF16), wh_ref[...], wl_ref[...])


def send_vectors(total, maps_ref, joint_ref, msg_ref):
    zh = lax.axis_index("zh")
    vec = stacked(total)
    pairs = apply_map(vec, maps_ref[0], maps_ref[1])[0:3]
    near = apply_map(vec, maps_ref[2], maps_ref[3])[0:3]
    far = apply_map(vec, joint_ref[0], joint_ref[1])[0:3]
    far = jnp.where(zh == 0, far, near)
    raw = total[0:3]
    for g in range(4):
        for h in range(2):
            inner = jnp.where(high_bit() == h, raw, pairs)
            value = jnp.where(zh == g, inner, near if g < 2 else far)
            msg_ref[4 * g + 2 * h] = value
            msg_ref[4 * g + 2 * h + 1] = value


def plane_kernel(got_ref, wh_ref, wl_ref, both_ref, vec_ref):
    both_ref[...] = plane_vectors(got_ref, wh_ref, wl_ref, vec_ref)


def send_kernel(both_ref, maps_ref, far_ref, s_ref, e_ref, joint_ref, msg_ref):
    joint_map(far_ref, s_ref, e_ref, joint_ref)
    send_vectors(both_ref[:, :CB], maps_ref, joint_ref, msg_ref)


def plane_send_kernel(got_ref, wh_ref, wl_ref, maps_ref, joint_ref, both_ref, msg_ref, vec_ref):
    both = plane_vectors(got_ref, wh_ref, wl_ref, vec_ref)
    both_ref[...] = both
    send_vectors(both[:, :CB], maps_ref, joint_ref, msg_ref)


def finish(
    got_ref, both_ref, maps_ref, joint_ref, eh_ref, el_ref, stiff_ref, base_ref, inv_ref, vec_ref
):
    zh = lax.axis_index("zh")
    row = lax.broadcasted_iota(jnp.int32, (8, CB), 0)
    none = jnp.zeros((3, CB), F32)
    vec_ref[...] = jnp.zeros(vec_ref.shape, F32)
    first_two = got_ref[4 * zh] + got_ref[4 * zh + 1]
    put_vector(vec_ref, 0, jnp.where(high_bit() == 1, first_two, none))
    sums = [
        (got_ref[4 * g] + got_ref[4 * g + 1]) + (got_ref[4 * g + 2] + got_ref[4 * g + 3])
        for g in range(3)
    ]
    lower = jnp.where(zh >= 1, sums[0], none) + jnp.where(zh >= 2, sums[1], none)
    put_vector(vec_ref, 1, jnp.where(zh == 3, sums[2], lower))
    put_vector(vec_ref, 2, jnp.where(zh == 3, lower, none))
    vec = vec_ref[...].astype(BF16)
    arrived = apply_map(vec[:, :CB], maps_ref[4], maps_ref[5])
    arrived = arrived + apply_map(vec[:, CB : 2 * CB], maps_ref[6], maps_ref[7])
    arrived = arrived + apply_map(vec[:, 2 * CB :], joint_ref[0], joint_ref[1])
    beside = jnp.where(low_bit() == 1, got_ref[4 * zh + 2 * high_bit()], none)
    arrived = arrived + jnp.concatenate([beside, jnp.zeros((5, CB), F32)], axis=0)
    came = both_ref[:, CB:] + apply_map(stacked(arrived), eh_ref[...], el_ref[...])
    weights = stiff_ref[1]
    state = [base_ref[k] for k in range(3)]
    blank = jnp.zeros((8, CB), F32)
    for k in range(4):
        if k == 0:
            source = [jnp.broadcast_to(came[j : j + 1], (8, CB)) for j in range(3)]
        else:
            source = [weights * state[j] for j in range(3)]
        moved = halves_sum(dot_t(stacked(jnp.concatenate(source + [blank], axis=0)), inv_ref[k]))
        for j in range(3):
            part = moved[8 * j : 8 * j + 8]
            state[j] = state[j] + jnp.where(
                row == 2 * k,
                pltpu.roll(part[:, :CB], 1, 0),
                jnp.where(row == 2 * k + 1, pltpu.roll(part[:, CB:], 2, 0), 0.0),
            )
    return state, came


def middle_kernel(
    got_ref, both_ref, maps_ref, joint_ref, eh_ref, el_ref, stiff_ref, base_ref, inv_ref,
    u_ref, side_ref, row_ref, vec_ref,
):
    state, came = finish(
        got_ref, both_ref, maps_ref, joint_ref, eh_ref, el_ref, stiff_ref, base_ref, inv_ref, vec_ref
    )
    for k in range(3):
        u_ref[k] = state[k]
    u_ref[3] = came
    write_halos(state, side_ref, row_ref)


def final_kernel(
    got_ref, both_ref, maps_ref, joint_ref, eh_ref, el_ref, stiff_ref, base_ref, inv_ref,
    u_ref, vec_ref,
):
    state, came = finish(
        got_ref, both_ref, maps_ref, joint_ref, eh_ref, el_ref, stiff_ref, base_ref, inv_ref, vec_ref
    )
    for k in range(3):
        u_ref[k] = state[k]


def swap(value, axes):
    return lax.all_to_all(value, axes, 0, 0)


def shards(positions, target, inertia, stiffness, pin_columns, inverses):
    smem = pl.BlockSpec(memory_space=pltpu.SMEM)
    anywhere = pl.BlockSpec(memory_space=pl.ANY)
    grid = (1,)

    def full(shape):
        return pl.BlockSpec(shape, lambda i: (0,) * len(shape))

    own_map = pl.pallas_call(
        local_map_kernel,
        grid=grid,
        out_shape=sds((CB, CB)),
        in_specs=[pl.BlockSpec((4, CB, CB), lambda i: (0, 1, 0)), full((3, 8, CB))],
        out_specs=full((CB, CB)),
        compiler_params=pltpu.CompilerParams(vmem_limit_bytes=VMEM_LIMIT),
        cost_estimate=pl.CostEstimate(flops=10**8, bytes_accessed=10**6, transcendentals=0),
    )(inverses, stiffness)
    core_maps = lax.all_gather(own_map, "c")
    chip_copies = call(chip_map_kernel, sds((4, CB, CB)), (core_maps,))
    chips = swap(chip_copies, "x")

    tile = sds((8, 128))
    left, right, near, cross = call(
        halo_kernel,
        [tile] * 4,
        (positions, stiffness, chip_copies),
        specs=[None, None, anywhere],
    )
    pairs = [(2 * k + 1, 2 * k + 2) for k in range(63)]
    from_right = lax.ppermute(left, "y", [(1, 0), (2, 1), (3, 2)])
    from_left = lax.ppermute(right, "y", [(0, 1), (1, 2), (2, 3)])
    cross = lax.ppermute(cross, STRIP, pairs + [(b, a) for a, b in pairs])
    near = lax.ppermute(near, "c", [(0, 1), (1, 0)])
    halos = (from_left, from_right, near, cross)

    square = sds((CB, CB))
    plane = call(
        plane_product_kernel, square, (chips,) + halos, specs=[None] + [anywhere] * 4
    )
    beside = lax.ppermute(plane, ZAX, [(k, k ^ 1) for k in range(16)])

    field = sds((3, 8, CB))
    vector = sds((8, CB))
    base, offset, inertial, ext, above = call(
        first_side_kernel,
        [field, vector, field, sds((2, 8, 512)), vector],
        (positions, target, inertia, stiffness, pin_columns) + halos + (inverses, plane),
        specs=[None] * 4 + [smem] + [None] * 5 + [anywhere],
        flops=10**8,
        size=3 * 10**6,
    )
    wide = sds((5 * CB, 2 * CB), BF16)
    xh, xl, eh, el = call(
        plane_maps_kernel,
        [wide, wide, sds((CB, CB), BF16), sds((CB, CB), BF16)],
        (chips, core_maps, plane),
        specs=[None, None, anywhere],
        scratch=[pltpu.VMEM((4, CB, CB), F32), pltpu.VMEM((CB, CB), F32)],
        flops=10**9,
    )
    two = call(
        two_planes_kernel, square, (plane, beside, base, eh), specs=[None, None, anywhere, anywhere]
    )
    other_two = lax.ppermute(two, ZAX, [(k, k ^ 2) for k in range(16)])

    msg = call(
        offsets_kernel, sds((8, 3, CB)), (offset, core_maps, two), specs=[None, None, anywhere]
    )
    got = swap(msg, PLANE)
    both = call(
        plane_kernel,
        sds((8, 2 * CB)),
        (got, xh, xl),
        scratch=[pltpu.VMEM((16, 5 * CB), F32)],
        size=3 * 10**6,
    )
    group_half = call(
        four_planes_kernel, sds((128, CB)), (two, other_two, both), specs=[None, None, anywhere]
    )
    steps = [(4 + k, k) for k in range(4)] + [(8 + k, 12 + k) for k in range(4)]
    far_half = lax.ppermute(group_half, ZAX, steps)
    maps, send_map, take_map = call(
        group_maps_kernel,
        [sds((8, CB, CB), BF16), square, square],
        (beside, other_two, group_half),
        specs=[None, None, anywhere],
        flops=5 * 10**8,
    )
    far_parts = lax.all_gather(far_half, "c")
    joint, msg = call(
        send_kernel,
        [sds((2, CB, CB), BF16), sds((16, 3, CB))],
        (both, maps, far_parts, send_map, take_map),
    )
    got = swap(msg, ZAX)
    sizes = ((16, 3, CB), (8, 2 * CB), (8, CB, CB), (2, CB, CB), (CB, CB), (CB, CB), (3, 8, CB), (3, 8, CB))
    finish_specs = [full(s) for s in sizes] + [pl.BlockSpec((4, 2 * CB, CB), lambda i: (0, 0, 0))]
    params = pltpu.CompilerParams(vmem_limit_bytes=VMEM_LIMIT)
    cost = pl.CostEstimate(flops=10**8, bytes_accessed=4 * 10**6, transcendentals=0)
    middle, side, edge = pl.pallas_call(
        middle_kernel,
        grid=grid,
        out_shape=[sds((4, 8, CB)), sds((8, 8, 128)), tile],
        in_specs=finish_specs,
        out_specs=[full((4, 8, CB)), full((8, 8, 128)), full((8, 128))],
        scratch_shapes=[pltpu.VMEM((16, 3 * CB), F32)],
        compiler_params=params,
        cost_estimate=cost,
    )(got, both, maps, joint, eh, el, stiffness, base, inverses)

    side = swap(side, SIDES)
    edge = lax.ppermute(edge, STRIP, [(b, a) for a, b in pairs])
    base, msg = call(
        second_side_kernel,
        [field, sds((8, 3, CB))],
        (middle, stiffness, side, edge, inverses, core_maps, inertial, ext, above),
        flops=10**8,
        size=3 * 10**6,
    )
    got = swap(msg, PLANE)
    both, msg = call(
        plane_send_kernel,
        [sds((8, 2 * CB)), sds((16, 3, CB))],
        (got, xh, xl, maps, joint),
        scratch=[pltpu.VMEM((16, 5 * CB), F32)],
        size=3 * 10**6,
    )
    got = swap(msg, ZAX)
    return pl.pallas_call(
        final_kernel,
        grid=grid,
        out_shape=field,
        in_specs=finish_specs,
        out_specs=full((3, 8, CB)),
        scratch_shapes=[pltpu.VMEM((16, 3 * CB), F32)],
        compiler_params=params,
        cost_estimate=cost,
    )(got, both, maps, joint, eh, el, stiffness, base, inverses)


def solution(mesh):
    split = Mesh(mesh.devices.reshape(4, 4, 4, 2, 4), ("zh", "zl", "x", "c", "y"))
    return jax.shard_map(
        shards,
        mesh=split,
        in_specs=(
            P(None, STRIP, "y"),
            P(None, STRIP, "y"),
            P(STRIP, "y"),
            P(None, STRIP, "y"),
            P(),
            P(STRIP, None, None),
        ),
        out_specs=P(None, STRIP, "y"),
        check_vma=False,
    )
```

```python
import jax
import jax.numpy as jnp
from jax import lax
from jax.experimental import pallas as pl
from jax.experimental.pallas import tpu as pltpu
from jax.sharding import Mesh
from jax.sharding import PartitionSpec as P

F32 = jnp.float32
BF16 = jnp.bfloat16
STRIP = ("zh", "zl", "x", "c")
ZAX = ("zh", "zl")
PLANE = ("x", "c")
CB = 256
PIN = 20.0
VMEM_LIMIT = 14 * 1024 * 1024
WHOLE_VMEM = 64 * 1024 * 1024 - 96 * 1024


def dot(a, b):
    return lax.dot_general(a, b, (((1,), (0,)), ((), ())), preferred_element_type=F32)


def dot_t(a, b):
    return lax.dot_general(a, b, (((1,), (1,)), ((), ())), preferred_element_type=F32)


def pair(value):
    high = value.astype(BF16)
    low = (value - high.astype(F32)).astype(BF16)
    return high, low


def mm(a, b):
    return dot(a[0], b[0]) + (dot(a[0], b[1]) + dot(a[1], b[0]))


def eye():
    rows = lax.broadcasted_iota(jnp.int32, (CB, CB), 0)
    cols = lax.broadcasted_iota(jnp.int32, (CB, CB), 1)
    return jnp.where(rows == cols, 1.0, 0.0).astype(F32)


def stacked(value):
    high = value.astype(BF16)
    low = value - high.astype(F32)
    return jnp.concatenate([high.astype(F32), low], axis=0).astype(BF16)


def halves_sum(value):
    half = value.shape[0] // 2
    return value[:half] + value[half:]


def put_vector(vec_ref, slot, value):
    high = value.astype(BF16).astype(F32)
    vec_ref[0:3, slot * CB : (slot + 1) * CB] = high
    vec_ref[8:11, slot * CB : (slot + 1) * CB] = value - high


def apply_map(vec, high, low):
    return halves_sum(dot(vec, high) + dot(vec, low))


def call(kernel, outs, args, specs=None, scratch=(), flops=10**7, size=10**6, limit=VMEM_LIMIT):
    vmem = pl.BlockSpec(memory_space=pltpu.VMEM)
    in_specs = [vmem] * len(args) if specs is None else [vmem if s is None else s for s in specs]
    many = isinstance(outs, (list, tuple))
    out_specs = [vmem] * len(outs) if many else vmem
    return pl.pallas_call(
        kernel,
        out_shape=outs,
        in_specs=in_specs,
        out_specs=out_specs,
        scratch_shapes=list(scratch),
        compiler_params=pltpu.CompilerParams(vmem_limit_bytes=limit),
        cost_estimate=pl.CostEstimate(flops=flops, bytes_accessed=size, transcendentals=0),
    )(*args)


def sds(shape, dtype=F32):
    return jax.ShapeDtypeStruct(shape, dtype)


def local_map_kernel(inv_hbm, stiff_hbm, u_hbm, out_ref, inv_ref, stiff_ref, u_ref, sems):
    copies = [
        pltpu.make_async_copy(stiff_hbm, stiff_ref, sems.at[4]),
        pltpu.make_async_copy(u_hbm, u_ref, sems.at[5]),
    ]
    copies += [
        pltpu.make_async_copy(inv_hbm.at[k, CB : 2 * CB, 0:CB], inv_ref.at[k], sems.at[k])
        for k in range(4)
    ]
    for copy in copies:
        copy.start()
    core = lax.axis_index("c")
    copies[0].wait()
    copies[2].wait()
    first = dot_t(eye().astype(BF16), inv_ref[0]) * stiff_ref[1, 1:2, :]
    for k in range(1, 4):
        copies[2 + k].wait()
        high, low = pair(first)
        first = (dot_t(high, inv_ref[k]) + dot_t(low, inv_ref[k])) * stiff_ref[
            1, 2 * k + 1 : 2 * k + 2, :
        ]
    out_ref[0:CB, :] = first
    copies[1].wait()
    rows = [u_ref[k] for k in range(3)] + [stiff_ref[1]]
    rows = [jnp.where(core == 0, r[7:8], r[0:1]) for r in rows]
    out_ref[CB : CB + 8, :] = jnp.concatenate(rows + rows, axis=0)


def chip_map_kernel(both_ref, out_ref, near_ref):
    core = lax.axis_index("c")
    product = mm(pair(both_ref[0, 0:CB, :]), pair(both_ref[1, 0:CB, :]))
    for k in range(4):
        out_ref[k] = product
    tails = [both_ref[k, CB : CB + 8, :] for k in range(2)]
    near_ref[...] = jnp.where(core == 0, tails[1], tails[0])


def plane_product_kernel(chips_hbm, *rest):
    out_ref, chips_ref, sems = rest[-3:]
    copies = [
        pltpu.make_async_copy(chips_hbm.at[k], chips_ref.at[k], sems.at[k]) for k in range(4)
    ]
    for copy in copies:
        copy.start()
    copies[0].wait()
    copies[1].wait()
    left = mm(pair(chips_ref[0]), pair(chips_ref[1]))
    copies[2].wait()
    copies[3].wait()
    right = mm(pair(chips_ref[2]), pair(chips_ref[3]))
    out_ref[...] = mm(pair(left), pair(right))


def low_bit():
    return lax.rem(lax.axis_index("zl"), 2)


def high_bit():
    return lax.div(lax.axis_index("zl"), 2)


def own_half(ref):
    return ref[pl.ds(pl.multiple_of(lax.axis_index("c") * 128, 128), 128), :]


def joined(mine_ref, other_ref):
    core = lax.axis_index("c")
    mine, other = mine_ref[...], other_ref[...]
    top = jnp.where(core == 0, mine, other)
    return jnp.concatenate([top, jnp.where(core == 0, other, mine)], axis=0)


def two_planes_kernel(own_ref, other_ref, *rest):
    out_ref, half_ref = rest[-2:]
    right = low_bit() == 1
    left_map = jnp.where(right, other_ref[...], own_ref[...])
    right_map = jnp.where(right, own_ref[...], other_ref[...])
    out_ref[...] = mm(pair(left_map), pair(right_map))
    half_ref[...] = own_half(out_ref)


def four_planes_kernel(own_ref, mine_ref, other_ref, out_ref):
    right = high_bit() == 1
    left_map = jnp.where(right, mine_ref[...], own_half(own_ref))
    right_map = jnp.where(right, own_ref[...], joined(mine_ref, other_ref))
    out_ref[...] = mm(pair(left_map), pair(right_map))


def plane_maps_kernel(chips_ref, cores_ref, after_ref, wh_ref, wl_ref, eh_ref, el_ref, suf_ref, cur_ref):
    x = lax.axis_index("x")
    core = lax.axis_index("c")
    one = eye()
    chips = [pair(chips_ref[k]) for k in range(4)]

    def store(slot, col, value):
        high, low = pair(value)
        wh_ref[slot * CB : (slot + 1) * CB, col * CB : (col + 1) * CB] = high
        wl_ref[slot * CB : (slot + 1) * CB, col * CB : (col + 1) * CB] = low

    suffix = one
    suf_ref[3] = suffix
    store(3, 0, suffix)
    for k in (2, 1, 0):
        if k == 2:
            suffix = chips_ref[3]
        else:
            suffix = mm(chips[k + 1], pair(suffix))
        suf_ref[k] = suffix
        store(k, 0, suffix)
    store(4, 0, mm(pair(cores_ref[1, 0:CB, :]), pair(suf_ref[x])))
    store(4, 1, jnp.where(core == 1, one, 0.0))
    cur_ref[...] = jnp.where(core == 1, cores_ref[0, 0:CB, :], one)
    for k in (3, 2, 1, 0):

        @pl.when(k < x)
        def _():
            current = cur_ref[...]
            store(k, 1, current)
            cur_ref[...] = mm(chips[k], pair(current))

        @pl.when(k >= x)
        def _():
            store(k, 1, jnp.zeros((CB, CB), F32))

    high, low = pair(cur_ref[...])
    eh_ref[...] = high
    el_ref[...] = low


def group_maps_kernel(one_ref, mine_ref, other_ref, after_ref, out_ref, s_ref, e_ref):
    one = eye()
    sibling = one_ref[...]
    two = pair(joined(mine_ref, other_ref))
    send = jnp.where(low_bit() == 0, sibling, one)
    take = jnp.where(low_bit() == 1, sibling, one)
    for k, value in ((0, send), (4, take)):
        parts = pair(value)
        out_ref[k] = parts[0]
        out_ref[k + 1] = parts[1]
    send = jnp.where(high_bit() == 0, mm(pair(send), two), send)
    take = jnp.where(high_bit() == 1, mm(two, pair(take)), take)
    for k, value in ((2, send), (6, take)):
        parts = pair(value)
        out_ref[k] = parts[0]
        out_ref[k + 1] = parts[1]
    s_ref[...] = send
    e_ref[...] = take


def joint_map(mine_ref, other_ref, s_ref, e_ref, out_ref):
    zh = lax.axis_index("zh")
    far = joined(mine_ref, other_ref)
    left = jnp.where(zh == 0, s_ref[...], far)
    right = jnp.where(zh == 0, far, e_ref[...])
    joint = pair(mm(pair(left), pair(right)))
    out_ref[0] = joint[0]
    out_ref[1] = joint[1]


def edge_tiles(comps, weights):
    lane = lax.broadcasted_iota(jnp.int32, (8, 128), 1)
    right = jnp.zeros((8, 128), F32)
    left = jnp.zeros((8, 128), F32)
    for k, value in enumerate(comps + weights):
        mask = (lane == 2 * k) | (lane == 2 * k + 1)
        right = jnp.where(mask, pltpu.roll(value[:, 128:], (2 * k - 126) % 128, 1), right)
        if k < 3:
            left = jnp.where(mask, pltpu.roll(value[:, :128], 2 * k, 1), left)
    return left, right


def halo_kernel(u_ref, stiff_ref, after_ref, left_ref, right_ref, cross_ref):
    core = lax.axis_index("c")
    comps = [u_ref[k] for k in range(3)]
    left, right = edge_tiles(comps, [stiff_ref[0], stiff_ref[2]])
    left_ref[...] = left
    right_ref[...] = right
    for k, rows in enumerate(comps + [stiff_ref[1]]):
        cross_ref[k : k + 1, :] = jnp.where(core == 0, rows[0:1], rows[7:8])


def springs(ends, others, weight, rest, length):
    gaps = [o - e for o, e in zip(others, ends)]
    gaps = [g + r if r != 0.0 else g for g, r in zip(gaps, rest)]
    norm = jnp.sqrt(gaps[0] * gaps[0] + gaps[1] * gaps[1] + gaps[2] * gaps[2])
    factor = length / jnp.maximum(norm, 0.5 * length)
    return [weight * (g * factor - r if r != 0.0 else g * factor) for g, r in zip(gaps, rest)]


def solve_right_side(
    comps, inertial, from_left, from_right, below_rows, above_rows, above_weight, h_ext, b_ext,
    vertical, stiff_ref, inv_ref, base_ref,
):
    row = lax.broadcasted_iota(jnp.int32, (8, CB), 0)
    lane = lax.broadcasted_iota(jnp.int32, (8, 512), 1)
    wide = []
    for k in range(3):
        head = pltpu.roll(from_left, 126 - 2 * k, 1)
        tail = pltpu.roll(from_right, (-2 * k) % 128, 1) if k else from_right
        wide.append(jnp.concatenate([head, comps[k], tail], axis=1))
    total = [jnp.zeros((8, 512), F32)] * 3
    for offset, weight in ((1, h_ext), (2, b_ext)):
        shifted = [pltpu.roll(w, 512 - offset, 1) for w in wide]
        rest = (float(offset), 0.0, 0.0)
        pulls = springs(wide, shifted, weight, rest, float(offset))
        crossing = ((lane >= 128 - offset) & (lane < 128)) | (
            (lane >= 384 - offset) & (lane < 384)
        )
        across = jnp.where(crossing, weight, 0.0)
        for k in range(3):
            here = across * shifted[k] - pulls[k]
            there = across * wide[k] + pulls[k]
            total[k] = total[k] + here + pltpu.roll(there, offset, 1)
    lower = [
        jnp.where(row == 7, below_rows[k], pltpu.roll(comps[k], 7, 0)) for k in range(3)
    ]
    down = springs(comps, lower, vertical, (0.0, 1.0, 0.0), 1.0)
    upper = springs(
        above_rows, [c[0:1] for c in comps], above_weight, (0.0, 1.0, 0.0), 1.0
    )
    below_weight = jnp.where(lax.rem(row, 2) == 1, vertical, 0.0)
    rhs = []
    for k in range(3):
        received = jnp.where(row == 0, upper[k], pltpu.roll(down[k], 1, 0))
        rhs.append(
            inertial[k] + total[k][:, 128:384] + received - down[k] + below_weight * lower[k]
        )
    first = jnp.concatenate(rhs + [jnp.zeros((8, CB), F32)], axis=0)
    second = jnp.concatenate(
        [pltpu.roll(r, 7, 0) for r in rhs] + [jnp.zeros((8, CB), F32)], axis=0
    )
    wide_rhs = stacked(jnp.concatenate([first, second], axis=1))
    base = [jnp.zeros((8, CB), F32)] * 3
    for k in range(4):
        solved = halves_sum(dot_t(wide_rhs, inv_ref[k]))
        for j in range(3):
            part = solved[8 * j : 8 * j + 8]
            base[j] = jnp.where(
                row == 2 * k,
                part[:, :CB],
                jnp.where(row == 2 * k + 1, pltpu.roll(part[:, CB:], 1, 0), base[j]),
            )
    for j in range(3):
        base_ref[j] = base[j]
    weights = stiff_ref[1]
    last = base
    for k in range(1, 4):
        carried = jnp.concatenate(
            [weights * last[j] for j in range(3)] + [jnp.zeros((8, CB), F32)], axis=0
        )
        moved = halves_sum(dot_t(stacked(carried), inv_ref[k, CB:, :CB]))
        last = [
            jnp.where(row == 2 * k + 1, base[j] + pltpu.roll(moved[8 * j : 8 * j + 8], 2, 0), last[j])
            for j in range(3)
        ]
    rows = [(weights * last[j])[7:8] for j in range(3)]
    return jnp.concatenate(rows + [jnp.zeros((5, CB), F32)], axis=0)


def write_offsets(offset, chip_ref, msg_ref):
    core = lax.axis_index("c")
    x = lax.axis_index("x")
    chip = pair(chip_ref[1, 0:CB, :])
    onward = apply_map(stacked(offset), chip[0], chip[1])[0:3]
    raw = offset[0:3]
    onward = jnp.where(core == 0, onward, raw)
    for j in range(8):
        msg_ref[j] = jnp.where(x == j // 2, raw, onward)


def offsets_kernel(offset_ref, chip_ref, after_ref, msg_ref):
    write_offsets(offset_ref[...], chip_ref, msg_ref)


def first_side_kernel(
    u_ref, target_ref, inertia_ref, stiff_ref, pin_ref, left_ref, right_ref, near_ref, cross_ref,
    inv_ref, after_ref, base_ref, offset_ref, inertial_ref, ext_ref, above_ref,
):
    core = lax.axis_index("c")
    y = lax.axis_index("y")
    strip = (lax.axis_index("zh") * 4 + lax.axis_index("zl")) * 8 + lax.axis_index("x") * 2 + core
    comps = [u_ref[k] for k in range(3)]
    row = lax.broadcasted_iota(jnp.int32, (8, CB), 0)
    column = lax.broadcasted_iota(jnp.int32, (8, CB), 1) + y * CB
    hit = column < 0
    for k in range(pin_ref.shape[0]):
        hit = hit | (column == pin_ref[k])
    pinned = hit & (row == 0) & (strip == 0)
    inertial = []
    for k in range(3):
        value = inertia_ref[...] * target_ref[k] + PIN * jnp.where(pinned, comps[k], 0.0)
        inertial.append(value)
        inertial_ref[k] = value
    lane = lax.broadcasted_iota(jnp.int32, (8, 512), 1)
    from_left = left_ref[...]
    extended = []
    for k, channel, offset in ((3, 0, 1), (4, 2, 2)):
        head = pltpu.roll(from_left, 126 - 2 * k, 1)
        weight = jnp.concatenate([head, stiff_ref[channel], jnp.zeros((8, 128), F32)], axis=1)
        low = jnp.where(y == 0, 128, 128 - offset)
        high = jnp.where(y == 3, 384 - offset, 384)
        weight = jnp.where((lane >= low) & (lane < high), weight, 0.0)
        extended.append(weight)
        ext_ref[k - 3] = weight
    near, cross = near_ref[0:4, :], cross_ref[...]
    above = jnp.where(core == 0, cross, near)
    below = jnp.where(core == 0, near, cross)
    above_weight = jnp.where(strip == 0, 0.0, above[3:4])
    above_ref[...] = jnp.broadcast_to(above_weight, (8, CB))
    vertical = jnp.where((row == 7) & (strip == 127), 0.0, stiff_ref[1])
    offset_ref[...] = solve_right_side(
        comps, inertial, from_left, right_ref[...], [below[k : k + 1] for k in range(3)],
        [above[k : k + 1] for k in range(3)], above_weight, extended[0], extended[1], vertical,
        stiff_ref, inv_ref, base_ref,
    )


def second_side_kernel(
    u_ref, stiff_ref, left_ref, right_ref, row_ref, inv_ref, chip_ref, inertial_ref, ext_ref,
    above_ref, base_ref, msg_ref,
):
    core = lax.axis_index("c")
    y = lax.axis_index("y")
    strip = (lax.axis_index("zh") * 4 + lax.axis_index("zl")) * 8 + lax.axis_index("x") * 2 + core
    comps = [u_ref[k] for k in range(3)]
    row = lax.broadcasted_iota(jnp.int32, (8, CB), 0)
    above_weight = above_ref[0:1, :]
    divisor = jnp.where(strip == 0, 1.0, above_weight)
    above_rows = [u_ref[3, k : k + 1, :] / divisor for k in range(3)]
    vertical = jnp.where((row == 7) & (strip == 127), 0.0, stiff_ref[1])
    offset = solve_right_side(
        comps, [inertial_ref[k] for k in range(3)], left_ref[...], right_ref[...],
        [row_ref[k : k + 1, :] for k in range(3)], above_rows, above_weight, ext_ref[0], ext_ref[1],
        vertical, stiff_ref, inv_ref, base_ref,
    )
    write_offsets(offset, chip_ref, msg_ref)


def plane_vectors(got_ref, wh_ref, wl_ref, vec_ref):
    x = lax.axis_index("x")
    vec_ref[...] = jnp.zeros(vec_ref.shape, F32)
    for k in range(4):
        own = got_ref[2 * k + 1]
        put_vector(vec_ref, k, jnp.where(x == k, own, own + got_ref[2 * k]))
    put_vector(vec_ref, 4, got_ref[2 * x])
    return apply_map(vec_ref[...].astype(BF16), wh_ref[...], wl_ref[...])


def send_vectors(total, maps_ref, joint_ref, msg_ref):
    zh = lax.axis_index("zh")
    vec = stacked(total)
    pairs = apply_map(vec, maps_ref[0], maps_ref[1])[0:3]
    near = apply_map(vec, maps_ref[2], maps_ref[3])[0:3]
    far = apply_map(vec, joint_ref[0], joint_ref[1])[0:3]
    far = jnp.where(zh == 0, far, near)
    raw = total[0:3]
    for g in range(4):
        for h in range(2):
            inner = jnp.where(high_bit() == h, raw, pairs)
            value = jnp.where(zh == g, inner, near if g < 2 else far)
            msg_ref[4 * g + 2 * h] = value
            msg_ref[4 * g + 2 * h + 1] = value


def plane_kernel(got_ref, wh_ref, wl_ref, both_ref, vec_ref):
    both_ref[...] = plane_vectors(got_ref, wh_ref, wl_ref, vec_ref)


def send_kernel(both_ref, maps_ref, mine_ref, other_ref, s_ref, e_ref, joint_ref, msg_ref):
    joint_map(mine_ref, other_ref, s_ref, e_ref, joint_ref)
    send_vectors(both_ref[:, :CB], maps_ref, joint_ref, msg_ref)


def plane_send_kernel(got_ref, wh_ref, wl_ref, maps_ref, joint_ref, both_ref, msg_ref, vec_ref):
    both = plane_vectors(got_ref, wh_ref, wl_ref, vec_ref)
    both_ref[...] = both
    send_vectors(both[:, :CB], maps_ref, joint_ref, msg_ref)


def finish(
    got_ref, both_ref, maps_ref, joint_ref, eh_ref, el_ref, stiff_ref, base_ref, inv_ref, vec_ref
):
    zh = lax.axis_index("zh")
    row = lax.broadcasted_iota(jnp.int32, (8, CB), 0)
    none = jnp.zeros((3, CB), F32)
    vec_ref[...] = jnp.zeros(vec_ref.shape, F32)
    first_two = got_ref[4 * zh] + got_ref[4 * zh + 1]
    put_vector(vec_ref, 0, jnp.where(high_bit() == 1, first_two, none))
    sums = [
        (got_ref[4 * g] + got_ref[4 * g + 1]) + (got_ref[4 * g + 2] + got_ref[4 * g + 3])
        for g in range(3)
    ]
    lower = jnp.where(zh >= 1, sums[0], none) + jnp.where(zh >= 2, sums[1], none)
    put_vector(vec_ref, 1, jnp.where(zh == 3, sums[2], lower))
    put_vector(vec_ref, 2, jnp.where(zh == 3, lower, none))
    vec = vec_ref[...].astype(BF16)
    arrived = apply_map(vec[:, :CB], maps_ref[4], maps_ref[5])
    arrived = arrived + apply_map(vec[:, CB : 2 * CB], maps_ref[6], maps_ref[7])
    arrived = arrived + apply_map(vec[:, 2 * CB :], joint_ref[0], joint_ref[1])
    beside = jnp.where(low_bit() == 1, got_ref[4 * zh + 2 * high_bit()], none)
    arrived = arrived + jnp.concatenate([beside, jnp.zeros((5, CB), F32)], axis=0)
    came = both_ref[:, CB:] + apply_map(stacked(arrived), eh_ref[...], el_ref[...])
    weights = stiff_ref[1]
    state = [base_ref[k] for k in range(3)]
    blank = jnp.zeros((8, CB), F32)
    for k in range(4):
        if k == 0:
            source = [jnp.broadcast_to(came[j : j + 1], (8, CB)) for j in range(3)]
        else:
            source = [weights * state[j] for j in range(3)]
        moved = halves_sum(dot_t(stacked(jnp.concatenate(source + [blank], axis=0)), inv_ref[k]))
        for j in range(3):
            part = moved[8 * j : 8 * j + 8]
            state[j] = state[j] + jnp.where(
                row == 2 * k,
                pltpu.roll(part[:, :CB], 1, 0),
                jnp.where(row == 2 * k + 1, pltpu.roll(part[:, CB:], 2, 0), 0.0),
            )
    return state, came


def middle_kernel(
    got_ref, both_ref, maps_ref, joint_ref, eh_ref, el_ref, stiff_ref, base_ref, inv_ref,
    u_ref, left_ref, right_ref, row_ref, vec_ref,
):
    state, came = finish(
        got_ref, both_ref, maps_ref, joint_ref, eh_ref, el_ref, stiff_ref, base_ref, inv_ref, vec_ref
    )
    for k in range(3):
        u_ref[k] = state[k]
    u_ref[3] = came
    left, right = edge_tiles(state, [])
    left_ref[...] = left
    right_ref[...] = right
    row_ref[...] = jnp.concatenate([state[0][0:1], state[1][0:1], state[2][0:1], state[0][0:1]], axis=0)


def final_kernel(
    got_ref, both_ref, maps_ref, joint_ref, eh_ref, el_ref, stiff_ref, base_ref, inv_ref,
    u_ref, vec_ref,
):
    state, came = finish(
        got_ref, both_ref, maps_ref, joint_ref, eh_ref, el_ref, stiff_ref, base_ref, inv_ref, vec_ref
    )
    for k in range(3):
        u_ref[k] = state[k]


def swap(value, axes):
    return lax.all_to_all(value, axes, 0, 0)


def shards(positions, target, inertia, stiffness, pin_columns, inverses):
    smem = pl.BlockSpec(memory_space=pltpu.SMEM)
    anywhere = pl.BlockSpec(memory_space=pl.ANY)
    grid = (1,)

    def full(shape):
        return pl.BlockSpec(shape, lambda i: (0,) * len(shape))

    hbm = pl.BlockSpec(memory_space=pltpu.HBM)
    own_map = call(
        local_map_kernel,
        sds((CB + 8, CB)),
        (inverses, stiffness, positions),
        specs=[hbm] * 3,
        scratch=[
            pltpu.VMEM((4, CB, CB), BF16),
            pltpu.VMEM((3, 8, CB), F32),
            pltpu.VMEM((3, 8, CB), F32),
            pltpu.SemaphoreType.DMA((6,)),
        ],
        flops=10**8,
        limit=WHOLE_VMEM,
    )
    core_maps = lax.all_gather(own_map, "c")
    chip_copies, near = call(chip_map_kernel, [sds((4, CB, CB)), sds((8, CB))], (core_maps,))
    chips = swap(chip_copies, "x")

    tile = sds((8, 128))
    rows = sds((4, CB))
    left, right, cross = call(
        halo_kernel,
        [tile, tile, rows],
        (positions, stiffness, chip_copies),
        specs=[None, None, anywhere],
    )
    pairs = [(2 * k + 1, 2 * k + 2) for k in range(63)]
    to_left = [(1, 0), (2, 1), (3, 2)]
    to_right = [(0, 1), (1, 2), (2, 3)]
    cores = [(0, 1), (1, 0)]
    from_right = lax.ppermute(left, "y", to_left)
    from_left = lax.ppermute(right, "y", to_right)
    cross = lax.ppermute(cross, STRIP, pairs + [(b, a) for a, b in pairs])
    halos = (from_left, from_right, near, cross)

    square = sds((CB, CB))
    plane = call(
        plane_product_kernel,
        square,
        (chips, from_left, from_right, cross),
        specs=[hbm] + [anywhere] * 3,
        scratch=[pltpu.VMEM((4, CB, CB), F32), pltpu.SemaphoreType.DMA((4,))],
    )
    beside = lax.ppermute(plane, ZAX, [(k, k ^ 1) for k in range(16)])

    field = sds((3, 8, CB))
    vector = sds((8, CB))
    base, offset, inertial, ext, above = call(
        first_side_kernel,
        [field, vector, field, sds((2, 8, 512)), vector],
        (positions, target, inertia, stiffness, pin_columns) + halos + (inverses, plane),
        specs=[None] * 4 + [smem] + [None] * 5 + [anywhere],
        flops=10**8,
        size=3 * 10**6,
    )
    wide = sds((5 * CB, 2 * CB), BF16)
    xh, xl, eh, el = call(
        plane_maps_kernel,
        [wide, wide, sds((CB, CB), BF16), sds((CB, CB), BF16)],
        (chips, core_maps, plane),
        specs=[None, None, anywhere],
        scratch=[pltpu.VMEM((4, CB, CB), F32), pltpu.VMEM((CB, CB), F32)],
        flops=10**9,
    )
    half = sds((128, CB))
    two, two_half = call(
        two_planes_kernel,
        [square, half],
        (plane, beside, base, eh),
        specs=[None, None, anywhere, anywhere],
    )
    two_mine = lax.ppermute(two_half, ZAX, [(k, k ^ 2) for k in range(16)])
    two_other = lax.ppermute(two_mine, "c", cores)
    group_half = call(four_planes_kernel, half, (two, two_mine, two_other))
    steps = [(4 + k, k) for k in range(4)] + [(8 + k, 12 + k) for k in range(4)]
    far_mine = lax.ppermute(group_half, ZAX, steps)

    msg = call(
        offsets_kernel, sds((8, 3, CB)), (offset, core_maps, group_half), specs=[None, None, anywhere]
    )
    got = swap(msg, PLANE)
    both = call(
        plane_kernel,
        sds((8, 2 * CB)),
        (got, xh, xl),
        scratch=[pltpu.VMEM((16, 5 * CB), F32)],
        size=3 * 10**6,
    )
    maps, send_map, take_map = call(
        group_maps_kernel,
        [sds((8, CB, CB), BF16), square, square],
        (beside, two_mine, two_other, both),
        specs=[None, None, None, anywhere],
        flops=5 * 10**8,
    )
    far_mine, both, maps = lax.optimization_barrier((far_mine, both, maps))
    far_other = lax.ppermute(far_mine, "c", cores)
    joint, msg = call(
        send_kernel,
        [sds((2, CB, CB), BF16), sds((16, 3, CB))],
        (both, maps, far_mine, far_other, send_map, take_map),
    )
    got = swap(msg, ZAX)
    sizes = ((16, 3, CB), (8, 2 * CB), (8, CB, CB), (2, CB, CB), (CB, CB), (CB, CB), (3, 8, CB), (3, 8, CB))
    finish_specs = [full(s) for s in sizes] + [pl.BlockSpec((4, 2 * CB, CB), lambda i: (0, 0, 0))]
    params = pltpu.CompilerParams(vmem_limit_bytes=VMEM_LIMIT)
    cost = pl.CostEstimate(flops=10**8, bytes_accessed=4 * 10**6, transcendentals=0)
    middle, left, right, low_row = pl.pallas_call(
        middle_kernel,
        grid=grid,
        out_shape=[sds((4, 8, CB)), tile, tile, rows],
        in_specs=finish_specs,
        out_specs=[full((4, 8, CB)), full((8, 128)), full((8, 128)), full((4, CB))],
        scratch_shapes=[pltpu.VMEM((16, 3 * CB), F32)],
        compiler_params=params,
        cost_estimate=cost,
    )(got, both, maps, joint, eh, el, stiffness, base, inverses)

    low_row = lax.ppermute(low_row, STRIP, [(k + 1, k) for k in range(127)])
    from_right = lax.ppermute(left, "y", to_left)
    from_left = lax.ppermute(right, "y", to_right)
    base, msg = call(
        second_side_kernel,
        [field, sds((8, 3, CB))],
        (middle, stiffness, from_left, from_right, low_row, inverses, core_maps)
        + (inertial, ext, above),
        flops=10**8,
        size=3 * 10**6,
    )
    got = swap(msg, PLANE)
    both, msg = call(
        plane_send_kernel,
        [sds((8, 2 * CB)), sds((16, 3, CB))],
        (got, xh, xl, maps, joint),
        scratch=[pltpu.VMEM((16, 5 * CB), F32)],
        size=3 * 10**6,
    )
    got = swap(msg, ZAX)
    return pl.pallas_call(
        final_kernel,
        grid=grid,
        out_shape=field,
        in_specs=finish_specs,
        out_specs=full((3, 8, CB)),
        scratch_shapes=[pltpu.VMEM((16, 3 * CB), F32)],
        compiler_params=params,
        cost_estimate=cost,
    )(got, both, maps, joint, eh, el, stiffness, base, inverses)


def solution(mesh):
    split = Mesh(mesh.devices.reshape(4, 4, 4, 2, 4), ("zh", "zl", "x", "c", "y"))
    return jax.shard_map(
        shards,
        mesh=split,
        in_specs=(
            P(None, STRIP, "y"),
            P(None, STRIP, "y"),
            P(STRIP, "y"),
            P(None, STRIP, "y"),
            P(),
            P(STRIP, None, None),
        ),
        out_specs=P(None, STRIP, "y"),
        check_vma=False,
    )
```

```python
import jax
import jax.numpy as jnp
from jax import lax
from jax.experimental import pallas as pl
from jax.experimental.pallas import tpu as pltpu
from jax.sharding import Mesh
from jax.sharding import PartitionSpec as P

F32 = jnp.float32
BF16 = jnp.bfloat16
STRIP = ("zh", "zl", "x", "c")
ZAX = ("zh", "zl")
PLANE = ("x", "c")
CB = 256
PIN = 20.0
VMEM_LIMIT = 14 * 1024 * 1024
WHOLE_VMEM = 64 * 1024 * 1024 - 96 * 1024


def dot(a, b):
    return lax.dot_general(a, b, (((1,), (0,)), ((), ())), preferred_element_type=F32)


def dot_t(a, b):
    return lax.dot_general(a, b, (((1,), (1,)), ((), ())), preferred_element_type=F32)


def pair(value):
    high = value.astype(BF16)
    low = (value - high.astype(F32)).astype(BF16)
    return high, low


def mm(a, b):
    return dot(a[0], b[0]) + (dot(a[0], b[1]) + dot(a[1], b[0]))


def eye():
    rows = lax.broadcasted_iota(jnp.int32, (CB, CB), 0)
    cols = lax.broadcasted_iota(jnp.int32, (CB, CB), 1)
    return jnp.where(rows == cols, 1.0, 0.0).astype(F32)


def stacked(value):
    high = value.astype(BF16)
    low = value - high.astype(F32)
    return jnp.concatenate([high.astype(F32), low], axis=0).astype(BF16)


def halves_sum(value):
    half = value.shape[0] // 2
    return value[:half] + value[half:]


def put_vector(vec_ref, slot, value):
    high = value.astype(BF16).astype(F32)
    vec_ref[0:3, slot * CB : (slot + 1) * CB] = high
    vec_ref[8:11, slot * CB : (slot + 1) * CB] = value - high


def apply_map(vec, high, low):
    return halves_sum(dot(vec, high) + dot(vec, low))


def call(kernel, outs, args, specs=None, scratch=(), flops=10**7, size=10**6, limit=VMEM_LIMIT):
    vmem = pl.BlockSpec(memory_space=pltpu.VMEM)
    in_specs = [vmem] * len(args) if specs is None else [vmem if s is None else s for s in specs]
    many = isinstance(outs, (list, tuple))
    out_specs = [vmem] * len(outs) if many else vmem
    return pl.pallas_call(
        kernel,
        out_shape=outs,
        in_specs=in_specs,
        out_specs=out_specs,
        scratch_shapes=list(scratch),
        compiler_params=pltpu.CompilerParams(vmem_limit_bytes=limit),
        cost_estimate=pl.CostEstimate(flops=flops, bytes_accessed=size, transcendentals=0),
    )(*args)


def sds(shape, dtype=F32):
    return jax.ShapeDtypeStruct(shape, dtype)


def local_map_kernel(inv_hbm, stiff_hbm, u_hbm, out_ref, inv_ref, stiff_ref, u_ref, sems):
    copies = [
        pltpu.make_async_copy(stiff_hbm, stiff_ref, sems.at[4]),
        pltpu.make_async_copy(u_hbm, u_ref, sems.at[5]),
    ]
    copies += [
        pltpu.make_async_copy(inv_hbm.at[k, CB : 2 * CB, 0:CB], inv_ref.at[k], sems.at[k])
        for k in range(4)
    ]
    for copy in copies:
        copy.start()
    core = lax.axis_index("c")
    copies[0].wait()
    copies[2].wait()
    first = dot_t(eye().astype(BF16), inv_ref[0]) * stiff_ref[1, 1:2, :]
    for k in range(1, 4):
        copies[2 + k].wait()
        high, low = pair(first)
        first = (dot_t(high, inv_ref[k]) + dot_t(low, inv_ref[k])) * stiff_ref[
            1, 2 * k + 1 : 2 * k + 2, :
        ]
    out_ref[0:CB, :] = first
    copies[1].wait()
    rows = [u_ref[k] for k in range(3)] + [stiff_ref[1]]
    rows = [jnp.where(core == 0, r[7:8], r[0:1]) for r in rows]
    out_ref[CB : CB + 8, :] = jnp.concatenate(rows + rows, axis=0)


def chip_map_kernel(both_ref, out_ref, near_ref):
    core = lax.axis_index("c")
    out_ref[...] = mm(pair(both_ref[0, 0:CB, :]), pair(both_ref[1, 0:CB, :]))
    tails = [both_ref[k, CB : CB + 8, :] for k in range(2)]
    near_ref[...] = jnp.where(core == 0, tails[1], tails[0])


def low_bit(axis="zl"):
    return lax.rem(lax.axis_index(axis), 2)


def high_bit(axis="zl"):
    return lax.div(lax.axis_index(axis), 2)


def in_order(own, other, right):
    return jnp.where(right, other, own), jnp.where(right, own, other)


def two_chips_kernel(own_ref, other_ref, cross_ref, from_left_ref, from_right_ref, out_ref, row_ref):
    left_map, right_map = in_order(own_ref[...], other_ref[...], low_bit("x") == 1)
    out_ref[...] = mm(pair(left_map), pair(right_map))
    row_ref[...] = cross_ref[...]


def four_chips_kernel(own_ref, other_ref, after_ref, out_ref):
    left_map, right_map = in_order(own_ref[...], other_ref[...], high_bit("x") == 1)
    out_ref[...] = mm(pair(left_map), pair(right_map))


def rows_of_half(half):
    return jnp.concatenate([half[:128], half[128:]], axis=1)


def half_of_rows(rows):
    return jnp.concatenate([rows[:, :128], rows[:, 128:]], axis=0)


def joined(mine_ref, other_ref):
    core = lax.axis_index("c")
    first, second = in_order(mine_ref[...], other_ref[...], core == 1)
    columns = jnp.concatenate([first, second], axis=1)
    rows = jnp.concatenate([rows_of_half(first), rows_of_half(second)], axis=0)
    return jnp.where(high_bit() == 0, columns, rows)


def two_planes_kernel(own_ref, other_ref, *rest):
    out_ref, half_ref = rest[-2:]
    core = lax.axis_index("c")
    left_map, right_map = in_order(own_ref[...], other_ref[...], low_bit() == 1)
    product = mm(pair(left_map), pair(right_map))
    out_ref[...] = product
    columns = jnp.where(core == 0, product[:, :128], product[:, 128:])
    rows = half_of_rows(jnp.where(core == 0, product[:128], product[128:]))
    half_ref[...] = jnp.where(high_bit() == 0, rows, columns)


def four_planes_kernel(own_ref, half_ref, out_ref):
    own = pair(own_ref[...])
    half = half_ref[...]
    columns = mm(own, pair(half))
    rows = half_of_rows(mm(pair(rows_of_half(half)), own))
    out_ref[...] = jnp.where(high_bit() == 0, columns, rows)


def plane_maps_kernel(
    own_ref, sib_ref, two_ref, far_ref, cores_ref, after_ref, wh_ref, wl_ref, eh_ref, el_ref, sends_ref
):
    core = lax.axis_index("c")
    one = eye()
    low, high = low_bit("x"), high_bit("x")
    own, sib, two, far = own_ref[...], sib_ref[...], two_ref[...], far_ref[...]
    first, second = cores_ref[0, 0:CB, :], cores_ref[1, 0:CB, :]

    def store(slot, col, value):
        parts = pair(value)
        wh_ref[slot * CB : (slot + 1) * CB, col * CB : (col + 1) * CB] = parts[0]
        wl_ref[slot * CB : (slot + 1) * CB, col * CB : (col + 1) * CB] = parts[1]

    sib_after = jnp.where(low == 0, sib, one)
    rest = pair(jnp.where(high == 0, far, one))
    to_end = mm(pair(sib_after), rest)
    store(0, 0, mm(pair(second), pair(to_end)))
    store(1, 0, to_end)
    store(2, 0, mm(pair(jnp.where(low == 0, one, own)), rest))
    store(3, 0, jnp.where(high == 1, two, one))
    none = jnp.zeros((CB, CB), F32)
    core_before = jnp.where(core == 1, first, one)
    chip_before = mm(pair(jnp.where(low == 1, sib, one)), pair(core_before))
    store(0, 1, jnp.where(core == 1, one, none))
    store(1, 1, none)
    store(2, 1, jnp.where(low == 1, core_before, none))
    store(3, 1, jnp.where(high == 1, chip_before, none))
    parts = pair(mm(pair(jnp.where(high == 1, far, one)), pair(chip_before)))
    eh_ref[...] = parts[0]
    el_ref[...] = parts[1]
    core_after = jnp.where(core == 0, second, one)
    parts = pair(core_after)
    sends_ref[0] = parts[0]
    sends_ref[1] = parts[1]
    parts = pair(mm(parts, pair(sib_after)))
    sends_ref[2] = parts[0]
    sends_ref[3] = parts[1]


def bundle_kernel(two_ref, far_ref, after_ref, out_ref):
    out_ref[0] = two_ref[...]
    out_ref[1] = far_ref[...]


def group_maps_kernel(both_ref, one_ref, mine_ref, other_ref, out_ref, joint_ref, msg_ref):
    zh = lax.axis_index("zh")
    one = eye()
    sibling = one_ref[...]
    two = pair(joined(mine_ref.at[0], other_ref.at[0]))
    far = joined(mine_ref.at[1], other_ref.at[1])
    send = jnp.where(low_bit() == 0, sibling, one)
    take = jnp.where(low_bit() == 1, sibling, one)
    for k, value in ((0, send), (4, take)):
        parts = pair(value)
        out_ref[k] = parts[0]
        out_ref[k + 1] = parts[1]
    send = jnp.where(high_bit() == 0, mm(pair(send), two), send)
    take = jnp.where(high_bit() == 1, mm(two, pair(take)), take)
    for k, value in ((2, send), (6, take)):
        parts = pair(value)
        out_ref[k] = parts[0]
        out_ref[k + 1] = parts[1]
    left = jnp.where(zh == 0, send, far)
    right = jnp.where(zh == 0, far, take)
    joint = pair(mm(pair(left), pair(right)))
    joint_ref[0] = joint[0]
    joint_ref[1] = joint[1]
    send_vectors(both_ref[:, :CB], out_ref, joint_ref, msg_ref)


def edge_tiles(comps, weights):
    lane = lax.broadcasted_iota(jnp.int32, (8, 128), 1)
    right = jnp.zeros((8, 128), F32)
    left = jnp.zeros((8, 128), F32)
    for k, value in enumerate(comps + weights):
        mask = (lane == 2 * k) | (lane == 2 * k + 1)
        right = jnp.where(mask, pltpu.roll(value[:, 128:], (2 * k - 126) % 128, 1), right)
        if k < 3:
            left = jnp.where(mask, pltpu.roll(value[:, :128], 2 * k, 1), left)
    return left, right


def halo_kernel(u_ref, stiff_ref, after_ref, left_ref, right_ref, cross_ref):
    core = lax.axis_index("c")
    comps = [u_ref[k] for k in range(3)]
    left, right = edge_tiles(comps, [stiff_ref[0], stiff_ref[2]])
    left_ref[...] = left
    right_ref[...] = right
    for k, rows in enumerate(comps + [stiff_ref[1]]):
        cross_ref[k : k + 1, :] = jnp.where(core == 0, rows[0:1], rows[7:8])


def springs(ends, others, weight, rest, length):
    gaps = [o - e for o, e in zip(others, ends)]
    gaps = [g + r if r != 0.0 else g for g, r in zip(gaps, rest)]
    norm = jnp.sqrt(gaps[0] * gaps[0] + gaps[1] * gaps[1] + gaps[2] * gaps[2])
    factor = length / jnp.maximum(norm, 0.5 * length)
    return [weight * (g * factor - r if r != 0.0 else g * factor) for g, r in zip(gaps, rest)]


def solve_right_side(
    comps, inertial, from_left, from_right, below_rows, above_rows, above_weight, h_ext, b_ext,
    vertical, stiff_ref, inv_ref, base_ref,
):
    row = lax.broadcasted_iota(jnp.int32, (8, CB), 0)
    lane = lax.broadcasted_iota(jnp.int32, (8, 512), 1)
    wide = []
    for k in range(3):
        head = pltpu.roll(from_left, 126 - 2 * k, 1)
        tail = pltpu.roll(from_right, (-2 * k) % 128, 1) if k else from_right
        wide.append(jnp.concatenate([head, comps[k], tail], axis=1))
    total = [jnp.zeros((8, 512), F32)] * 3
    for offset, weight in ((1, h_ext), (2, b_ext)):
        shifted = [pltpu.roll(w, 512 - offset, 1) for w in wide]
        rest = (float(offset), 0.0, 0.0)
        pulls = springs(wide, shifted, weight, rest, float(offset))
        crossing = ((lane >= 128 - offset) & (lane < 128)) | (
            (lane >= 384 - offset) & (lane < 384)
        )
        across = jnp.where(crossing, weight, 0.0)
        for k in range(3):
            here = across * shifted[k] - pulls[k]
            there = across * wide[k] + pulls[k]
            total[k] = total[k] + here + pltpu.roll(there, offset, 1)
    lower = [
        jnp.where(row == 7, below_rows[k], pltpu.roll(comps[k], 7, 0)) for k in range(3)
    ]
    down = springs(comps, lower, vertical, (0.0, 1.0, 0.0), 1.0)
    upper = springs(
        above_rows, [c[0:1] for c in comps], above_weight, (0.0, 1.0, 0.0), 1.0
    )
    below_weight = jnp.where(lax.rem(row, 2) == 1, vertical, 0.0)
    rhs = []
    for k in range(3):
        received = jnp.where(row == 0, upper[k], pltpu.roll(down[k], 1, 0))
        rhs.append(
            inertial[k] + total[k][:, 128:384] + received - down[k] + below_weight * lower[k]
        )
    first = jnp.concatenate(rhs + [jnp.zeros((8, CB), F32)], axis=0)
    second = jnp.concatenate(
        [pltpu.roll(r, 7, 0) for r in rhs] + [jnp.zeros((8, CB), F32)], axis=0
    )
    wide_rhs = stacked(jnp.concatenate([first, second], axis=1))
    base = [jnp.zeros((8, CB), F32)] * 3
    for k in range(4):
        solved = halves_sum(dot_t(wide_rhs, inv_ref[k]))
        for j in range(3):
            part = solved[8 * j : 8 * j + 8]
            base[j] = jnp.where(
                row == 2 * k,
                part[:, :CB],
                jnp.where(row == 2 * k + 1, pltpu.roll(part[:, CB:], 1, 0), base[j]),
            )
    for j in range(3):
        base_ref[j] = base[j]
    weights = stiff_ref[1]
    last = base
    for k in range(1, 4):
        carried = jnp.concatenate(
            [weights * last[j] for j in range(3)] + [jnp.zeros((8, CB), F32)], axis=0
        )
        moved = halves_sum(dot_t(stacked(carried), inv_ref[k, CB:, :CB]))
        last = [
            jnp.where(row == 2 * k + 1, base[j] + pltpu.roll(moved[8 * j : 8 * j + 8], 2, 0), last[j])
            for j in range(3)
        ]
    rows = [(weights * last[j])[7:8] for j in range(3)]
    return jnp.concatenate(rows + [jnp.zeros((5, CB), F32)], axis=0)


def write_offsets(offset, sends_ref, msg_ref):
    core = lax.axis_index("c")
    x = lax.axis_index("x")
    vec = stacked(offset)
    raw = offset[0:3]
    beside = jnp.where(core == 0, apply_map(vec, sends_ref[0], sends_ref[1])[0:3], raw)
    far = apply_map(vec, sends_ref[2], sends_ref[3])[0:3]
    for k in range(4):
        value = jnp.where(high_bit("x") == k // 2, beside, far)
        value = jnp.where(x == k, raw, value)
        msg_ref[2 * k] = value
        msg_ref[2 * k + 1] = value


def offsets_kernel(offset_ref, sends_ref, after_ref, msg_ref):
    write_offsets(offset_ref[...], sends_ref, msg_ref)


def first_side_kernel(
    u_ref, target_ref, inertia_ref, stiff_ref, pin_ref, left_ref, right_ref, near_ref, cross_ref,
    inv_ref, after_ref, base_ref, offset_ref, inertial_ref, ext_ref, above_ref,
):
    core = lax.axis_index("c")
    y = lax.axis_index("y")
    strip = (lax.axis_index("zh") * 4 + lax.axis_index("zl")) * 8 + lax.axis_index("x") * 2 + core
    comps = [u_ref[k] for k in range(3)]
    row = lax.broadcasted_iota(jnp.int32, (8, CB), 0)
    column = lax.broadcasted_iota(jnp.int32, (8, CB), 1) + y * CB
    hit = column < 0
    for k in range(pin_ref.shape[0]):
        hit = hit | (column == pin_ref[k])
    pinned = hit & (row == 0) & (strip == 0)
    inertial = []
    for k in range(3):
        value = inertia_ref[...] * target_ref[k] + PIN * jnp.where(pinned, comps[k], 0.0)
        inertial.append(value)
        inertial_ref[k] = value
    lane = lax.broadcasted_iota(jnp.int32, (8, 512), 1)
    from_left = left_ref[...]
    extended = []
    for k, channel, offset in ((3, 0, 1), (4, 2, 2)):
        head = pltpu.roll(from_left, 126 - 2 * k, 1)
        weight = jnp.concatenate([head, stiff_ref[channel], jnp.zeros((8, 128), F32)], axis=1)
        low = jnp.where(y == 0, 128, 128 - offset)
        high = jnp.where(y == 3, 384 - offset, 384)
        weight = jnp.where((lane >= low) & (lane < high), weight, 0.0)
        extended.append(weight)
        ext_ref[k - 3] = weight
    near, cross = near_ref[0:4, :], cross_ref[...]
    above = jnp.where(core == 0, cross, near)
    below = jnp.where(core == 0, near, cross)
    above_weight = jnp.where(strip == 0, 0.0, above[3:4])
    above_ref[...] = jnp.broadcast_to(above_weight, (8, CB))
    vertical = jnp.where((row == 7) & (strip == 127), 0.0, stiff_ref[1])
    offset_ref[...] = solve_right_side(
        comps, inertial, from_left, right_ref[...], [below[k : k + 1] for k in range(3)],
        [above[k : k + 1] for k in range(3)], above_weight, extended[0], extended[1], vertical,
        stiff_ref, inv_ref, base_ref,
    )


def second_side_kernel(
    u_ref, stiff_ref, left_ref, right_ref, row_ref, inv_ref, sends_ref, inertial_ref, ext_ref,
    above_ref, base_ref, msg_ref,
):
    core = lax.axis_index("c")
    y = lax.axis_index("y")
    strip = (lax.axis_index("zh") * 4 + lax.axis_index("zl")) * 8 + lax.axis_index("x") * 2 + core
    comps = [u_ref[k] for k in range(3)]
    row = lax.broadcasted_iota(jnp.int32, (8, CB), 0)
    above_weight = above_ref[0:1, :]
    divisor = jnp.where(strip == 0, 1.0, above_weight)
    above_rows = [u_ref[3, k : k + 1, :] / divisor for k in range(3)]
    vertical = jnp.where((row == 7) & (strip == 127), 0.0, stiff_ref[1])
    offset = solve_right_side(
        comps, [inertial_ref[k] for k in range(3)], left_ref[...], right_ref[...],
        [row_ref[k : k + 1, :] for k in range(3)], above_rows, above_weight, ext_ref[0], ext_ref[1],
        vertical, stiff_ref, inv_ref, base_ref,
    )
    write_offsets(offset, sends_ref, msg_ref)


def plane_vectors(got_ref, wh_ref, wl_ref, vec_ref):
    x = lax.axis_index("x")
    sib = x + 1 - 2 * low_bit("x")
    far = 4 - 4 * high_bit("x")
    vec_ref[...] = jnp.zeros(vec_ref.shape, F32)
    put_vector(vec_ref, 0, got_ref[2 * x])
    put_vector(vec_ref, 1, got_ref[2 * x + 1])
    put_vector(vec_ref, 2, got_ref[2 * sib] + got_ref[2 * sib + 1])
    others = (got_ref[far] + got_ref[far + 1]) + (got_ref[far + 2] + got_ref[far + 3])
    put_vector(vec_ref, 3, others)
    return apply_map(vec_ref[...].astype(BF16), wh_ref[...], wl_ref[...])


def send_vectors(total, maps_ref, joint_ref, msg_ref):
    zh = lax.axis_index("zh")
    vec = stacked(total)
    pairs = apply_map(vec, maps_ref[0], maps_ref[1])[0:3]
    near = apply_map(vec, maps_ref[2], maps_ref[3])[0:3]
    far = apply_map(vec, joint_ref[0], joint_ref[1])[0:3]
    far = jnp.where(zh == 0, far, near)
    raw = total[0:3]
    for g in range(4):
        for h in range(2):
            inner = jnp.where(high_bit() == h, raw, pairs)
            value = jnp.where(zh == g, inner, near if g < 2 else far)
            msg_ref[4 * g + 2 * h] = value
            msg_ref[4 * g + 2 * h + 1] = value


def plane_kernel(got_ref, wh_ref, wl_ref, both_ref, vec_ref):
    both_ref[...] = plane_vectors(got_ref, wh_ref, wl_ref, vec_ref)


def plane_send_kernel(got_ref, wh_ref, wl_ref, maps_ref, joint_ref, both_ref, msg_ref, vec_ref):
    both = plane_vectors(got_ref, wh_ref, wl_ref, vec_ref)
    both_ref[...] = both
    send_vectors(both[:, :CB], maps_ref, joint_ref, msg_ref)


def finish(
    got_ref, both_ref, maps_ref, joint_ref, eh_ref, el_ref, stiff_ref, base_ref, inv_ref, vec_ref
):
    zh = lax.axis_index("zh")
    row = lax.broadcasted_iota(jnp.int32, (8, CB), 0)
    none = jnp.zeros((3, CB), F32)
    vec_ref[...] = jnp.zeros(vec_ref.shape, F32)
    first_two = got_ref[4 * zh] + got_ref[4 * zh + 1]
    put_vector(vec_ref, 0, jnp.where(high_bit() == 1, first_two, none))
    sums = [
        (got_ref[4 * g] + got_ref[4 * g + 1]) + (got_ref[4 * g + 2] + got_ref[4 * g + 3])
        for g in range(3)
    ]
    lower = jnp.where(zh >= 1, sums[0], none) + jnp.where(zh >= 2, sums[1], none)
    put_vector(vec_ref, 1, jnp.where(zh == 3, sums[2], lower))
    put_vector(vec_ref, 2, jnp.where(zh == 3, lower, none))
    vec = vec_ref[...].astype(BF16)
    arrived = apply_map(vec[:, :CB], maps_ref[4], maps_ref[5])
    arrived = arrived + apply_map(vec[:, CB : 2 * CB], maps_ref[6], maps_ref[7])
    arrived = arrived + apply_map(vec[:, 2 * CB :], joint_ref[0], joint_ref[1])
    beside = jnp.where(low_bit() == 1, got_ref[4 * zh + 2 * high_bit()], none)
    arrived = arrived + jnp.concatenate([beside, jnp.zeros((5, CB), F32)], axis=0)
    came = both_ref[:, CB:] + apply_map(stacked(arrived), eh_ref[...], el_ref[...])
    weights = stiff_ref[1]
    state = [base_ref[k] for k in range(3)]
    blank = jnp.zeros((8, CB), F32)
    for k in range(4):
        if k == 0:
            source = [jnp.broadcast_to(came[j : j + 1], (8, CB)) for j in range(3)]
        else:
            source = [weights * state[j] for j in range(3)]
        moved = halves_sum(dot_t(stacked(jnp.concatenate(source + [blank], axis=0)), inv_ref[k, :, :CB]))
        for j in range(3):
            part = moved[8 * j : 8 * j + 8]
            state[j] = state[j] + jnp.where(
                row == 2 * k,
                pltpu.roll(part[:, :CB], 1, 0),
                jnp.where(row == 2 * k + 1, pltpu.roll(part[:, CB:], 2, 0), 0.0),
            )
    return state, came


def middle_kernel(
    got_ref, both_ref, maps_ref, joint_ref, eh_ref, el_ref, stiff_ref, base_ref, inv_ref,
    u_ref, left_ref, right_ref, row_ref, vec_ref,
):
    state, came = finish(
        got_ref, both_ref, maps_ref, joint_ref, eh_ref, el_ref, stiff_ref, base_ref, inv_ref, vec_ref
    )
    for k in range(3):
        u_ref[k] = state[k]
    u_ref[3] = came
    left, right = edge_tiles(state, [])
    left_ref[...] = left
    right_ref[...] = right
    row_ref[...] = jnp.concatenate([state[0][0:1], state[1][0:1], state[2][0:1], state[0][0:1]], axis=0)


def final_kernel(
    got_ref, both_ref, maps_ref, joint_ref, eh_ref, el_ref, stiff_ref, base_ref, inv_ref,
    u_ref, vec_ref,
):
    state, came = finish(
        got_ref, both_ref, maps_ref, joint_ref, eh_ref, el_ref, stiff_ref, base_ref, inv_ref, vec_ref
    )
    for k in range(3):
        u_ref[k] = state[k]


def swap(value, axes):
    return lax.all_to_all(value, axes, 0, 0)


def shards(positions, target, inertia, stiffness, pin_columns, inverses):
    smem = pl.BlockSpec(memory_space=pltpu.SMEM)
    anywhere = pl.BlockSpec(memory_space=pl.ANY)

    hbm = pl.BlockSpec(memory_space=pltpu.HBM)
    own_map = call(
        local_map_kernel,
        sds((CB + 8, CB)),
        (inverses, stiffness, positions),
        specs=[hbm] * 3,
        scratch=[
            pltpu.VMEM((4, CB, CB), BF16),
            pltpu.VMEM((3, 8, CB), F32),
            pltpu.VMEM((3, 8, CB), F32),
            pltpu.SemaphoreType.DMA((6,)),
        ],
        flops=10**8,
        limit=WHOLE_VMEM,
    )
    core_maps = lax.all_gather(own_map, "c")
    square = sds((CB, CB))
    chip, near = call(chip_map_kernel, [square, sds((8, CB))], (core_maps,))
    sib_chip = lax.ppermute(chip, "x", [(k, k ^ 1) for k in range(4)])

    tile = sds((8, 128))
    rows = sds((4, CB))
    left, right, cross = call(
        halo_kernel, [tile, tile, rows], (positions, stiffness, chip), specs=[None, None, anywhere]
    )
    to_left = [(1, 0), (2, 1), (3, 2)]
    to_right = [(0, 1), (1, 2), (2, 3)]
    cores = [(0, 1), (1, 0)]
    from_right = lax.ppermute(left, "y", to_left)
    from_left = lax.ppermute(right, "y", to_right)
    two_chips, cross = call(
        two_chips_kernel,
        [square, rows],
        (chip, sib_chip, cross, from_left, from_right),
        specs=[None] * 3 + [anywhere] * 2,
    )
    far_chips = lax.ppermute(two_chips, "x", [(k, k ^ 2) for k in range(4)])
    pairs = [(2 * k + 1, 2 * k + 2) for k in range(63)]
    cross = lax.ppermute(cross, STRIP, pairs + [(b, a) for a, b in pairs])
    halos = (from_left, from_right, near, cross)
    plane = call(
        four_chips_kernel, square, (two_chips, far_chips, cross), specs=[None, None, anywhere]
    )
    beside = lax.ppermute(plane, ZAX, [(k, k ^ 1) for k in range(16)])

    field = sds((3, 8, CB))
    vector = sds((8, CB))
    base, offset, inertial, ext, above = call(
        first_side_kernel,
        [field, vector, field, sds((2, 8, 512)), vector],
        (positions, target, inertia, stiffness, pin_columns) + halos + (inverses, plane),
        specs=[None] * 4 + [smem] + [None] * 5 + [anywhere],
        flops=10**8,
        size=3 * 10**6,
    )
    wide = sds((4 * CB, 2 * CB), BF16)
    narrow = sds((CB, CB), BF16)
    xh, xl, eh, el, sends = call(
        plane_maps_kernel,
        [wide, wide, narrow, narrow, sds((4, CB, CB), BF16)],
        (chip, sib_chip, two_chips, far_chips, core_maps, plane),
        specs=[None] * 5 + [anywhere],
        flops=10**9,
    )
    half = sds((CB, 128))
    two, two_half = call(
        two_planes_kernel,
        [square, half],
        (plane, beside, base, eh),
        specs=[None, None, anywhere, anywhere],
    )
    two_mine = lax.ppermute(two_half, ZAX, [(k, k ^ 2) for k in range(16)])
    group_half = call(four_planes_kernel, half, (two, two_mine))
    steps = [(4 + k, k) for k in range(4)] + [(8 + k, 12 + k) for k in range(4)]
    far_mine = lax.ppermute(group_half, ZAX, steps)

    msg = call(
        offsets_kernel, sds((8, 3, CB)), (offset, sends, group_half), specs=[None, None, anywhere]
    )
    got = swap(msg, PLANE)
    both = call(
        plane_kernel,
        sds((8, 2 * CB)),
        (got, xh, xl),
        scratch=[pltpu.VMEM((16, 4 * CB), F32)],
        size=3 * 10**6,
    )
    mine = call(
        bundle_kernel, sds((2, CB, 128)), (two_mine, far_mine, both), specs=[None, None, anywhere]
    )
    other = lax.ppermute(mine, "c", cores)
    maps, joint, msg = call(
        group_maps_kernel,
        [sds((8, CB, CB), BF16), sds((2, CB, CB), BF16), sds((16, 3, CB))],
        (both, beside, mine, other),
        flops=5 * 10**8,
    )
    got = swap(msg, ZAX)
    middle, left, right, low_row = call(
        middle_kernel,
        [sds((4, 8, CB)), tile, tile, rows],
        (got, both, maps, joint, eh, el, stiffness, base, inverses),
        scratch=[pltpu.VMEM((16, 3 * CB), F32)],
        flops=10**8,
    )

    low_row = lax.ppermute(low_row, STRIP, [(k + 1, k) for k in range(127)])
    from_right = lax.ppermute(left, "y", to_left)
    from_left = lax.ppermute(right, "y", to_right)
    base, msg = call(
        second_side_kernel,
        [field, sds((8, 3, CB))],
        (middle, stiffness, from_left, from_right, low_row, inverses, sends)
        + (inertial, ext, above),
        flops=10**8,
        size=3 * 10**6,
    )
    got = swap(msg, PLANE)
    both, msg = call(
        plane_send_kernel,
        [sds((8, 2 * CB)), sds((16, 3, CB))],
        (got, xh, xl, maps, joint),
        scratch=[pltpu.VMEM((16, 4 * CB), F32)],
        size=3 * 10**6,
    )
    got = swap(msg, ZAX)
    return call(
        final_kernel,
        field,
        (got, both, maps, joint, eh, el, stiffness, base, inverses),
        scratch=[pltpu.VMEM((16, 3 * CB), F32)],
        flops=10**8,
    )


def solution(mesh):
    split = Mesh(mesh.devices.reshape(4, 4, 4, 2, 4), ("zh", "zl", "x", "c", "y"))
    return jax.shard_map(
        shards,
        mesh=split,
        in_specs=(
            P(None, STRIP, "y"),
            P(None, STRIP, "y"),
            P(STRIP, "y"),
            P(None, STRIP, "y"),
            P(),
            P(STRIP, None, None),
        ),
        out_specs=P(None, STRIP, "y"),
        check_vma=False,
    )
```

```python
import jax
import jax.numpy as jnp
from jax import lax
from jax.experimental import pallas as pl
from jax.experimental.pallas import tpu as pltpu
from jax.sharding import Mesh
from jax.sharding import PartitionSpec as P

F32 = jnp.float32
BF16 = jnp.bfloat16
STRIP = ("zh", "zl", "x", "c")
ZAX = ("zh", "zl")
PLANE = ("x", "c")
CB = 256
PIN = 20.0
VMEM_LIMIT = 14 * 1024 * 1024
WHOLE_VMEM = 64 * 1024 * 1024 - 96 * 1024


def dot(a, b):
    return lax.dot_general(a, b, (((1,), (0,)), ((), ())), preferred_element_type=F32)


def dot_t(a, b):
    return lax.dot_general(a, b, (((1,), (1,)), ((), ())), preferred_element_type=F32)


def pair(value):
    high = value.astype(BF16)
    low = (value - high.astype(F32)).astype(BF16)
    return high, low


def mm(a, b):
    return dot(a[0], b[0]) + (dot(a[0], b[1]) + dot(a[1], b[0]))


def eye():
    rows = lax.broadcasted_iota(jnp.int32, (CB, CB), 0)
    cols = lax.broadcasted_iota(jnp.int32, (CB, CB), 1)
    return jnp.where(rows == cols, 1.0, 0.0).astype(F32)


def stacked(value):
    high = value.astype(BF16)
    low = value - high.astype(F32)
    return jnp.concatenate([high.astype(F32), low], axis=0).astype(BF16)


def halves_sum(value):
    half = value.shape[0] // 2
    return value[:half] + value[half:]


def put_vector(vec_ref, slot, value):
    high = value.astype(BF16).astype(F32)
    vec_ref[0:3, slot * CB : (slot + 1) * CB] = high
    vec_ref[8:11, slot * CB : (slot + 1) * CB] = value - high


def apply_map(vec, high, low):
    return halves_sum(dot(vec, high) + dot(vec, low))


def call(kernel, outs, args, specs=None, scratch=(), flops=10**7, size=10**6, limit=VMEM_LIMIT):
    vmem = pl.BlockSpec(memory_space=pltpu.VMEM)
    in_specs = [vmem] * len(args) if specs is None else [vmem if s is None else s for s in specs]
    many = isinstance(outs, (list, tuple))
    out_specs = [vmem] * len(outs) if many else vmem
    return pl.pallas_call(
        kernel,
        out_shape=outs,
        in_specs=in_specs,
        out_specs=out_specs,
        scratch_shapes=list(scratch),
        compiler_params=pltpu.CompilerParams(vmem_limit_bytes=limit),
        cost_estimate=pl.CostEstimate(flops=flops, bytes_accessed=size, transcendentals=0),
    )(*args)


def sds(shape, dtype=F32):
    return jax.ShapeDtypeStruct(shape, dtype)


def local_map_kernel(inv_hbm, stiff_hbm, u_hbm, out_ref, inv_ref, stiff_ref, u_ref, sems):
    copies = [
        pltpu.make_async_copy(stiff_hbm, stiff_ref, sems.at[4]),
        pltpu.make_async_copy(u_hbm, u_ref, sems.at[5]),
    ]
    copies += [
        pltpu.make_async_copy(inv_hbm.at[k, CB : 2 * CB, 0:CB], inv_ref.at[k], sems.at[k])
        for k in range(4)
    ]
    for copy in copies:
        copy.start()
    core = lax.axis_index("c")
    copies[0].wait()
    copies[2].wait()
    first = dot_t(eye().astype(BF16), inv_ref[0]) * stiff_ref[1, 1:2, :]
    for k in range(1, 4):
        copies[2 + k].wait()
        high, low = pair(first)
        first = (dot_t(high, inv_ref[k]) + dot_t(low, inv_ref[k])) * stiff_ref[
            1, 2 * k + 1 : 2 * k + 2, :
        ]
    out_ref[0:CB, :] = first
    copies[1].wait()
    rows = [u_ref[k] for k in range(3)] + [stiff_ref[1]]
    rows = [jnp.where(core == 0, r[7:8], r[0:1]) for r in rows]
    out_ref[CB : CB + 8, :] = jnp.concatenate(rows + rows, axis=0)


def chip_map_kernel(both_ref, out_ref, near_ref):
    core = lax.axis_index("c")
    out_ref[...] = mm(pair(both_ref[0, 0:CB, :]), pair(both_ref[1, 0:CB, :]))
    tails = [both_ref[k, CB : CB + 8, :] for k in range(2)]
    near_ref[...] = jnp.where(core == 0, tails[1], tails[0])


def low_bit(axis="zl"):
    return lax.rem(lax.axis_index(axis), 2)


def high_bit(axis="zl"):
    return lax.div(lax.axis_index(axis), 2)


def in_order(own, other, right):
    return jnp.where(right, other, own), jnp.where(right, own, other)


def two_chips_kernel(own_ref, other_ref, cross_ref, after_ref, out_ref, row_ref):
    left_map, right_map = in_order(own_ref[...], other_ref[...], low_bit("x") == 1)
    out_ref[...] = mm(pair(left_map), pair(right_map))
    row_ref[...] = cross_ref[...]


def four_chips_kernel(own_ref, other_ref, edge_ref, after_ref, out_ref, tile_ref):
    tile_ref[...] = edge_ref[...]
    left_map, right_map = in_order(own_ref[...], other_ref[...], high_bit("x") == 1)
    out_ref[...] = mm(pair(left_map), pair(right_map))


def rows_of_half(half):
    return jnp.concatenate([half[:128], half[128:]], axis=1)


def half_of_rows(rows):
    return jnp.concatenate([rows[:, :128], rows[:, 128:]], axis=0)


def joined(mine_ref, other_ref):
    core = lax.axis_index("c")
    first, second = in_order(mine_ref[...], other_ref[...], core == 1)
    columns = jnp.concatenate([first, second], axis=1)
    rows = jnp.concatenate([rows_of_half(first), rows_of_half(second)], axis=0)
    return jnp.where(high_bit() == 0, columns, rows)


def two_planes_kernel(own_ref, other_ref, *rest):
    out_ref, half_ref = rest[-2:]
    core = lax.axis_index("c")
    left_map, right_map = in_order(own_ref[...], other_ref[...], low_bit() == 1)
    product = mm(pair(left_map), pair(right_map))
    out_ref[...] = product
    columns = jnp.where(core == 0, product[:, :128], product[:, 128:])
    rows = half_of_rows(jnp.where(core == 0, product[:128], product[128:]))
    half_ref[...] = jnp.where(high_bit() == 0, rows, columns)


def four_planes_kernel(own_ref, half_ref, after_ref, out_ref):
    own = pair(own_ref[...])
    half = half_ref[...]
    columns = mm(own, pair(half))
    rows = half_of_rows(mm(pair(rows_of_half(half)), own))
    out_ref[...] = jnp.where(high_bit() == 0, columns, rows)


def plane_maps_kernel(
    own_ref, sib_ref, two_ref, far_ref, cores_ref, after_ref, wh_ref, wl_ref, eh_ref, el_ref, sends_ref
):
    core = lax.axis_index("c")
    one = eye()
    low, high = low_bit("x"), high_bit("x")
    own, sib, two, far = own_ref[...], sib_ref[...], two_ref[...], far_ref[...]
    first, second = cores_ref[0, 0:CB, :], cores_ref[1, 0:CB, :]

    def store(slot, col, value):
        parts = pair(value)
        wh_ref[slot * CB : (slot + 1) * CB, col * CB : (col + 1) * CB] = parts[0]
        wl_ref[slot * CB : (slot + 1) * CB, col * CB : (col + 1) * CB] = parts[1]

    sib_after = jnp.where(low == 0, sib, one)
    rest = pair(jnp.where(high == 0, far, one))
    to_end = mm(pair(sib_after), rest)
    store(0, 0, mm(pair(second), pair(to_end)))
    store(1, 0, to_end)
    store(2, 0, mm(pair(jnp.where(low == 0, one, own)), rest))
    store(3, 0, jnp.where(high == 1, two, one))
    none = jnp.zeros((CB, CB), F32)
    core_before = jnp.where(core == 1, first, one)
    chip_before = mm(pair(jnp.where(low == 1, sib, one)), pair(core_before))
    store(0, 1, jnp.where(core == 1, one, none))
    store(1, 1, none)
    store(2, 1, jnp.where(low == 1, core_before, none))
    store(3, 1, jnp.where(high == 1, chip_before, none))
    parts = pair(mm(pair(jnp.where(high == 1, far, one)), pair(chip_before)))
    eh_ref[...] = parts[0]
    el_ref[...] = parts[1]
    core_after = jnp.where(core == 0, second, one)
    parts = pair(core_after)
    sends_ref[0] = parts[0]
    sends_ref[1] = parts[1]
    parts = pair(mm(parts, pair(sib_after)))
    sends_ref[2] = parts[0]
    sends_ref[3] = parts[1]


def bundle_kernel(two_ref, far_ref, after_ref, out_ref):
    out_ref[0] = two_ref[...]
    out_ref[1] = far_ref[...]


def group_maps_kernel(both_ref, one_ref, mine_ref, other_ref, out_ref, joint_ref, msg_ref):
    zh = lax.axis_index("zh")
    one = eye()
    sibling = one_ref[...]
    two = pair(joined(mine_ref.at[0], other_ref.at[0]))
    far = joined(mine_ref.at[1], other_ref.at[1])
    send = jnp.where(low_bit() == 0, sibling, one)
    take = jnp.where(low_bit() == 1, sibling, one)
    for k, value in ((0, send), (4, take)):
        parts = pair(value)
        out_ref[k] = parts[0]
        out_ref[k + 1] = parts[1]
    send = jnp.where(high_bit() == 0, mm(pair(send), two), send)
    take = jnp.where(high_bit() == 1, mm(two, pair(take)), take)
    for k, value in ((2, send), (6, take)):
        parts = pair(value)
        out_ref[k] = parts[0]
        out_ref[k + 1] = parts[1]
    left = jnp.where(zh == 0, send, far)
    right = jnp.where(zh == 0, far, take)
    joint = pair(mm(pair(left), pair(right)))
    joint_ref[0] = joint[0]
    joint_ref[1] = joint[1]
    send_vectors(both_ref[:, :CB], out_ref, joint_ref, msg_ref)


def edge_tiles(comps, weights):
    lane = lax.broadcasted_iota(jnp.int32, (8, 128), 1)
    right = jnp.zeros((8, 128), F32)
    left = jnp.zeros((8, 128), F32)
    for k, value in enumerate(comps + weights):
        mask = (lane == 2 * k) | (lane == 2 * k + 1)
        right = jnp.where(mask, pltpu.roll(value[:, 128:], (2 * k - 126) % 128, 1), right)
        if k < 3:
            left = jnp.where(mask, pltpu.roll(value[:, :128], 2 * k, 1), left)
    return left, right


def halo_kernel(u_ref, stiff_ref, after_ref, left_ref, right_ref, cross_ref):
    core = lax.axis_index("c")
    comps = [u_ref[k] for k in range(3)]
    left, right = edge_tiles(comps, [stiff_ref[0], stiff_ref[2]])
    left_ref[...] = left
    right_ref[...] = right
    for k, rows in enumerate(comps + [stiff_ref[1]]):
        cross_ref[k : k + 1, :] = jnp.where(core == 0, rows[0:1], rows[7:8])


def springs(ends, others, weight, rest, length):
    gaps = [o - e for o, e in zip(others, ends)]
    gaps = [g + r if r != 0.0 else g for g, r in zip(gaps, rest)]
    norm = jnp.sqrt(gaps[0] * gaps[0] + gaps[1] * gaps[1] + gaps[2] * gaps[2])
    factor = length / jnp.maximum(norm, 0.5 * length)
    return [weight * (g * factor - r if r != 0.0 else g * factor) for g, r in zip(gaps, rest)]


def solve_right_side(
    comps, inertial, from_left, from_right, below_rows, above_rows, above_weight, h_ext, b_ext,
    vertical, stiff_ref, inv_ref, base_ref,
):
    row = lax.broadcasted_iota(jnp.int32, (8, CB), 0)
    lane = lax.broadcasted_iota(jnp.int32, (8, 512), 1)
    wide = []
    for k in range(3):
        head = pltpu.roll(from_left, 126 - 2 * k, 1)
        tail = pltpu.roll(from_right, (-2 * k) % 128, 1) if k else from_right
        wide.append(jnp.concatenate([head, comps[k], tail], axis=1))
    total = [jnp.zeros((8, 512), F32)] * 3
    for offset, weight in ((1, h_ext), (2, b_ext)):
        shifted = [pltpu.roll(w, 512 - offset, 1) for w in wide]
        rest = (float(offset), 0.0, 0.0)
        pulls = springs(wide, shifted, weight, rest, float(offset))
        crossing = ((lane >= 128 - offset) & (lane < 128)) | (
            (lane >= 384 - offset) & (lane < 384)
        )
        across = jnp.where(crossing, weight, 0.0)
        for k in range(3):
            here = across * shifted[k] - pulls[k]
            there = across * wide[k] + pulls[k]
            total[k] = total[k] + here + pltpu.roll(there, offset, 1)
    lower = [
        jnp.where(row == 7, below_rows[k], pltpu.roll(comps[k], 7, 0)) for k in range(3)
    ]
    down = springs(comps, lower, vertical, (0.0, 1.0, 0.0), 1.0)
    upper = springs(
        above_rows, [c[0:1] for c in comps], above_weight, (0.0, 1.0, 0.0), 1.0
    )
    below_weight = jnp.where(lax.rem(row, 2) == 1, vertical, 0.0)
    rhs = []
    for k in range(3):
        received = jnp.where(row == 0, upper[k], pltpu.roll(down[k], 1, 0))
        rhs.append(
            inertial[k] + total[k][:, 128:384] + received - down[k] + below_weight * lower[k]
        )
    first = jnp.concatenate(rhs + [jnp.zeros((8, CB), F32)], axis=0)
    second = jnp.concatenate(
        [pltpu.roll(r, 7, 0) for r in rhs] + [jnp.zeros((8, CB), F32)], axis=0
    )
    wide_rhs = stacked(jnp.concatenate([first, second], axis=1))
    base = [jnp.zeros((8, CB), F32)] * 3
    for k in range(4):
        solved = halves_sum(dot_t(wide_rhs, inv_ref[k]))
        for j in range(3):
            part = solved[8 * j : 8 * j + 8]
            base[j] = jnp.where(
                row == 2 * k,
                part[:, :CB],
                jnp.where(row == 2 * k + 1, pltpu.roll(part[:, CB:], 1, 0), base[j]),
            )
    for j in range(3):
        base_ref[j] = base[j]
    weights = stiff_ref[1]
    last = base
    for k in range(1, 4):
        carried = jnp.concatenate(
            [weights * last[j] for j in range(3)] + [jnp.zeros((8, CB), F32)], axis=0
        )
        moved = halves_sum(dot_t(stacked(carried), inv_ref[k, CB:, :CB]))
        last = [
            jnp.where(row == 2 * k + 1, base[j] + pltpu.roll(moved[8 * j : 8 * j + 8], 2, 0), last[j])
            for j in range(3)
        ]
    rows = [(weights * last[j])[7:8] for j in range(3)]
    return jnp.concatenate(rows + [jnp.zeros((5, CB), F32)], axis=0)


def write_offsets(offset, sends_ref, msg_ref):
    core = lax.axis_index("c")
    x = lax.axis_index("x")
    vec = stacked(offset)
    raw = offset[0:3]
    beside = jnp.where(core == 0, apply_map(vec, sends_ref[0], sends_ref[1])[0:3], raw)
    far = apply_map(vec, sends_ref[2], sends_ref[3])[0:3]
    for k in range(4):
        value = jnp.where(high_bit("x") == k // 2, beside, far)
        value = jnp.where(x == k, raw, value)
        msg_ref[2 * k] = value
        msg_ref[2 * k + 1] = value


def offsets_kernel(offset_ref, sends_ref, msg_ref):
    write_offsets(offset_ref[...], sends_ref, msg_ref)


def first_side_kernel(
    u_ref, target_ref, inertia_ref, stiff_ref, pin_ref, left_ref, right_ref, near_ref, cross_ref,
    inv_ref, after_ref, base_ref, offset_ref, inertial_ref, ext_ref, above_ref,
):
    core = lax.axis_index("c")
    y = lax.axis_index("y")
    strip = (lax.axis_index("zh") * 4 + lax.axis_index("zl")) * 8 + lax.axis_index("x") * 2 + core
    comps = [u_ref[k] for k in range(3)]
    row = lax.broadcasted_iota(jnp.int32, (8, CB), 0)
    column = lax.broadcasted_iota(jnp.int32, (8, CB), 1) + y * CB
    hit = column < 0
    for k in range(pin_ref.shape[0]):
        hit = hit | (column == pin_ref[k])
    pinned = hit & (row == 0) & (strip == 0)
    inertial = []
    for k in range(3):
        value = inertia_ref[...] * target_ref[k] + PIN * jnp.where(pinned, comps[k], 0.0)
        inertial.append(value)
        inertial_ref[k] = value
    lane = lax.broadcasted_iota(jnp.int32, (8, 512), 1)
    from_left = left_ref[...]
    extended = []
    for k, channel, offset in ((3, 0, 1), (4, 2, 2)):
        head = pltpu.roll(from_left, 126 - 2 * k, 1)
        weight = jnp.concatenate([head, stiff_ref[channel], jnp.zeros((8, 128), F32)], axis=1)
        low = jnp.where(y == 0, 128, 128 - offset)
        high = jnp.where(y == 3, 384 - offset, 384)
        weight = jnp.where((lane >= low) & (lane < high), weight, 0.0)
        extended.append(weight)
        ext_ref[k - 3] = weight
    near, cross = near_ref[0:4, :], cross_ref[...]
    above = jnp.where(core == 0, cross, near)
    below = jnp.where(core == 0, near, cross)
    above_weight = jnp.where(strip == 0, 0.0, above[3:4])
    above_ref[...] = jnp.broadcast_to(above_weight, (8, CB))
    vertical = jnp.where((row == 7) & (strip == 127), 0.0, stiff_ref[1])
    offset_ref[...] = solve_right_side(
        comps, inertial, from_left, right_ref[...], [below[k : k + 1] for k in range(3)],
        [above[k : k + 1] for k in range(3)], above_weight, extended[0], extended[1], vertical,
        stiff_ref, inv_ref, base_ref,
    )


def second_side_kernel(
    u_ref, stiff_ref, left_ref, right_ref, row_ref, inv_ref, sends_ref, inertial_ref, ext_ref,
    above_ref, base_ref, msg_ref,
):
    core = lax.axis_index("c")
    y = lax.axis_index("y")
    strip = (lax.axis_index("zh") * 4 + lax.axis_index("zl")) * 8 + lax.axis_index("x") * 2 + core
    comps = [u_ref[k] for k in range(3)]
    row = lax.broadcasted_iota(jnp.int32, (8, CB), 0)
    above_weight = above_ref[0:1, :]
    divisor = jnp.where(strip == 0, 1.0, above_weight)
    above_rows = [u_ref[3, k : k + 1, :] / divisor for k in range(3)]
    vertical = jnp.where((row == 7) & (strip == 127), 0.0, stiff_ref[1])
    offset = solve_right_side(
        comps, [inertial_ref[k] for k in range(3)], left_ref[...], right_ref[...],
        [row_ref[k : k + 1, :] for k in range(3)], above_rows, above_weight, ext_ref[0], ext_ref[1],
        vertical, stiff_ref, inv_ref, base_ref,
    )
    write_offsets(offset, sends_ref, msg_ref)


def plane_vectors(got_ref, wh_ref, wl_ref, vec_ref):
    x = lax.axis_index("x")
    sib = x + 1 - 2 * low_bit("x")
    far = 4 - 4 * high_bit("x")
    vec_ref[...] = jnp.zeros(vec_ref.shape, F32)
    put_vector(vec_ref, 0, got_ref[2 * x])
    put_vector(vec_ref, 1, got_ref[2 * x + 1])
    put_vector(vec_ref, 2, got_ref[2 * sib] + got_ref[2 * sib + 1])
    others = (got_ref[far] + got_ref[far + 1]) + (got_ref[far + 2] + got_ref[far + 3])
    put_vector(vec_ref, 3, others)
    return apply_map(vec_ref[...].astype(BF16), wh_ref[...], wl_ref[...])


def send_vectors(total, maps_ref, joint_ref, msg_ref):
    zh = lax.axis_index("zh")
    vec = stacked(total)
    pairs = apply_map(vec, maps_ref[0], maps_ref[1])[0:3]
    near = apply_map(vec, maps_ref[2], maps_ref[3])[0:3]
    far = apply_map(vec, joint_ref[0], joint_ref[1])[0:3]
    far = jnp.where(zh == 0, far, near)
    raw = total[0:3]
    for g in range(4):
        for h in range(2):
            inner = jnp.where(high_bit() == h, raw, pairs)
            value = jnp.where(zh == g, inner, near if g < 2 else far)
            msg_ref[4 * g + 2 * h] = value
            msg_ref[4 * g + 2 * h + 1] = value


def plane_kernel(got_ref, wh_ref, wl_ref, both_ref, vec_ref):
    both_ref[...] = plane_vectors(got_ref, wh_ref, wl_ref, vec_ref)


def plane_send_kernel(got_ref, wh_ref, wl_ref, maps_ref, joint_ref, both_ref, msg_ref, vec_ref):
    both = plane_vectors(got_ref, wh_ref, wl_ref, vec_ref)
    both_ref[...] = both
    send_vectors(both[:, :CB], maps_ref, joint_ref, msg_ref)


def finish(
    got_ref, both_ref, maps_ref, joint_ref, eh_ref, el_ref, stiff_ref, base_ref, inv_ref, vec_ref
):
    zh = lax.axis_index("zh")
    row = lax.broadcasted_iota(jnp.int32, (8, CB), 0)
    none = jnp.zeros((3, CB), F32)
    vec_ref[...] = jnp.zeros(vec_ref.shape, F32)
    first_two = got_ref[4 * zh] + got_ref[4 * zh + 1]
    put_vector(vec_ref, 0, jnp.where(high_bit() == 1, first_two, none))
    sums = [
        (got_ref[4 * g] + got_ref[4 * g + 1]) + (got_ref[4 * g + 2] + got_ref[4 * g + 3])
        for g in range(3)
    ]
    lower = jnp.where(zh >= 1, sums[0], none) + jnp.where(zh >= 2, sums[1], none)
    put_vector(vec_ref, 1, jnp.where(zh == 3, sums[2], lower))
    put_vector(vec_ref, 2, jnp.where(zh == 3, lower, none))
    vec = vec_ref[...].astype(BF16)
    arrived = apply_map(vec[:, :CB], maps_ref[4], maps_ref[5])
    arrived = arrived + apply_map(vec[:, CB : 2 * CB], maps_ref[6], maps_ref[7])
    arrived = arrived + apply_map(vec[:, 2 * CB :], joint_ref[0], joint_ref[1])
    beside = jnp.where(low_bit() == 1, got_ref[4 * zh + 2 * high_bit()], none)
    arrived = arrived + jnp.concatenate([beside, jnp.zeros((5, CB), F32)], axis=0)
    came = both_ref[:, CB:] + apply_map(stacked(arrived), eh_ref[...], el_ref[...])
    weights = stiff_ref[1]
    state = [base_ref[k] for k in range(3)]
    blank = jnp.zeros((8, CB), F32)
    for k in range(4):
        if k == 0:
            source = [jnp.broadcast_to(came[j : j + 1], (8, CB)) for j in range(3)]
        else:
            source = [weights * state[j] for j in range(3)]
        moved = halves_sum(dot_t(stacked(jnp.concatenate(source + [blank], axis=0)), inv_ref[k, :, :CB]))
        for j in range(3):
            part = moved[8 * j : 8 * j + 8]
            state[j] = state[j] + jnp.where(
                row == 2 * k,
                pltpu.roll(part[:, :CB], 1, 0),
                jnp.where(row == 2 * k + 1, pltpu.roll(part[:, CB:], 2, 0), 0.0),
            )
    return state, came


def middle_kernel(
    got_ref, both_ref, maps_ref, joint_ref, eh_ref, el_ref, stiff_ref, base_ref, inv_ref,
    u_ref, left_ref, right_ref, row_ref, vec_ref,
):
    state, came = finish(
        got_ref, both_ref, maps_ref, joint_ref, eh_ref, el_ref, stiff_ref, base_ref, inv_ref, vec_ref
    )
    for k in range(3):
        u_ref[k] = state[k]
    u_ref[3] = came
    left, right = edge_tiles(state, [])
    left_ref[...] = left
    right_ref[...] = right
    row_ref[...] = jnp.concatenate([state[0][0:1], state[1][0:1], state[2][0:1], state[0][0:1]], axis=0)


def final_kernel(
    got_ref, both_ref, maps_ref, joint_ref, eh_ref, el_ref, stiff_ref, base_ref, inv_ref,
    u_ref, vec_ref,
):
    state, came = finish(
        got_ref, both_ref, maps_ref, joint_ref, eh_ref, el_ref, stiff_ref, base_ref, inv_ref, vec_ref
    )
    for k in range(3):
        u_ref[k] = state[k]


def swap(value, axes):
    return lax.all_to_all(value, axes, 0, 0)


def shards(positions, target, inertia, stiffness, pin_columns, inverses):
    smem = pl.BlockSpec(memory_space=pltpu.SMEM)
    anywhere = pl.BlockSpec(memory_space=pl.ANY)

    hbm = pl.BlockSpec(memory_space=pltpu.HBM)
    own_map = call(
        local_map_kernel,
        sds((CB + 8, CB)),
        (inverses, stiffness, positions),
        specs=[hbm] * 3,
        scratch=[
            pltpu.VMEM((4, CB, CB), BF16),
            pltpu.VMEM((3, 8, CB), F32),
            pltpu.VMEM((3, 8, CB), F32),
            pltpu.SemaphoreType.DMA((6,)),
        ],
        flops=10**8,
        limit=WHOLE_VMEM,
    )
    core_maps = lax.all_gather(own_map, "c")
    square = sds((CB, CB))
    chip, near = call(chip_map_kernel, [square, sds((8, CB))], (core_maps,))
    sib_chip = lax.ppermute(chip, "x", [(k, k ^ 1) for k in range(4)])

    tile = sds((8, 128))
    rows = sds((4, CB))
    left, right, cross = call(
        halo_kernel, [tile, tile, rows], (positions, stiffness, chip), specs=[None, None, anywhere]
    )
    to_left = [(1, 0), (2, 1), (3, 2)]
    to_right = [(0, 1), (1, 2), (2, 3)]
    cores = [(0, 1), (1, 0)]
    from_right = lax.ppermute(left, "y", to_left)
    two_chips, cross = call(
        two_chips_kernel,
        [square, rows],
        (chip, sib_chip, cross, from_right),
        specs=[None] * 3 + [anywhere],
    )
    far_chips = lax.ppermute(two_chips, "x", [(k, k ^ 2) for k in range(4)])
    pairs = [(2 * k + 1, 2 * k + 2) for k in range(63)]
    cross = lax.ppermute(cross, STRIP, pairs + [(b, a) for a, b in pairs])
    plane, right = call(
        four_chips_kernel,
        [square, tile],
        (two_chips, far_chips, right, cross),
        specs=[None] * 3 + [anywhere],
    )
    beside = lax.ppermute(plane, ZAX, [(k, k ^ 1) for k in range(16)])

    from_left = lax.ppermute(right, "y", to_right)
    half = sds((CB, 128))
    two, two_half = call(
        two_planes_kernel, [square, half], (plane, beside, from_left), specs=[None, None, anywhere]
    )
    two_mine = lax.ppermute(two_half, ZAX, [(k, k ^ 2) for k in range(16)])

    halos = (from_left, from_right, near, cross)
    field = sds((3, 8, CB))
    vector = sds((8, CB))
    base, offset, inertial, ext, above = call(
        first_side_kernel,
        [field, vector, field, sds((2, 8, 512)), vector],
        (positions, target, inertia, stiffness, pin_columns) + halos + (inverses, two),
        specs=[None] * 4 + [smem] + [None] * 5 + [anywhere],
        flops=10**8,
        size=3 * 10**6,
    )
    group_half = call(
        four_planes_kernel, half, (two, two_mine, base), specs=[None, None, anywhere]
    )
    steps = [(4 + k, k) for k in range(4)] + [(8 + k, 12 + k) for k in range(4)]
    far_mine = lax.ppermute(group_half, ZAX, steps)

    wide = sds((4 * CB, 2 * CB), BF16)
    narrow = sds((CB, CB), BF16)
    xh, xl, eh, el, sends = call(
        plane_maps_kernel,
        [wide, wide, narrow, narrow, sds((4, CB, CB), BF16)],
        (chip, sib_chip, two_chips, far_chips, core_maps, group_half),
        specs=[None] * 5 + [anywhere],
        flops=10**9,
    )
    msg = call(offsets_kernel, sds((8, 3, CB)), (offset, sends))
    got = swap(msg, PLANE)
    both = call(
        plane_kernel,
        sds((8, 2 * CB)),
        (got, xh, xl),
        scratch=[pltpu.VMEM((16, 4 * CB), F32)],
        size=3 * 10**6,
    )
    mine = call(
        bundle_kernel, sds((2, CB, 128)), (two_mine, far_mine, both), specs=[None, None, anywhere]
    )
    other = lax.ppermute(mine, "c", cores)
    maps, joint, msg = call(
        group_maps_kernel,
        [sds((8, CB, CB), BF16), sds((2, CB, CB), BF16), sds((16, 3, CB))],
        (both, beside, mine, other),
        flops=5 * 10**8,
    )
    got = swap(msg, ZAX)
    middle, left, right, low_row = call(
        middle_kernel,
        [sds((4, 8, CB)), tile, tile, rows],
        (got, both, maps, joint, eh, el, stiffness, base, inverses),
        scratch=[pltpu.VMEM((16, 3 * CB), F32)],
        flops=10**8,
    )

    low_row = lax.ppermute(low_row, STRIP, [(k + 1, k) for k in range(127)])
    from_right = lax.ppermute(left, "y", to_left)
    from_left = lax.ppermute(right, "y", to_right)
    base, msg = call(
        second_side_kernel,
        [field, sds((8, 3, CB))],
        (middle, stiffness, from_left, from_right, low_row, inverses, sends)
        + (inertial, ext, above),
        flops=10**8,
        size=3 * 10**6,
    )
    got = swap(msg, PLANE)
    both, msg = call(
        plane_send_kernel,
        [sds((8, 2 * CB)), sds((16, 3, CB))],
        (got, xh, xl, maps, joint),
        scratch=[pltpu.VMEM((16, 4 * CB), F32)],
        size=3 * 10**6,
    )
    got = swap(msg, ZAX)
    return call(
        final_kernel,
        field,
        (got, both, maps, joint, eh, el, stiffness, base, inverses),
        scratch=[pltpu.VMEM((16, 3 * CB), F32)],
        flops=10**8,
    )


def solution(mesh):
    split = Mesh(mesh.devices.reshape(4, 4, 4, 2, 4), ("zh", "zl", "x", "c", "y"))
    return jax.shard_map(
        shards,
        mesh=split,
        in_specs=(
            P(None, STRIP, "y"),
            P(None, STRIP, "y"),
            P(STRIP, "y"),
            P(None, STRIP, "y"),
            P(),
            P(STRIP, None, None),
        ),
        out_specs=P(None, STRIP, "y"),
        check_vma=False,
    )
```

```python
import jax
import jax.numpy as jnp
from jax import lax
from jax.experimental import pallas as pl
from jax.experimental.pallas import tpu as pltpu
from jax.sharding import Mesh
from jax.sharding import PartitionSpec as P

F32 = jnp.float32
BF16 = jnp.bfloat16
STRIP = ("zh", "zl", "x", "c")
ZAX = ("zh", "zl")
PLANE = ("x", "c")
CB = 256
PIN = 20.0
VMEM_LIMIT = 14 * 1024 * 1024
WHOLE_VMEM = 64 * 1024 * 1024 - (64 + 280) * 1024


def dot(a, b):
    return lax.dot_general(a, b, (((1,), (0,)), ((), ())), preferred_element_type=F32)


def dot_t(a, b):
    return lax.dot_general(a, b, (((1,), (1,)), ((), ())), preferred_element_type=F32)


def pair(value):
    high = value.astype(BF16)
    low = (value - high.astype(F32)).astype(BF16)
    return high, low


def mm(a, b):
    return dot(a[0], b[0]) + (dot(a[0], b[1]) + dot(a[1], b[0]))


def eye():
    rows = lax.broadcasted_iota(jnp.int32, (CB, CB), 0)
    cols = lax.broadcasted_iota(jnp.int32, (CB, CB), 1)
    return jnp.where(rows == cols, 1.0, 0.0).astype(F32)


def stacked(value):
    high = value.astype(BF16)
    low = value - high.astype(F32)
    return jnp.concatenate([high.astype(F32), low], axis=0).astype(BF16)


def halves_sum(value):
    half = value.shape[0] // 2
    return value[:half] + value[half:]


def put_vector(vec_ref, slot, value):
    high = value.astype(BF16).astype(F32)
    vec_ref[0:3, slot * CB : (slot + 1) * CB] = high
    vec_ref[8:11, slot * CB : (slot + 1) * CB] = value - high


def apply_map(vec, high, low):
    return halves_sum(dot(vec, high) + dot(vec, low))


def call(kernel, outs, args, specs=None, scratch=(), flops=10**7, size=10**6, limit=VMEM_LIMIT):
    vmem = pl.BlockSpec(memory_space=pltpu.VMEM)
    in_specs = [vmem] * len(args) if specs is None else [vmem if s is None else s for s in specs]
    many = isinstance(outs, (list, tuple))
    out_specs = [vmem] * len(outs) if many else vmem
    return pl.pallas_call(
        kernel,
        out_shape=outs,
        in_specs=in_specs,
        out_specs=out_specs,
        scratch_shapes=list(scratch),
        compiler_params=pltpu.CompilerParams(vmem_limit_bytes=limit),
        cost_estimate=pl.CostEstimate(flops=flops, bytes_accessed=size, transcendentals=0),
    )(*args)


def sds(shape, dtype=F32):
    return jax.ShapeDtypeStruct(shape, dtype)


def local_map_kernel(inv_hbm, stiff_hbm, u_hbm, out_ref, inv_ref, stiff_ref, u_ref, sems):
    copies = [
        pltpu.make_async_copy(stiff_hbm, stiff_ref, sems.at[4]),
        pltpu.make_async_copy(u_hbm, u_ref, sems.at[5]),
    ]
    copies += [
        pltpu.make_async_copy(inv_hbm.at[k, CB : 2 * CB, 0:CB], inv_ref.at[k], sems.at[k])
        for k in range(4)
    ]
    for copy in copies:
        copy.start()
    core = lax.axis_index("c")
    copies[0].wait()
    copies[2].wait()
    first = dot_t(eye().astype(BF16), inv_ref[0]) * stiff_ref[1, 1:2, :]
    for k in range(1, 4):
        copies[2 + k].wait()
        high, low = pair(first)
        first = (dot_t(high, inv_ref[k]) + dot_t(low, inv_ref[k])) * stiff_ref[
            1, 2 * k + 1 : 2 * k + 2, :
        ]
    out_ref[0:CB, :] = first
    copies[1].wait()
    rows = [u_ref[k] for k in range(3)] + [stiff_ref[1]]
    rows = [jnp.where(core == 0, r[7:8], r[0:1]) for r in rows]
    out_ref[CB : CB + 8, :] = jnp.concatenate(rows + rows, axis=0)


def chip_map_kernel(both_ref, out_ref, near_ref):
    core = lax.axis_index("c")
    out_ref[...] = mm(pair(both_ref[0, 0:CB, :]), pair(both_ref[1, 0:CB, :]))
    tails = [both_ref[k, CB : CB + 8, :] for k in range(2)]
    near_ref[...] = jnp.where(core == 0, tails[1], tails[0])


def low_bit(axis="zl"):
    return lax.rem(lax.axis_index(axis), 2)


def high_bit(axis="zl"):
    return lax.div(lax.axis_index(axis), 2)


def in_order(own, other, right):
    return jnp.where(right, other, own), jnp.where(right, own, other)


def two_chips_kernel(own_ref, other_ref, cross_ref, after_ref, out_ref, row_ref):
    left_map, right_map = in_order(own_ref[...], other_ref[...], low_bit("x") == 1)
    out_ref[...] = mm(pair(left_map), pair(right_map))
    row_ref[...] = cross_ref[...]


def four_chips_kernel(own_ref, other_ref, edge_ref, after_ref, out_ref, tile_ref):
    tile_ref[...] = edge_ref[...]
    left_map, right_map = in_order(own_ref[...], other_ref[...], high_bit("x") == 1)
    out_ref[...] = mm(pair(left_map), pair(right_map))


def rows_of_half(half):
    return jnp.concatenate([half[:128], half[128:]], axis=1)


def half_of_rows(rows):
    return jnp.concatenate([rows[:, :128], rows[:, 128:]], axis=0)


def joined(mine_ref, other_ref):
    core = lax.axis_index("c")
    first, second = in_order(mine_ref[...], other_ref[...], core == 1)
    columns = jnp.concatenate([first, second], axis=1)
    rows = jnp.concatenate([rows_of_half(first), rows_of_half(second)], axis=0)
    return jnp.where(high_bit() == 0, columns, rows)


def two_planes_kernel(own_ref, other_ref, *rest):
    out_ref, half_ref = rest[-2:]
    core = lax.axis_index("c")
    left_map, right_map = in_order(own_ref[...], other_ref[...], low_bit() == 1)
    product = mm(pair(left_map), pair(right_map))
    out_ref[...] = product
    columns = jnp.where(core == 0, product[:, :128], product[:, 128:])
    rows = half_of_rows(jnp.where(core == 0, product[:128], product[128:]))
    half_ref[...] = jnp.where(high_bit() == 0, rows, columns)


def four_planes_kernel(own_ref, half_ref, after_ref, out_ref):
    own = pair(own_ref[...])
    half = half_ref[...]
    columns = mm(own, pair(half))
    rows = half_of_rows(mm(pair(rows_of_half(half)), own))
    out_ref[...] = jnp.where(high_bit() == 0, columns, rows)


def plane_maps_kernel(
    own_ref, sib_ref, two_ref, far_ref, cores_ref, after_ref, wh_ref, wl_ref, eh_ref, el_ref, sends_ref
):
    core = lax.axis_index("c")
    one = eye()
    low, high = low_bit("x"), high_bit("x")
    own, sib, two, far = own_ref[...], sib_ref[...], two_ref[...], far_ref[...]
    first, second = cores_ref[0, 0:CB, :], cores_ref[1, 0:CB, :]

    def store(slot, col, value):
        parts = pair(value)
        wh_ref[slot * CB : (slot + 1) * CB, col * CB : (col + 1) * CB] = parts[0]
        wl_ref[slot * CB : (slot + 1) * CB, col * CB : (col + 1) * CB] = parts[1]

    sib_after = jnp.where(low == 0, sib, one)
    rest = pair(jnp.where(high == 0, far, one))
    to_end = mm(pair(sib_after), rest)
    store(0, 0, mm(pair(second), pair(to_end)))
    store(1, 0, to_end)
    store(2, 0, mm(pair(jnp.where(low == 0, one, own)), rest))
    store(3, 0, jnp.where(high == 1, two, one))
    none = jnp.zeros((CB, CB), F32)
    core_before = jnp.where(core == 1, first, one)
    chip_before = mm(pair(jnp.where(low == 1, sib, one)), pair(core_before))
    store(0, 1, jnp.where(core == 1, one, none))
    store(1, 1, none)
    store(2, 1, jnp.where(low == 1, core_before, none))
    store(3, 1, jnp.where(high == 1, chip_before, none))
    parts = pair(mm(pair(jnp.where(high == 1, far, one)), pair(chip_before)))
    eh_ref[...] = parts[0]
    el_ref[...] = parts[1]
    core_after = jnp.where(core == 0, second, one)
    parts = pair(core_after)
    sends_ref[0] = parts[0]
    sends_ref[1] = parts[1]
    parts = pair(mm(parts, pair(sib_after)))
    sends_ref[2] = parts[0]
    sends_ref[3] = parts[1]


def bundle_kernel(two_ref, far_ref, after_ref, out_ref):
    out_ref[0] = two_ref[...]
    out_ref[1] = far_ref[...]


def group_maps_kernel(both_ref, one_ref, mine_ref, other_ref, out_ref, joint_ref, msg_ref):
    zh = lax.axis_index("zh")
    one = eye()
    sibling = one_ref[...]
    two = pair(joined(mine_ref.at[0], other_ref.at[0]))
    far = joined(mine_ref.at[1], other_ref.at[1])
    send = jnp.where(low_bit() == 0, sibling, one)
    take = jnp.where(low_bit() == 1, sibling, one)
    for k, value in ((0, send), (4, take)):
        parts = pair(value)
        out_ref[k] = parts[0]
        out_ref[k + 1] = parts[1]
    send = jnp.where(high_bit() == 0, mm(pair(send), two), send)
    take = jnp.where(high_bit() == 1, mm(two, pair(take)), take)
    for k, value in ((2, send), (6, take)):
        parts = pair(value)
        out_ref[k] = parts[0]
        out_ref[k + 1] = parts[1]
    left = jnp.where(zh == 0, send, far)
    right = jnp.where(zh == 0, far, take)
    joint = pair(mm(pair(left), pair(right)))
    joint_ref[0] = joint[0]
    joint_ref[1] = joint[1]
    send_vectors(both_ref[:, :CB], out_ref, joint_ref, msg_ref)


def edge_tiles(comps, weights):
    lane = lax.broadcasted_iota(jnp.int32, (8, 128), 1)
    right = jnp.zeros((8, 128), F32)
    left = jnp.zeros((8, 128), F32)
    for k, value in enumerate(comps + weights):
        mask = (lane == 2 * k) | (lane == 2 * k + 1)
        right = jnp.where(mask, pltpu.roll(value[:, 128:], (2 * k - 126) % 128, 1), right)
        if k < 3:
            left = jnp.where(mask, pltpu.roll(value[:, :128], 2 * k, 1), left)
    return left, right


def halo_kernel(u_ref, stiff_ref, after_ref, left_ref, right_ref, cross_ref):
    core = lax.axis_index("c")
    comps = [u_ref[k] for k in range(3)]
    left, right = edge_tiles(comps, [stiff_ref[0], stiff_ref[2]])
    left_ref[...] = left
    right_ref[...] = right
    for k, rows in enumerate(comps + [stiff_ref[1]]):
        cross_ref[k : k + 1, :] = jnp.where(core == 0, rows[0:1], rows[7:8])


def springs(ends, others, weight, rest, length):
    gaps = [o - e for o, e in zip(others, ends)]
    gaps = [g + r if r != 0.0 else g for g, r in zip(gaps, rest)]
    norm = jnp.sqrt(gaps[0] * gaps[0] + gaps[1] * gaps[1] + gaps[2] * gaps[2])
    factor = length / jnp.maximum(norm, 0.5 * length)
    return [weight * (g * factor - r if r != 0.0 else g * factor) for g, r in zip(gaps, rest)]


def solve_right_side(
    comps, inertial, from_left, from_right, below_rows, above_rows, above_weight, h_ext, b_ext,
    vertical, stiff_ref, inv_ref, base_ref,
):
    row = lax.broadcasted_iota(jnp.int32, (8, CB), 0)
    lane = lax.broadcasted_iota(jnp.int32, (8, 512), 1)
    wide = []
    for k in range(3):
        head = pltpu.roll(from_left, 126 - 2 * k, 1)
        tail = pltpu.roll(from_right, (-2 * k) % 128, 1) if k else from_right
        wide.append(jnp.concatenate([head, comps[k], tail], axis=1))
    total = [jnp.zeros((8, 512), F32)] * 3
    for offset, weight in ((1, h_ext), (2, b_ext)):
        shifted = [pltpu.roll(w, 512 - offset, 1) for w in wide]
        rest = (float(offset), 0.0, 0.0)
        pulls = springs(wide, shifted, weight, rest, float(offset))
        crossing = ((lane >= 128 - offset) & (lane < 128)) | (
            (lane >= 384 - offset) & (lane < 384)
        )
        across = jnp.where(crossing, weight, 0.0)
        for k in range(3):
            here = across * shifted[k] - pulls[k]
            there = across * wide[k] + pulls[k]
            total[k] = total[k] + here + pltpu.roll(there, offset, 1)
    lower = [
        jnp.where(row == 7, below_rows[k], pltpu.roll(comps[k], 7, 0)) for k in range(3)
    ]
    down = springs(comps, lower, vertical, (0.0, 1.0, 0.0), 1.0)
    upper = springs(
        above_rows, [c[0:1] for c in comps], above_weight, (0.0, 1.0, 0.0), 1.0
    )
    below_weight = jnp.where(lax.rem(row, 2) == 1, vertical, 0.0)
    rhs = []
    for k in range(3):
        received = jnp.where(row == 0, upper[k], pltpu.roll(down[k], 1, 0))
        rhs.append(
            inertial[k] + total[k][:, 128:384] + received - down[k] + below_weight * lower[k]
        )
    first = jnp.concatenate(rhs + [jnp.zeros((8, CB), F32)], axis=0)
    second = jnp.concatenate(
        [pltpu.roll(r, 7, 0) for r in rhs] + [jnp.zeros((8, CB), F32)], axis=0
    )
    wide_rhs = stacked(jnp.concatenate([first, second], axis=1))
    base = [jnp.zeros((8, CB), F32)] * 3
    for k in range(4):
        solved = halves_sum(dot_t(wide_rhs, inv_ref[k]))
        for j in range(3):
            part = solved[8 * j : 8 * j + 8]
            base[j] = jnp.where(
                row == 2 * k,
                part[:, :CB],
                jnp.where(row == 2 * k + 1, pltpu.roll(part[:, CB:], 1, 0), base[j]),
            )
    for j in range(3):
        base_ref[j] = base[j]
    weights = stiff_ref[1]
    last = base
    for k in range(1, 4):
        carried = jnp.concatenate(
            [weights * last[j] for j in range(3)] + [jnp.zeros((8, CB), F32)], axis=0
        )
        moved = halves_sum(dot_t(stacked(carried), inv_ref[k, CB:, :CB]))
        last = [
            jnp.where(row == 2 * k + 1, base[j] + pltpu.roll(moved[8 * j : 8 * j + 8], 2, 0), last[j])
            for j in range(3)
        ]
    rows = [(weights * last[j])[7:8] for j in range(3)]
    return jnp.concatenate(rows + [jnp.zeros((5, CB), F32)], axis=0)


def write_offsets(offset, sends_ref, msg_ref):
    core = lax.axis_index("c")
    x = lax.axis_index("x")
    vec = stacked(offset)
    raw = offset[0:3]
    beside = jnp.where(core == 0, apply_map(vec, sends_ref[0], sends_ref[1])[0:3], raw)
    far = apply_map(vec, sends_ref[2], sends_ref[3])[0:3]
    for k in range(4):
        value = jnp.where(high_bit("x") == k // 2, beside, far)
        value = jnp.where(x == k, raw, value)
        msg_ref[2 * k] = value
        msg_ref[2 * k + 1] = value


def offsets_kernel(offset_ref, sends_ref, msg_ref):
    write_offsets(offset_ref[...], sends_ref, msg_ref)


def first_side_kernel(
    u_ref, target_ref, inertia_ref, stiff_ref, pin_ref, left_ref, right_ref, near_ref, cross_ref,
    inv_ref, after_ref, base_ref, offset_ref, inertial_ref, ext_ref, above_ref,
):
    core = lax.axis_index("c")
    y = lax.axis_index("y")
    strip = (lax.axis_index("zh") * 4 + lax.axis_index("zl")) * 8 + lax.axis_index("x") * 2 + core
    comps = [u_ref[k] for k in range(3)]
    row = lax.broadcasted_iota(jnp.int32, (8, CB), 0)
    column = lax.broadcasted_iota(jnp.int32, (8, CB), 1) + y * CB
    hit = column < 0
    for k in range(pin_ref.shape[0]):
        hit = hit | (column == pin_ref[k])
    pinned = hit & (row == 0) & (strip == 0)
    inertial = []
    for k in range(3):
        value = inertia_ref[...] * target_ref[k] + PIN * jnp.where(pinned, comps[k], 0.0)
        inertial.append(value)
        inertial_ref[k] = value
    lane = lax.broadcasted_iota(jnp.int32, (8, 512), 1)
    from_left = left_ref[...]
    extended = []
    for k, channel, offset in ((3, 0, 1), (4, 2, 2)):
        head = pltpu.roll(from_left, 126 - 2 * k, 1)
        weight = jnp.concatenate([head, stiff_ref[channel], jnp.zeros((8, 128), F32)], axis=1)
        low = jnp.where(y == 0, 128, 128 - offset)
        high = jnp.where(y == 3, 384 - offset, 384)
        weight = jnp.where((lane >= low) & (lane < high), weight, 0.0)
        extended.append(weight)
        ext_ref[k - 3] = weight
    near, cross = near_ref[0:4, :], cross_ref[...]
    above = jnp.where(core == 0, cross, near)
    below = jnp.where(core == 0, near, cross)
    above_weight = jnp.where(strip == 0, 0.0, above[3:4])
    above_ref[...] = jnp.broadcast_to(above_weight, (8, CB))
    vertical = jnp.where((row == 7) & (strip == 127), 0.0, stiff_ref[1])
    offset_ref[...] = solve_right_side(
        comps, inertial, from_left, right_ref[...], [below[k : k + 1] for k in range(3)],
        [above[k : k + 1] for k in range(3)], above_weight, extended[0], extended[1], vertical,
        stiff_ref, inv_ref, base_ref,
    )


def second_side_kernel(
    u_ref, stiff_ref, left_ref, right_ref, row_ref, inv_ref, sends_ref, inertial_ref, ext_ref,
    above_ref, base_ref, msg_ref,
):
    core = lax.axis_index("c")
    y = lax.axis_index("y")
    strip = (lax.axis_index("zh") * 4 + lax.axis_index("zl")) * 8 + lax.axis_index("x") * 2 + core
    comps = [u_ref[k] for k in range(3)]
    row = lax.broadcasted_iota(jnp.int32, (8, CB), 0)
    above_weight = above_ref[0:1, :]
    divisor = jnp.where(strip == 0, 1.0, above_weight)
    above_rows = [u_ref[3, k : k + 1, :] / divisor for k in range(3)]
    vertical = jnp.where((row == 7) & (strip == 127), 0.0, stiff_ref[1])
    offset = solve_right_side(
        comps, [inertial_ref[k] for k in range(3)], left_ref[...], right_ref[...],
        [row_ref[k : k + 1, :] for k in range(3)], above_rows, above_weight, ext_ref[0], ext_ref[1],
        vertical, stiff_ref, inv_ref, base_ref,
    )
    write_offsets(offset, sends_ref, msg_ref)


def plane_vectors(got_ref, wh_ref, wl_ref, vec_ref):
    x = lax.axis_index("x")
    sib = x + 1 - 2 * low_bit("x")
    far = 4 - 4 * high_bit("x")
    vec_ref[...] = jnp.zeros(vec_ref.shape, F32)
    put_vector(vec_ref, 0, got_ref[2 * x])
    put_vector(vec_ref, 1, got_ref[2 * x + 1])
    put_vector(vec_ref, 2, got_ref[2 * sib] + got_ref[2 * sib + 1])
    others = (got_ref[far] + got_ref[far + 1]) + (got_ref[far + 2] + got_ref[far + 3])
    put_vector(vec_ref, 3, others)
    return apply_map(vec_ref[...].astype(BF16), wh_ref[...], wl_ref[...])


def send_vectors(total, maps_ref, joint_ref, msg_ref):
    zh = lax.axis_index("zh")
    vec = stacked(total)
    pairs = apply_map(vec, maps_ref[0], maps_ref[1])[0:3]
    near = apply_map(vec, maps_ref[2], maps_ref[3])[0:3]
    far = apply_map(vec, joint_ref[0], joint_ref[1])[0:3]
    far = jnp.where(zh == 0, far, near)
    raw = total[0:3]
    for g in range(4):
        for h in range(2):
            inner = jnp.where(high_bit() == h, raw, pairs)
            value = jnp.where(zh == g, inner, near if g < 2 else far)
            msg_ref[4 * g + 2 * h] = value
            msg_ref[4 * g + 2 * h + 1] = value


def plane_kernel(got_ref, wh_ref, wl_ref, both_ref, vec_ref):
    both_ref[...] = plane_vectors(got_ref, wh_ref, wl_ref, vec_ref)


def plane_send_kernel(got_ref, wh_ref, wl_ref, maps_ref, joint_ref, both_ref, msg_ref, vec_ref):
    both = plane_vectors(got_ref, wh_ref, wl_ref, vec_ref)
    both_ref[...] = both
    send_vectors(both[:, :CB], maps_ref, joint_ref, msg_ref)


def finish(
    got_ref, both_ref, maps_ref, joint_ref, eh_ref, el_ref, stiff_ref, base_ref, inv_ref, vec_ref
):
    zh = lax.axis_index("zh")
    row = lax.broadcasted_iota(jnp.int32, (8, CB), 0)
    none = jnp.zeros((3, CB), F32)
    vec_ref[...] = jnp.zeros(vec_ref.shape, F32)
    first_two = got_ref[4 * zh] + got_ref[4 * zh + 1]
    put_vector(vec_ref, 0, jnp.where(high_bit() == 1, first_two, none))
    sums = [
        (got_ref[4 * g] + got_ref[4 * g + 1]) + (got_ref[4 * g + 2] + got_ref[4 * g + 3])
        for g in range(3)
    ]
    lower = jnp.where(zh >= 1, sums[0], none) + jnp.where(zh >= 2, sums[1], none)
    put_vector(vec_ref, 1, jnp.where(zh == 3, sums[2], lower))
    put_vector(vec_ref, 2, jnp.where(zh == 3, lower, none))
    vec = vec_ref[...].astype(BF16)
    arrived = apply_map(vec[:, :CB], maps_ref[4], maps_ref[5])
    arrived = arrived + apply_map(vec[:, CB : 2 * CB], maps_ref[6], maps_ref[7])
    arrived = arrived + apply_map(vec[:, 2 * CB :], joint_ref[0], joint_ref[1])
    beside = jnp.where(low_bit() == 1, got_ref[4 * zh + 2 * high_bit()], none)
    arrived = arrived + jnp.concatenate([beside, jnp.zeros((5, CB), F32)], axis=0)
    came = both_ref[:, CB:] + apply_map(stacked(arrived), eh_ref[...], el_ref[...])
    weights = stiff_ref[1]
    state = [base_ref[k] for k in range(3)]
    blank = jnp.zeros((8, CB), F32)
    for k in range(4):
        if k == 0:
            source = [jnp.broadcast_to(came[j : j + 1], (8, CB)) for j in range(3)]
        else:
            source = [weights * state[j] for j in range(3)]
        moved = halves_sum(dot_t(stacked(jnp.concatenate(source + [blank], axis=0)), inv_ref[k, :, :CB]))
        for j in range(3):
            part = moved[8 * j : 8 * j + 8]
            state[j] = state[j] + jnp.where(
                row == 2 * k,
                pltpu.roll(part[:, :CB], 1, 0),
                jnp.where(row == 2 * k + 1, pltpu.roll(part[:, CB:], 2, 0), 0.0),
            )
    return state, came


def middle_kernel(
    got_ref, both_ref, maps_ref, joint_ref, eh_ref, el_ref, stiff_ref, base_ref, inv_ref,
    u_ref, left_ref, right_ref, row_ref, vec_ref,
):
    state, came = finish(
        got_ref, both_ref, maps_ref, joint_ref, eh_ref, el_ref, stiff_ref, base_ref, inv_ref, vec_ref
    )
    for k in range(3):
        u_ref[k] = state[k]
    u_ref[3] = came
    left, right = edge_tiles(state, [])
    left_ref[...] = left
    right_ref[...] = right
    row_ref[...] = jnp.concatenate([state[0][0:1], state[1][0:1], state[2][0:1], state[0][0:1]], axis=0)


def final_kernel(
    got_ref, both_ref, maps_ref, joint_ref, eh_ref, el_ref, stiff_ref, base_ref, inv_ref,
    u_ref, vec_ref,
):
    state, came = finish(
        got_ref, both_ref, maps_ref, joint_ref, eh_ref, el_ref, stiff_ref, base_ref, inv_ref, vec_ref
    )
    for k in range(3):
        u_ref[k] = state[k]


def swap(value, axes):
    return lax.all_to_all(value, axes, 0, 0)


def shards(positions, target, inertia, stiffness, pin_columns, inverses):
    smem = pl.BlockSpec(memory_space=pltpu.SMEM)
    anywhere = pl.BlockSpec(memory_space=pl.ANY)

    hbm = pl.BlockSpec(memory_space=pltpu.HBM)
    own_map = call(
        local_map_kernel,
        sds((CB + 8, CB)),
        (inverses, stiffness, positions),
        specs=[hbm] * 3,
        scratch=[
            pltpu.VMEM((4, CB, CB), BF16),
            pltpu.VMEM((3, 8, CB), F32),
            pltpu.VMEM((3, 8, CB), F32),
            pltpu.SemaphoreType.DMA((6,)),
        ],
        flops=10**8,
        limit=WHOLE_VMEM,
    )
    core_maps = lax.all_gather(own_map, "c")
    square = sds((CB, CB))
    chip, near = call(chip_map_kernel, [square, sds((8, CB))], (core_maps,))
    sib_chip = lax.ppermute(chip, "x", [(k, k ^ 1) for k in range(4)])

    tile = sds((8, 128))
    rows = sds((4, CB))
    left, right, cross = call(
        halo_kernel, [tile, tile, rows], (positions, stiffness, chip), specs=[None, None, anywhere]
    )
    to_left = [(1, 0), (2, 1), (3, 2)]
    to_right = [(0, 1), (1, 2), (2, 3)]
    cores = [(0, 1), (1, 0)]
    from_right = lax.ppermute(left, "y", to_left)
    two_chips, cross = call(
        two_chips_kernel,
        [square, rows],
        (chip, sib_chip, cross, from_right),
        specs=[None] * 3 + [anywhere],
    )
    far_chips = lax.ppermute(two_chips, "x", [(k, 3 - k) for k in range(4)])
    pairs = [(2 * k + 1, 2 * k + 2) for k in range(63)]
    cross = lax.ppermute(cross, STRIP, pairs + [(b, a) for a, b in pairs])
    plane, right = call(
        four_chips_kernel,
        [square, tile],
        (two_chips, far_chips, right, cross),
        specs=[None] * 3 + [anywhere],
    )
    beside = lax.ppermute(plane, ZAX, [(k, k ^ 1) for k in range(16)])

    from_left = lax.ppermute(right, "y", to_right)
    half = sds((CB, 128))
    two, two_half = call(
        two_planes_kernel, [square, half], (plane, beside, from_left), specs=[None, None, anywhere]
    )
    two_mine = lax.ppermute(two_half, ZAX, [(k, k ^ 2) for k in range(16)])

    halos = (from_left, from_right, near, cross)
    field = sds((3, 8, CB))
    vector = sds((8, CB))
    base, offset, inertial, ext, above = call(
        first_side_kernel,
        [field, vector, field, sds((2, 8, 512)), vector],
        (positions, target, inertia, stiffness, pin_columns) + halos + (inverses, two),
        specs=[None] * 4 + [smem] + [None] * 5 + [anywhere],
        flops=10**8,
        size=3 * 10**6,
    )
    group_half = call(
        four_planes_kernel, half, (two, two_mine, base), specs=[None, None, anywhere]
    )
    steps = [(4 + k, k) for k in range(4)] + [(8 + k, 12 + k) for k in range(4)]
    far_mine = lax.ppermute(group_half, ZAX, steps)

    wide = sds((4 * CB, 2 * CB), BF16)
    narrow = sds((CB, CB), BF16)
    xh, xl, eh, el, sends = call(
        plane_maps_kernel,
        [wide, wide, narrow, narrow, sds((4, CB, CB), BF16)],
        (chip, sib_chip, two_chips, far_chips, core_maps, group_half),
        specs=[None] * 5 + [anywhere],
        flops=10**9,
    )
    msg = call(offsets_kernel, sds((8, 3, CB)), (offset, sends))
    got = swap(msg, PLANE)
    both = call(
        plane_kernel,
        sds((8, 2 * CB)),
        (got, xh, xl),
        scratch=[pltpu.VMEM((16, 4 * CB), F32)],
        size=3 * 10**6,
    )
    mine = call(
        bundle_kernel, sds((2, CB, 128)), (two_mine, far_mine, both), specs=[None, None, anywhere]
    )
    other = lax.ppermute(mine, "c", cores)
    maps, joint, msg = call(
        group_maps_kernel,
        [sds((8, CB, CB), BF16), sds((2, CB, CB), BF16), sds((16, 3, CB))],
        (both, beside, mine, other),
        flops=5 * 10**8,
    )
    got = swap(msg, ZAX)
    middle, left, right, low_row = call(
        middle_kernel,
        [sds((4, 8, CB)), tile, tile, rows],
        (got, both, maps, joint, eh, el, stiffness, base, inverses),
        scratch=[pltpu.VMEM((16, 3 * CB), F32)],
        flops=10**8,
    )

    low_row = lax.ppermute(low_row, STRIP, [(k + 1, k) for k in range(127)])
    from_right = lax.ppermute(left, "y", to_left)
    from_left = lax.ppermute(right, "y", to_right)
    base, msg = call(
        second_side_kernel,
        [field, sds((8, 3, CB))],
        (middle, stiffness, from_left, from_right, low_row, inverses, sends)
        + (inertial, ext, above),
        flops=10**8,
        size=3 * 10**6,
    )
    got = swap(msg, PLANE)
    both, msg = call(
        plane_send_kernel,
        [sds((8, 2 * CB)), sds((16, 3, CB))],
        (got, xh, xl, maps, joint),
        scratch=[pltpu.VMEM((16, 4 * CB), F32)],
        size=3 * 10**6,
    )
    got = swap(msg, ZAX)
    return call(
        final_kernel,
        field,
        (got, both, maps, joint, eh, el, stiffness, base, inverses),
        scratch=[pltpu.VMEM((16, 3 * CB), F32)],
        flops=10**8,
    )


def solution(mesh):
    split = Mesh(mesh.devices.reshape(4, 4, 4, 2, 4), ("zh", "zl", "x", "c", "y"))
    return jax.shard_map(
        shards,
        mesh=split,
        in_specs=(
            P(None, STRIP, "y"),
            P(None, STRIP, "y"),
            P(STRIP, "y"),
            P(None, STRIP, "y"),
            P(),
            P(STRIP, None, None),
        ),
        out_specs=P(None, STRIP, "y"),
        check_vma=False,
    )
```

```python
import jax
import jax.numpy as jnp
from jax import lax
from jax.experimental import pallas as pl
from jax.experimental.pallas import tpu as pltpu
from jax.sharding import Mesh
from jax.sharding import PartitionSpec as P

F32 = jnp.float32
BF16 = jnp.bfloat16
STRIP = ("zh", "zl", "x", "c")
ZAX = ("zh", "zl")
PLANE = ("x", "c")
CB = 256
PIN = 20.0
VMEM_LIMIT = 14 * 1024 * 1024
WHOLE_VMEM = 64 * 1024 * 1024 - (64 + 280) * 1024


def dot(a, b):
    return lax.dot_general(a, b, (((1,), (0,)), ((), ())), preferred_element_type=F32)


def dot_t(a, b):
    return lax.dot_general(a, b, (((1,), (1,)), ((), ())), preferred_element_type=F32)


def pair(value):
    high = value.astype(BF16)
    low = (value - high.astype(F32)).astype(BF16)
    return high, low


def mm(a, b):
    return dot(a[0], b[0]) + (dot(a[0], b[1]) + dot(a[1], b[0]))


def eye():
    rows = lax.broadcasted_iota(jnp.int32, (CB, CB), 0)
    cols = lax.broadcasted_iota(jnp.int32, (CB, CB), 1)
    return jnp.where(rows == cols, 1.0, 0.0).astype(F32)


def stacked(value):
    high = value.astype(BF16)
    low = value - high.astype(F32)
    return jnp.concatenate([high.astype(F32), low], axis=0).astype(BF16)


def halves_sum(value):
    half = value.shape[0] // 2
    return value[:half] + value[half:]


def put_vector(vec_ref, slot, value):
    high = value.astype(BF16).astype(F32)
    vec_ref[0:3, slot * CB : (slot + 1) * CB] = high
    vec_ref[8:11, slot * CB : (slot + 1) * CB] = value - high


def apply_map(vec, high, low):
    return halves_sum(dot(vec, high) + dot(vec, low))


def call(kernel, outs, args, specs=None, scratch=(), flops=10**7, size=10**6, limit=VMEM_LIMIT):
    vmem = pl.BlockSpec(memory_space=pltpu.VMEM)
    in_specs = [vmem] * len(args) if specs is None else [vmem if s is None else s for s in specs]
    many = isinstance(outs, (list, tuple))
    out_specs = [vmem] * len(outs) if many else vmem
    return pl.pallas_call(
        kernel,
        out_shape=outs,
        in_specs=in_specs,
        out_specs=out_specs,
        scratch_shapes=list(scratch),
        compiler_params=pltpu.CompilerParams(vmem_limit_bytes=limit),
        cost_estimate=pl.CostEstimate(flops=flops, bytes_accessed=size, transcendentals=0),
    )(*args)


def sds(shape, dtype=F32):
    return jax.ShapeDtypeStruct(shape, dtype)


def local_map_kernel(inv_hbm, stiff_hbm, u_hbm, out_ref, inv_ref, stiff_ref, u_ref, sems):
    copies = [
        pltpu.make_async_copy(stiff_hbm, stiff_ref, sems.at[4]),
        pltpu.make_async_copy(u_hbm, u_ref, sems.at[5]),
    ]
    copies += [
        pltpu.make_async_copy(inv_hbm.at[k, CB : 2 * CB, 0:CB], inv_ref.at[k], sems.at[k])
        for k in range(4)
    ]
    for copy in copies:
        copy.start()
    core = lax.axis_index("c")
    copies[0].wait()
    copies[2].wait()
    first = dot_t(eye().astype(BF16), inv_ref[0]) * stiff_ref[1, 1:2, :]
    for k in range(1, 4):
        copies[2 + k].wait()
        high, low = pair(first)
        first = (dot_t(high, inv_ref[k]) + dot_t(low, inv_ref[k])) * stiff_ref[
            1, 2 * k + 1 : 2 * k + 2, :
        ]
    out_ref[0:CB, :] = first
    copies[1].wait()
    rows = [u_ref[k] for k in range(3)] + [stiff_ref[1]]
    rows = [jnp.where(core == 0, r[7:8], r[0:1]) for r in rows]
    out_ref[CB : CB + 8, :] = jnp.concatenate(rows + rows, axis=0)


def chip_map_kernel(both_ref, out_ref, near_ref):
    core = lax.axis_index("c")
    start = pl.multiple_of(core * 128, 128)
    half = mm(pair(both_ref[0, pl.ds(start, 128), :]), pair(both_ref[1, 0:CB, :]))
    for k in range(4):
        out_ref[k] = half
    tails = [both_ref[k, CB : CB + 8, :] for k in range(2)]
    near_ref[...] = jnp.where(core == 0, tails[1], tails[0])


def low_bit(axis="zl"):
    return lax.rem(lax.axis_index(axis), 2)


def high_bit(axis="zl"):
    return lax.div(lax.axis_index(axis), 2)


def in_order(own, other, right):
    return jnp.where(right, other, own), jnp.where(right, own, other)


def chips_kernel(
    mine_ref, other_ref, edge_ref, own_ref, sib_ref, two_ref, far_ref, plane_ref, tile_ref
):
    core, x = lax.axis_index("c"), lax.axis_index("x")
    tile_ref[...] = edge_ref[...]
    chips = []
    for k in range(4):
        top, bottom = in_order(mine_ref[k], other_ref[k], core == 1)
        chips.append(jnp.concatenate([top, bottom], axis=0))
    left = mm(pair(chips[0]), pair(chips[1]))
    right = mm(pair(chips[2]), pair(chips[3]))
    plane_ref[...] = mm(pair(left), pair(right))
    even, odd = in_order(chips[0], chips[2], high_bit("x") == 1)[0], in_order(
        chips[1], chips[3], high_bit("x") == 1
    )[0]
    own_ref[...], sib_ref[...] = in_order(even, odd, low_bit("x") == 1)
    two_ref[...], far_ref[...] = in_order(left, right, high_bit("x") == 1)


def rows_of_half(half):
    return jnp.concatenate([half[:128], half[128:]], axis=1)


def half_of_rows(rows):
    return jnp.concatenate([rows[:, :128], rows[:, 128:]], axis=0)


def joined(mine_ref, other_ref):
    core = lax.axis_index("c")
    first, second = in_order(mine_ref[...], other_ref[...], core == 1)
    columns = jnp.concatenate([first, second], axis=1)
    rows = jnp.concatenate([rows_of_half(first), rows_of_half(second)], axis=0)
    return jnp.where(high_bit() == 0, columns, rows)


def two_planes_kernel(own_ref, other_ref, cross_ref, after_ref, out_ref, half_ref, row_ref):
    row_ref[...] = cross_ref[...]
    core = lax.axis_index("c")
    left_map, right_map = in_order(own_ref[...], other_ref[...], low_bit() == 1)
    product = mm(pair(left_map), pair(right_map))
    out_ref[...] = product
    columns = jnp.where(core == 0, product[:, :128], product[:, 128:])
    rows = half_of_rows(jnp.where(core == 0, product[:128], product[128:]))
    half_ref[...] = jnp.where(high_bit() == 0, rows, columns)


def four_planes_kernel(own_ref, half_ref, after_ref, out_ref):
    own = pair(own_ref[...])
    half = half_ref[...]
    columns = mm(own, pair(half))
    rows = half_of_rows(mm(pair(rows_of_half(half)), own))
    out_ref[...] = jnp.where(high_bit() == 0, columns, rows)


def plane_maps_kernel(
    own_ref, sib_ref, two_ref, far_ref, cores_ref, after_ref, wh_ref, wl_ref, eh_ref, el_ref, sends_ref
):
    core = lax.axis_index("c")
    one = eye()
    low, high = low_bit("x"), high_bit("x")
    own, sib, two, far = own_ref[...], sib_ref[...], two_ref[...], far_ref[...]
    first, second = cores_ref[0, 0:CB, :], cores_ref[1, 0:CB, :]

    def store(slot, col, value):
        parts = pair(value)
        wh_ref[slot * CB : (slot + 1) * CB, col * CB : (col + 1) * CB] = parts[0]
        wl_ref[slot * CB : (slot + 1) * CB, col * CB : (col + 1) * CB] = parts[1]

    sib_after = jnp.where(low == 0, sib, one)
    rest = pair(jnp.where(high == 0, far, one))
    to_end = mm(pair(sib_after), rest)
    store(0, 0, mm(pair(second), pair(to_end)))
    store(1, 0, to_end)
    store(2, 0, mm(pair(jnp.where(low == 0, one, own)), rest))
    store(3, 0, jnp.where(high == 1, two, one))
    none = jnp.zeros((CB, CB), F32)
    core_before = jnp.where(core == 1, first, one)
    chip_before = mm(pair(jnp.where(low == 1, sib, one)), pair(core_before))
    store(0, 1, jnp.where(core == 1, one, none))
    store(1, 1, none)
    store(2, 1, jnp.where(low == 1, core_before, none))
    store(3, 1, jnp.where(high == 1, chip_before, none))
    parts = pair(mm(pair(jnp.where(high == 1, far, one)), pair(chip_before)))
    eh_ref[...] = parts[0]
    el_ref[...] = parts[1]
    core_after = jnp.where(core == 0, second, one)
    parts = pair(core_after)
    sends_ref[0] = parts[0]
    sends_ref[1] = parts[1]
    parts = pair(mm(parts, pair(sib_after)))
    sends_ref[2] = parts[0]
    sends_ref[3] = parts[1]


def bundle_kernel(two_ref, far_ref, after_ref, out_ref):
    out_ref[0] = two_ref[...]
    out_ref[1] = far_ref[...]


def group_maps_kernel(both_ref, one_ref, mine_ref, other_ref, out_ref, joint_ref, msg_ref):
    zh = lax.axis_index("zh")
    one = eye()
    sibling = one_ref[...]
    two = pair(joined(mine_ref.at[0], other_ref.at[0]))
    far = joined(mine_ref.at[1], other_ref.at[1])
    send = jnp.where(low_bit() == 0, sibling, one)
    take = jnp.where(low_bit() == 1, sibling, one)
    for k, value in ((0, send), (4, take)):
        parts = pair(value)
        out_ref[k] = parts[0]
        out_ref[k + 1] = parts[1]
    send = jnp.where(high_bit() == 0, mm(pair(send), two), send)
    take = jnp.where(high_bit() == 1, mm(two, pair(take)), take)
    for k, value in ((2, send), (6, take)):
        parts = pair(value)
        out_ref[k] = parts[0]
        out_ref[k + 1] = parts[1]
    left = jnp.where(zh == 0, send, far)
    right = jnp.where(zh == 0, far, take)
    joint = pair(mm(pair(left), pair(right)))
    joint_ref[0] = joint[0]
    joint_ref[1] = joint[1]
    send_vectors(both_ref[:, :CB], out_ref, joint_ref, msg_ref)


def edge_tiles(comps, weights):
    lane = lax.broadcasted_iota(jnp.int32, (8, 128), 1)
    right = jnp.zeros((8, 128), F32)
    left = jnp.zeros((8, 128), F32)
    for k, value in enumerate(comps + weights):
        mask = (lane == 2 * k) | (lane == 2 * k + 1)
        right = jnp.where(mask, pltpu.roll(value[:, 128:], (2 * k - 126) % 128, 1), right)
        if k < 3:
            left = jnp.where(mask, pltpu.roll(value[:, :128], 2 * k, 1), left)
    return left, right


def halo_kernel(u_ref, stiff_ref, after_ref, left_ref, right_ref, cross_ref):
    core = lax.axis_index("c")
    comps = [u_ref[k] for k in range(3)]
    left, right = edge_tiles(comps, [stiff_ref[0], stiff_ref[2]])
    left_ref[...] = left
    right_ref[...] = right
    for k, rows in enumerate(comps + [stiff_ref[1]]):
        cross_ref[k : k + 1, :] = jnp.where(core == 0, rows[0:1], rows[7:8])


def springs(ends, others, weight, rest, length):
    gaps = [o - e for o, e in zip(others, ends)]
    gaps = [g + r if r != 0.0 else g for g, r in zip(gaps, rest)]
    norm = jnp.sqrt(gaps[0] * gaps[0] + gaps[1] * gaps[1] + gaps[2] * gaps[2])
    factor = length / jnp.maximum(norm, 0.5 * length)
    return [weight * (g * factor - r if r != 0.0 else g * factor) for g, r in zip(gaps, rest)]


def solve_right_side(
    comps, inertial, from_left, from_right, below_rows, above_rows, above_weight, h_ext, b_ext,
    vertical, stiff_ref, inv_ref, base_ref,
):
    row = lax.broadcasted_iota(jnp.int32, (8, CB), 0)
    lane = lax.broadcasted_iota(jnp.int32, (8, 512), 1)
    wide = []
    for k in range(3):
        head = pltpu.roll(from_left, 126 - 2 * k, 1)
        tail = pltpu.roll(from_right, (-2 * k) % 128, 1) if k else from_right
        wide.append(jnp.concatenate([head, comps[k], tail], axis=1))
    total = [jnp.zeros((8, 512), F32)] * 3
    for offset, weight in ((1, h_ext), (2, b_ext)):
        shifted = [pltpu.roll(w, 512 - offset, 1) for w in wide]
        rest = (float(offset), 0.0, 0.0)
        pulls = springs(wide, shifted, weight, rest, float(offset))
        crossing = ((lane >= 128 - offset) & (lane < 128)) | (
            (lane >= 384 - offset) & (lane < 384)
        )
        across = jnp.where(crossing, weight, 0.0)
        for k in range(3):
            here = across * shifted[k] - pulls[k]
            there = across * wide[k] + pulls[k]
            total[k] = total[k] + here + pltpu.roll(there, offset, 1)
    lower = [
        jnp.where(row == 7, below_rows[k], pltpu.roll(comps[k], 7, 0)) for k in range(3)
    ]
    down = springs(comps, lower, vertical, (0.0, 1.0, 0.0), 1.0)
    upper = springs(
        above_rows, [c[0:1] for c in comps], above_weight, (0.0, 1.0, 0.0), 1.0
    )
    below_weight = jnp.where(lax.rem(row, 2) == 1, vertical, 0.0)
    rhs = []
    for k in range(3):
        received = jnp.where(row == 0, upper[k], pltpu.roll(down[k], 1, 0))
        rhs.append(
            inertial[k] + total[k][:, 128:384] + received - down[k] + below_weight * lower[k]
        )
    first = jnp.concatenate(rhs + [jnp.zeros((8, CB), F32)], axis=0)
    second = jnp.concatenate(
        [pltpu.roll(r, 7, 0) for r in rhs] + [jnp.zeros((8, CB), F32)], axis=0
    )
    wide_rhs = stacked(jnp.concatenate([first, second], axis=1))
    base = [jnp.zeros((8, CB), F32)] * 3
    for k in range(4):
        solved = halves_sum(dot_t(wide_rhs, inv_ref[k]))
        for j in range(3):
            part = solved[8 * j : 8 * j + 8]
            base[j] = jnp.where(
                row == 2 * k,
                part[:, :CB],
                jnp.where(row == 2 * k + 1, pltpu.roll(part[:, CB:], 1, 0), base[j]),
            )
    for j in range(3):
        base_ref[j] = base[j]
    weights = stiff_ref[1]
    last = base
    for k in range(1, 4):
        carried = jnp.concatenate(
            [weights * last[j] for j in range(3)] + [jnp.zeros((8, CB), F32)], axis=0
        )
        moved = halves_sum(dot_t(stacked(carried), inv_ref[k, CB:, :CB]))
        last = [
            jnp.where(row == 2 * k + 1, base[j] + pltpu.roll(moved[8 * j : 8 * j + 8], 2, 0), last[j])
            for j in range(3)
        ]
    rows = [(weights * last[j])[7:8] for j in range(3)]
    return jnp.concatenate(rows + [jnp.zeros((5, CB), F32)], axis=0)


def write_offsets(offset, sends_ref, msg_ref):
    core = lax.axis_index("c")
    x = lax.axis_index("x")
    vec = stacked(offset)
    raw = offset[0:3]
    beside = jnp.where(core == 0, apply_map(vec, sends_ref[0], sends_ref[1])[0:3], raw)
    far = apply_map(vec, sends_ref[2], sends_ref[3])[0:3]
    for k in range(4):
        value = jnp.where(high_bit("x") == k // 2, beside, far)
        value = jnp.where(x == k, raw, value)
        msg_ref[2 * k] = value
        msg_ref[2 * k + 1] = value


def offsets_kernel(offset_ref, sends_ref, msg_ref):
    write_offsets(offset_ref[...], sends_ref, msg_ref)


def first_side_kernel(
    u_ref, target_ref, inertia_ref, stiff_ref, pin_ref, left_ref, right_ref, near_ref, cross_ref,
    inv_ref, after_ref, base_ref, offset_ref, inertial_ref, ext_ref, above_ref,
):
    core = lax.axis_index("c")
    y = lax.axis_index("y")
    strip = (lax.axis_index("zh") * 4 + lax.axis_index("zl")) * 8 + lax.axis_index("x") * 2 + core
    comps = [u_ref[k] for k in range(3)]
    row = lax.broadcasted_iota(jnp.int32, (8, CB), 0)
    column = lax.broadcasted_iota(jnp.int32, (8, CB), 1) + y * CB
    hit = column < 0
    for k in range(pin_ref.shape[0]):
        hit = hit | (column == pin_ref[k])
    pinned = hit & (row == 0) & (strip == 0)
    inertial = []
    for k in range(3):
        value = inertia_ref[...] * target_ref[k] + PIN * jnp.where(pinned, comps[k], 0.0)
        inertial.append(value)
        inertial_ref[k] = value
    lane = lax.broadcasted_iota(jnp.int32, (8, 512), 1)
    from_left = left_ref[...]
    extended = []
    for k, channel, offset in ((3, 0, 1), (4, 2, 2)):
        head = pltpu.roll(from_left, 126 - 2 * k, 1)
        weight = jnp.concatenate([head, stiff_ref[channel], jnp.zeros((8, 128), F32)], axis=1)
        low = jnp.where(y == 0, 128, 128 - offset)
        high = jnp.where(y == 3, 384 - offset, 384)
        weight = jnp.where((lane >= low) & (lane < high), weight, 0.0)
        extended.append(weight)
        ext_ref[k - 3] = weight
    near, cross = near_ref[0:4, :], cross_ref[...]
    above = jnp.where(core == 0, cross, near)
    below = jnp.where(core == 0, near, cross)
    above_weight = jnp.where(strip == 0, 0.0, above[3:4])
    above_ref[...] = jnp.broadcast_to(above_weight, (8, CB))
    vertical = jnp.where((row == 7) & (strip == 127), 0.0, stiff_ref[1])
    offset_ref[...] = solve_right_side(
        comps, inertial, from_left, right_ref[...], [below[k : k + 1] for k in range(3)],
        [above[k : k + 1] for k in range(3)], above_weight, extended[0], extended[1], vertical,
        stiff_ref, inv_ref, base_ref,
    )


def second_side_kernel(
    u_ref, stiff_ref, left_ref, right_ref, row_ref, inv_ref, sends_ref, inertial_ref, ext_ref,
    above_ref, base_ref, msg_ref,
):
    core = lax.axis_index("c")
    y = lax.axis_index("y")
    strip = (lax.axis_index("zh") * 4 + lax.axis_index("zl")) * 8 + lax.axis_index("x") * 2 + core
    comps = [u_ref[k] for k in range(3)]
    row = lax.broadcasted_iota(jnp.int32, (8, CB), 0)
    above_weight = above_ref[0:1, :]
    divisor = jnp.where(strip == 0, 1.0, above_weight)
    above_rows = [u_ref[3, k : k + 1, :] / divisor for k in range(3)]
    vertical = jnp.where((row == 7) & (strip == 127), 0.0, stiff_ref[1])
    offset = solve_right_side(
        comps, [inertial_ref[k] for k in range(3)], left_ref[...], right_ref[...],
        [row_ref[k : k + 1, :] for k in range(3)], above_rows, above_weight, ext_ref[0], ext_ref[1],
        vertical, stiff_ref, inv_ref, base_ref,
    )
    write_offsets(offset, sends_ref, msg_ref)


def plane_vectors(got_ref, wh_ref, wl_ref, vec_ref):
    x = lax.axis_index("x")
    sib = x + 1 - 2 * low_bit("x")
    far = 4 - 4 * high_bit("x")
    vec_ref[...] = jnp.zeros(vec_ref.shape, F32)
    put_vector(vec_ref, 0, got_ref[2 * x])
    put_vector(vec_ref, 1, got_ref[2 * x + 1])
    put_vector(vec_ref, 2, got_ref[2 * sib] + got_ref[2 * sib + 1])
    others = (got_ref[far] + got_ref[far + 1]) + (got_ref[far + 2] + got_ref[far + 3])
    put_vector(vec_ref, 3, others)
    return apply_map(vec_ref[...].astype(BF16), wh_ref[...], wl_ref[...])


def send_vectors(total, maps_ref, joint_ref, msg_ref):
    zh = lax.axis_index("zh")
    vec = stacked(total)
    pairs = apply_map(vec, maps_ref[0], maps_ref[1])[0:3]
    near = apply_map(vec, maps_ref[2], maps_ref[3])[0:3]
    far = apply_map(vec, joint_ref[0], joint_ref[1])[0:3]
    far = jnp.where(zh == 0, far, near)
    raw = total[0:3]
    for g in range(4):
        for h in range(2):
            inner = jnp.where(high_bit() == h, raw, pairs)
            value = jnp.where(zh == g, inner, near if g < 2 else far)
            msg_ref[4 * g + 2 * h] = value
            msg_ref[4 * g + 2 * h + 1] = value


def plane_kernel(got_ref, wh_ref, wl_ref, both_ref, vec_ref):
    both_ref[...] = plane_vectors(got_ref, wh_ref, wl_ref, vec_ref)


def plane_send_kernel(got_ref, wh_ref, wl_ref, maps_ref, joint_ref, both_ref, msg_ref, vec_ref):
    both = plane_vectors(got_ref, wh_ref, wl_ref, vec_ref)
    both_ref[...] = both
    send_vectors(both[:, :CB], maps_ref, joint_ref, msg_ref)


def finish(
    got_ref, both_ref, maps_ref, joint_ref, eh_ref, el_ref, stiff_ref, base_ref, inv_ref, vec_ref
):
    zh = lax.axis_index("zh")
    row = lax.broadcasted_iota(jnp.int32, (8, CB), 0)
    none = jnp.zeros((3, CB), F32)
    vec_ref[...] = jnp.zeros(vec_ref.shape, F32)
    first_two = got_ref[4 * zh] + got_ref[4 * zh + 1]
    put_vector(vec_ref, 0, jnp.where(high_bit() == 1, first_two, none))
    sums = [
        (got_ref[4 * g] + got_ref[4 * g + 1]) + (got_ref[4 * g + 2] + got_ref[4 * g + 3])
        for g in range(3)
    ]
    lower = jnp.where(zh >= 1, sums[0], none) + jnp.where(zh >= 2, sums[1], none)
    put_vector(vec_ref, 1, jnp.where(zh == 3, sums[2], lower))
    put_vector(vec_ref, 2, jnp.where(zh == 3, lower, none))
    vec = vec_ref[...].astype(BF16)
    arrived = apply_map(vec[:, :CB], maps_ref[4], maps_ref[5])
    arrived = arrived + apply_map(vec[:, CB : 2 * CB], maps_ref[6], maps_ref[7])
    arrived = arrived + apply_map(vec[:, 2 * CB :], joint_ref[0], joint_ref[1])
    beside = jnp.where(low_bit() == 1, got_ref[4 * zh + 2 * high_bit()], none)
    arrived = arrived + jnp.concatenate([beside, jnp.zeros((5, CB), F32)], axis=0)
    came = both_ref[:, CB:] + apply_map(stacked(arrived), eh_ref[...], el_ref[...])
    weights = stiff_ref[1]
    state = [base_ref[k] for k in range(3)]
    blank = jnp.zeros((8, CB), F32)
    for k in range(4):
        if k == 0:
            source = [jnp.broadcast_to(came[j : j + 1], (8, CB)) for j in range(3)]
        else:
            source = [weights * state[j] for j in range(3)]
        moved = halves_sum(dot_t(stacked(jnp.concatenate(source + [blank], axis=0)), inv_ref[k, :, :CB]))
        for j in range(3):
            part = moved[8 * j : 8 * j + 8]
            state[j] = state[j] + jnp.where(
                row == 2 * k,
                pltpu.roll(part[:, :CB], 1, 0),
                jnp.where(row == 2 * k + 1, pltpu.roll(part[:, CB:], 2, 0), 0.0),
            )
    return state, came


def middle_kernel(
    got_ref, both_ref, maps_ref, joint_ref, eh_ref, el_ref, stiff_ref, base_ref, inv_ref,
    u_ref, left_ref, right_ref, row_ref, vec_ref,
):
    state, came = finish(
        got_ref, both_ref, maps_ref, joint_ref, eh_ref, el_ref, stiff_ref, base_ref, inv_ref, vec_ref
    )
    for k in range(3):
        u_ref[k] = state[k]
    u_ref[3] = came
    left, right = edge_tiles(state, [])
    left_ref[...] = left
    right_ref[...] = right
    row_ref[...] = jnp.concatenate([state[0][0:1], state[1][0:1], state[2][0:1], state[0][0:1]], axis=0)


def final_kernel(
    got_ref, both_ref, maps_ref, joint_ref, eh_ref, el_ref, stiff_ref, base_ref, inv_ref,
    u_ref, vec_ref,
):
    state, came = finish(
        got_ref, both_ref, maps_ref, joint_ref, eh_ref, el_ref, stiff_ref, base_ref, inv_ref, vec_ref
    )
    for k in range(3):
        u_ref[k] = state[k]


def swap(value, axes):
    return lax.all_to_all(value, axes, 0, 0)


def shards(positions, target, inertia, stiffness, pin_columns, inverses):
    smem = pl.BlockSpec(memory_space=pltpu.SMEM)
    anywhere = pl.BlockSpec(memory_space=pl.ANY)

    hbm = pl.BlockSpec(memory_space=pltpu.HBM)
    own_map = call(
        local_map_kernel,
        sds((CB + 8, CB)),
        (inverses, stiffness, positions),
        specs=[hbm] * 3,
        scratch=[
            pltpu.VMEM((4, CB, CB), BF16),
            pltpu.VMEM((3, 8, CB), F32),
            pltpu.VMEM((3, 8, CB), F32),
            pltpu.SemaphoreType.DMA((6,)),
        ],
        flops=10**8,
        limit=WHOLE_VMEM,
    )
    core_maps = lax.all_gather(own_map, "c")
    square = sds((CB, CB))
    square = sds((CB, CB))
    chip_halves, near = call(
        chip_map_kernel, [sds((4, 128, CB)), sds((8, CB))], (core_maps,)
    )
    mine = swap(chip_halves, "x")

    tile = sds((8, 128))
    rows = sds((4, CB))
    left, right, cross = call(
        halo_kernel,
        [tile, tile, rows],
        (positions, stiffness, near),
        specs=[None, None, anywhere],
    )
    to_left = [(1, 0), (2, 1), (3, 2)]
    to_right = [(0, 1), (1, 2), (2, 3)]
    cores = [(0, 1), (1, 0)]
    from_right = lax.ppermute(left, "y", to_left)
    mine, from_right = lax.optimization_barrier((mine, from_right))
    other = lax.ppermute(mine, "c", cores)
    chip, sib_chip, two_chips, far_chips, plane, right = call(
        chips_kernel, [square] * 5 + [tile], (mine, other, right)
    )
    beside = lax.ppermute(plane, ZAX, [(k, k ^ 1) for k in range(16)])
    from_left = lax.ppermute(right, "y", to_right)
    half = sds((CB, 128))
    two, two_half, cross = call(
        two_planes_kernel,
        [square, half, rows],
        (plane, beside, cross, from_left),
        specs=[None] * 3 + [anywhere],
    )
    two_mine = lax.ppermute(two_half, ZAX, [(k, k ^ 2) for k in range(16)])
    pairs = [(2 * k + 1, 2 * k + 2) for k in range(63)]
    cross = lax.ppermute(cross, STRIP, pairs + [(b, a) for a, b in pairs])
    group_half = call(
        four_planes_kernel, half, (two, two_mine, cross), specs=[None, None, anywhere]
    )
    steps = [(4 + k, k) for k in range(4)] + [(8 + k, 12 + k) for k in range(4)]
    far_mine = lax.ppermute(group_half, ZAX, steps)

    halos = (from_left, from_right, near, cross)
    field = sds((3, 8, CB))
    vector = sds((8, CB))
    base, offset, inertial, ext, above = call(
        first_side_kernel,
        [field, vector, field, sds((2, 8, 512)), vector],
        (positions, target, inertia, stiffness, pin_columns) + halos + (inverses, group_half),
        specs=[None] * 4 + [smem] + [None] * 5 + [anywhere],
        flops=10**8,
        size=3 * 10**6,
    )
    wide = sds((4 * CB, 2 * CB), BF16)
    narrow = sds((CB, CB), BF16)
    xh, xl, eh, el, sends = call(
        plane_maps_kernel,
        [wide, wide, narrow, narrow, sds((4, CB, CB), BF16)],
        (chip, sib_chip, two_chips, far_chips, core_maps, group_half),
        specs=[None] * 5 + [anywhere],
        flops=10**9,
    )
    msg = call(offsets_kernel, sds((8, 3, CB)), (offset, sends))
    got = swap(msg, PLANE)
    both = call(
        plane_kernel,
        sds((8, 2 * CB)),
        (got, xh, xl),
        scratch=[pltpu.VMEM((16, 4 * CB), F32)],
        size=3 * 10**6,
    )
    mine = call(
        bundle_kernel, sds((2, CB, 128)), (two_mine, far_mine, both), specs=[None, None, anywhere]
    )
    other = lax.ppermute(mine, "c", cores)
    maps, joint, msg = call(
        group_maps_kernel,
        [sds((8, CB, CB), BF16), sds((2, CB, CB), BF16), sds((16, 3, CB))],
        (both, beside, mine, other),
        flops=5 * 10**8,
    )
    got = swap(msg, ZAX)
    middle, left, right, low_row = call(
        middle_kernel,
        [sds((4, 8, CB)), tile, tile, rows],
        (got, both, maps, joint, eh, el, stiffness, base, inverses),
        scratch=[pltpu.VMEM((16, 3 * CB), F32)],
        flops=10**8,
    )

    low_row = lax.ppermute(low_row, STRIP, [(k + 1, k) for k in range(127)])
    from_right = lax.ppermute(left, "y", to_left)
    from_left = lax.ppermute(right, "y", to_right)
    base, msg = call(
        second_side_kernel,
        [field, sds((8, 3, CB))],
        (middle, stiffness, from_left, from_right, low_row, inverses, sends)
        + (inertial, ext, above),
        flops=10**8,
        size=3 * 10**6,
    )
    got = swap(msg, PLANE)
    both, msg = call(
        plane_send_kernel,
        [sds((8, 2 * CB)), sds((16, 3, CB))],
        (got, xh, xl, maps, joint),
        scratch=[pltpu.VMEM((16, 4 * CB), F32)],
        size=3 * 10**6,
    )
    got = swap(msg, ZAX)
    return call(
        final_kernel,
        field,
        (got, both, maps, joint, eh, el, stiffness, base, inverses),
        scratch=[pltpu.VMEM((16, 3 * CB), F32)],
        flops=10**8,
    )


def solution(mesh):
    split = Mesh(mesh.devices.reshape(4, 4, 4, 2, 4), ("zh", "zl", "x", "c", "y"))
    return jax.shard_map(
        shards,
        mesh=split,
        in_specs=(
            P(None, STRIP, "y"),
            P(None, STRIP, "y"),
            P(STRIP, "y"),
            P(None, STRIP, "y"),
            P(),
            P(STRIP, None, None),
        ),
        out_specs=P(None, STRIP, "y"),
        check_vma=False,
    )
```

```python
import jax
import jax.numpy as jnp
from jax import lax
from jax.experimental import pallas as pl
from jax.experimental.pallas import tpu as pltpu
from jax.sharding import Mesh
from jax.sharding import PartitionSpec as P

F32 = jnp.float32
BF16 = jnp.bfloat16
STRIP = ("zh", "zl", "x", "c")
ZAX = ("zh", "zl")
PLANE = ("x", "c")
CB = 256
PIN = 20.0
VMEM_LIMIT = 14 * 1024 * 1024
WHOLE_VMEM = 64 * 1024 * 1024 - (64 + 280) * 1024


def dot(a, b):
    return lax.dot_general(a, b, (((1,), (0,)), ((), ())), preferred_element_type=F32)


def dot_t(a, b):
    return lax.dot_general(a, b, (((1,), (1,)), ((), ())), preferred_element_type=F32)


def pair(value):
    high = value.astype(BF16)
    low = (value - high.astype(F32)).astype(BF16)
    return high, low


def mm(a, b):
    return dot(a[0], b[0]) + (dot(a[0], b[1]) + dot(a[1], b[0]))


def eye():
    rows = lax.broadcasted_iota(jnp.int32, (CB, CB), 0)
    cols = lax.broadcasted_iota(jnp.int32, (CB, CB), 1)
    return jnp.where(rows == cols, 1.0, 0.0).astype(F32)


def stacked(value):
    high = value.astype(BF16)
    low = value - high.astype(F32)
    return jnp.concatenate([high.astype(F32), low], axis=0).astype(BF16)


def halves_sum(value):
    half = value.shape[0] // 2
    return value[:half] + value[half:]


def put_vector(vec_ref, slot, value):
    high = value.astype(BF16).astype(F32)
    vec_ref[0:3, slot * CB : (slot + 1) * CB] = high
    vec_ref[8:11, slot * CB : (slot + 1) * CB] = value - high


def apply_map(vec, high, low):
    return halves_sum(dot(vec, high) + dot(vec, low))


def call(kernel, outs, args, specs=None, scratch=(), flops=10**7, size=10**6, limit=VMEM_LIMIT):
    vmem = pl.BlockSpec(memory_space=pltpu.VMEM)
    in_specs = [vmem] * len(args) if specs is None else [vmem if s is None else s for s in specs]
    many = isinstance(outs, (list, tuple))
    out_specs = [vmem] * len(outs) if many else vmem
    return pl.pallas_call(
        kernel,
        out_shape=outs,
        in_specs=in_specs,
        out_specs=out_specs,
        scratch_shapes=list(scratch),
        compiler_params=pltpu.CompilerParams(vmem_limit_bytes=limit),
        cost_estimate=pl.CostEstimate(flops=flops, bytes_accessed=size, transcendentals=0),
    )(*args)


def sds(shape, dtype=F32):
    return jax.ShapeDtypeStruct(shape, dtype)


def local_map_kernel(inv_hbm, stiff_hbm, u_hbm, out_ref, inv_ref, stiff_ref, u_ref, sems):
    copies = [
        pltpu.make_async_copy(stiff_hbm, stiff_ref, sems.at[4]),
        pltpu.make_async_copy(u_hbm, u_ref, sems.at[5]),
    ]
    copies += [
        pltpu.make_async_copy(inv_hbm.at[k, CB : 2 * CB, 0:CB], inv_ref.at[k], sems.at[k])
        for k in range(4)
    ]
    for copy in copies:
        copy.start()
    core = lax.axis_index("c")
    copies[0].wait()
    copies[2].wait()
    first = dot_t(eye().astype(BF16), inv_ref[0]) * stiff_ref[1, 1:2, :]
    for k in range(1, 4):
        copies[2 + k].wait()
        high, low = pair(first)
        first = (dot_t(high, inv_ref[k]) + dot_t(low, inv_ref[k])) * stiff_ref[
            1, 2 * k + 1 : 2 * k + 2, :
        ]
    out_ref[0:CB, :] = first
    copies[1].wait()
    rows = [u_ref[k] for k in range(3)] + [stiff_ref[1]]
    rows = [jnp.where(core == 0, r[7:8], r[0:1]) for r in rows]
    out_ref[CB : CB + 8, :] = jnp.concatenate(rows + rows, axis=0)


def chip_map_kernel(both_ref, out_ref, near_ref):
    core = lax.axis_index("c")
    out_ref[...] = mm(pair(both_ref[0, 0:CB, :]), pair(both_ref[1, 0:CB, :]))
    tails = [both_ref[k, CB : CB + 8, :] for k in range(2)]
    near_ref[...] = jnp.where(core == 0, tails[1], tails[0])


def low_bit(axis="zl"):
    return lax.rem(lax.axis_index(axis), 2)


def high_bit(axis="zl"):
    return lax.div(lax.axis_index(axis), 2)


def in_order(own, other, right):
    return jnp.where(right, other, own), jnp.where(right, own, other)


def two_chips_kernel(own_ref, other_ref, cross_ref, after_ref, out_ref, row_ref):
    left_map, right_map = in_order(own_ref[...], other_ref[...], low_bit("x") == 1)
    out_ref[...] = mm(pair(left_map), pair(right_map))
    row_ref[...] = cross_ref[...]


def four_chips_kernel(own_ref, other_ref, edge_ref, after_ref, out_ref, tile_ref):
    tile_ref[...] = edge_ref[...]
    left_map, right_map = in_order(own_ref[...], other_ref[...], high_bit("x") == 1)
    out_ref[...] = mm(pair(left_map), pair(right_map))


def rows_of_half(half):
    return jnp.concatenate([half[:128], half[128:]], axis=1)


def half_of_rows(rows):
    return jnp.concatenate([rows[:, :128], rows[:, 128:]], axis=0)


def joined(first, second):
    columns = jnp.concatenate([first, second], axis=1)
    rows = jnp.concatenate([rows_of_half(first), rows_of_half(second)], axis=0)
    return jnp.where(high_bit() == 0, columns, rows)


def two_planes_kernel(own_ref, other_ref, *rest):
    out_ref, half_ref = rest[-2:]
    core = lax.axis_index("c")
    left_map, right_map = in_order(own_ref[...], other_ref[...], low_bit() == 1)
    product = mm(pair(left_map), pair(right_map))
    out_ref[...] = product
    columns = jnp.where(core == 0, product[:, :128], product[:, 128:])
    rows = half_of_rows(jnp.where(core == 0, product[:128], product[128:]))
    half_ref[...] = jnp.where(high_bit() == 0, rows, columns)


def four_planes_kernel(own_ref, half_ref, after_ref, out_ref):
    own = pair(own_ref[...])
    half = half_ref[...]
    columns = mm(own, pair(half))
    rows = half_of_rows(mm(pair(rows_of_half(half)), own))
    out_ref[...] = jnp.where(high_bit() == 0, columns, rows)


def plane_maps_kernel(
    own_ref, sib_ref, two_ref, far_ref, cores_ref, after_ref, wh_ref, wl_ref, eh_ref, el_ref, sends_ref
):
    core = lax.axis_index("c")
    one = eye()
    low, high = low_bit("x"), high_bit("x")
    own, sib, two, far = own_ref[...], sib_ref[...], two_ref[...], far_ref[...]
    first, second = cores_ref[0, 0:CB, :], cores_ref[1, 0:CB, :]

    def store(slot, col, value):
        parts = pair(value)
        wh_ref[slot * CB : (slot + 1) * CB, col * CB : (col + 1) * CB] = parts[0]
        wl_ref[slot * CB : (slot + 1) * CB, col * CB : (col + 1) * CB] = parts[1]

    sib_after = jnp.where(low == 0, sib, one)
    rest = pair(jnp.where(high == 0, far, one))
    to_end = mm(pair(sib_after), rest)
    store(0, 0, mm(pair(second), pair(to_end)))
    store(1, 0, to_end)
    store(2, 0, mm(pair(jnp.where(low == 0, one, own)), rest))
    store(3, 0, jnp.where(high == 1, two, one))
    none = jnp.zeros((CB, CB), F32)
    core_before = jnp.where(core == 1, first, one)
    chip_before = mm(pair(jnp.where(low == 1, sib, one)), pair(core_before))
    store(0, 1, jnp.where(core == 1, one, none))
    store(1, 1, none)
    store(2, 1, jnp.where(low == 1, core_before, none))
    store(3, 1, jnp.where(high == 1, chip_before, none))
    parts = pair(mm(pair(jnp.where(high == 1, far, one)), pair(chip_before)))
    eh_ref[...] = parts[0]
    el_ref[...] = parts[1]
    core_after = jnp.where(core == 0, second, one)
    parts = pair(core_after)
    sends_ref[0] = parts[0]
    sends_ref[1] = parts[1]
    parts = pair(mm(parts, pair(sib_after)))
    sends_ref[2] = parts[0]
    sends_ref[3] = parts[1]


def bundle_kernel(two_ref, far_ref, after_ref, out_ref):
    out_ref[0] = two_ref[...]
    out_ref[1] = far_ref[...]


def group_maps_kernel(both_ref, one_ref, halves_ref, out_ref, joint_ref, msg_ref):
    zh = lax.axis_index("zh")
    one = eye()
    sibling = one_ref[...]
    two = pair(joined(halves_ref[0, 0], halves_ref[1, 0]))
    far = joined(halves_ref[0, 1], halves_ref[1, 1])
    send = jnp.where(low_bit() == 0, sibling, one)
    take = jnp.where(low_bit() == 1, sibling, one)
    for k, value in ((0, send), (4, take)):
        parts = pair(value)
        out_ref[k] = parts[0]
        out_ref[k + 1] = parts[1]
    send = jnp.where(high_bit() == 0, mm(pair(send), two), send)
    take = jnp.where(high_bit() == 1, mm(two, pair(take)), take)
    for k, value in ((2, send), (6, take)):
        parts = pair(value)
        out_ref[k] = parts[0]
        out_ref[k + 1] = parts[1]
    left = jnp.where(zh == 0, send, far)
    right = jnp.where(zh == 0, far, take)
    joint = pair(mm(pair(left), pair(right)))
    joint_ref[0] = joint[0]
    joint_ref[1] = joint[1]
    send_vectors(both_ref[:, :CB], out_ref, joint_ref, msg_ref)


def edge_tiles(comps, weights):
    lane = lax.broadcasted_iota(jnp.int32, (8, 128), 1)
    right = jnp.zeros((8, 128), F32)
    left = jnp.zeros((8, 128), F32)
    for k, value in enumerate(comps + weights):
        mask = (lane == 2 * k) | (lane == 2 * k + 1)
        right = jnp.where(mask, pltpu.roll(value[:, 128:], (2 * k - 126) % 128, 1), right)
        if k < 3:
            left = jnp.where(mask, pltpu.roll(value[:, :128], 2 * k, 1), left)
    return left, right


def halo_kernel(u_ref, stiff_ref, after_ref, left_ref, right_ref, cross_ref):
    core = lax.axis_index("c")
    comps = [u_ref[k] for k in range(3)]
    left, right = edge_tiles(comps, [stiff_ref[0], stiff_ref[2]])
    left_ref[...] = left
    right_ref[...] = right
    for k, rows in enumerate(comps + [stiff_ref[1]]):
        cross_ref[k : k + 1, :] = jnp.where(core == 0, rows[0:1], rows[7:8])


def springs(ends, others, weight, rest, length):
    gaps = [o - e for o, e in zip(others, ends)]
    gaps = [g + r if r != 0.0 else g for g, r in zip(gaps, rest)]
    norm = jnp.sqrt(gaps[0] * gaps[0] + gaps[1] * gaps[1] + gaps[2] * gaps[2])
    factor = length / jnp.maximum(norm, 0.5 * length)
    return [weight * (g * factor - r if r != 0.0 else g * factor) for g, r in zip(gaps, rest)]


def solve_right_side(
    comps, inertial, from_left, from_right, below_rows, above_rows, above_weight, h_ext, b_ext,
    vertical, stiff_ref, inv_ref, base_ref,
):
    row = lax.broadcasted_iota(jnp.int32, (8, CB), 0)
    lane = lax.broadcasted_iota(jnp.int32, (8, 512), 1)
    wide = []
    for k in range(3):
        head = pltpu.roll(from_left, 126 - 2 * k, 1)
        tail = pltpu.roll(from_right, (-2 * k) % 128, 1) if k else from_right
        wide.append(jnp.concatenate([head, comps[k], tail], axis=1))
    total = [jnp.zeros((8, 512), F32)] * 3
    for offset, weight in ((1, h_ext), (2, b_ext)):
        shifted = [pltpu.roll(w, 512 - offset, 1) for w in wide]
        rest = (float(offset), 0.0, 0.0)
        pulls = springs(wide, shifted, weight, rest, float(offset))
        crossing = ((lane >= 128 - offset) & (lane < 128)) | (
            (lane >= 384 - offset) & (lane < 384)
        )
        across = jnp.where(crossing, weight, 0.0)
        for k in range(3):
            here = across * shifted[k] - pulls[k]
            there = across * wide[k] + pulls[k]
            total[k] = total[k] + here + pltpu.roll(there, offset, 1)
    lower = [
        jnp.where(row == 7, below_rows[k], pltpu.roll(comps[k], 7, 0)) for k in range(3)
    ]
    down = springs(comps, lower, vertical, (0.0, 1.0, 0.0), 1.0)
    upper = springs(
        above_rows, [c[0:1] for c in comps], above_weight, (0.0, 1.0, 0.0), 1.0
    )
    below_weight = jnp.where(lax.rem(row, 2) == 1, vertical, 0.0)
    rhs = []
    for k in range(3):
        received = jnp.where(row == 0, upper[k], pltpu.roll(down[k], 1, 0))
        rhs.append(
            inertial[k] + total[k][:, 128:384] + received - down[k] + below_weight * lower[k]
        )
    first = jnp.concatenate(rhs + [jnp.zeros((8, CB), F32)], axis=0)
    second = jnp.concatenate(
        [pltpu.roll(r, 7, 0) for r in rhs] + [jnp.zeros((8, CB), F32)], axis=0
    )
    wide_rhs = stacked(jnp.concatenate([first, second], axis=1))
    base = [jnp.zeros((8, CB), F32)] * 3
    for k in range(4):
        solved = halves_sum(dot_t(wide_rhs, inv_ref[k]))
        for j in range(3):
            part = solved[8 * j : 8 * j + 8]
            base[j] = jnp.where(
                row == 2 * k,
                part[:, :CB],
                jnp.where(row == 2 * k + 1, pltpu.roll(part[:, CB:], 1, 0), base[j]),
            )
    for j in range(3):
        base_ref[j] = base[j]
    weights = stiff_ref[1]
    last = base
    for k in range(1, 4):
        carried = jnp.concatenate(
            [weights * last[j] for j in range(3)] + [jnp.zeros((8, CB), F32)], axis=0
        )
        moved = halves_sum(dot_t(stacked(carried), inv_ref[k, CB:, :CB]))
        last = [
            jnp.where(row == 2 * k + 1, base[j] + pltpu.roll(moved[8 * j : 8 * j + 8], 2, 0), last[j])
            for j in range(3)
        ]
    rows = [(weights * last[j])[7:8] for j in range(3)]
    return jnp.concatenate(rows + [jnp.zeros((5, CB), F32)], axis=0)


def write_offsets(offset, sends_ref, msg_ref):
    core = lax.axis_index("c")
    x = lax.axis_index("x")
    vec = stacked(offset)
    raw = offset[0:3]
    beside = jnp.where(core == 0, apply_map(vec, sends_ref[0], sends_ref[1])[0:3], raw)
    far = apply_map(vec, sends_ref[2], sends_ref[3])[0:3]
    for k in range(4):
        value = jnp.where(high_bit("x") == k // 2, beside, far)
        value = jnp.where(x == k, raw, value)
        msg_ref[2 * k] = value
        msg_ref[2 * k + 1] = value


def offsets_kernel(offset_ref, sends_ref, msg_ref):
    write_offsets(offset_ref[...], sends_ref, msg_ref)


def first_side_kernel(
    u_ref, target_ref, inertia_ref, stiff_ref, pin_ref, left_ref, right_ref, near_ref, cross_ref,
    inv_ref, after_ref, base_ref, offset_ref, inertial_ref, ext_ref, above_ref,
):
    core = lax.axis_index("c")
    y = lax.axis_index("y")
    strip = (lax.axis_index("zh") * 4 + lax.axis_index("zl")) * 8 + lax.axis_index("x") * 2 + core
    comps = [u_ref[k] for k in range(3)]
    row = lax.broadcasted_iota(jnp.int32, (8, CB), 0)
    column = lax.broadcasted_iota(jnp.int32, (8, CB), 1) + y * CB
    hit = column < 0
    for k in range(pin_ref.shape[0]):
        hit = hit | (column == pin_ref[k])
    pinned = hit & (row == 0) & (strip == 0)
    inertial = []
    for k in range(3):
        value = inertia_ref[...] * target_ref[k] + PIN * jnp.where(pinned, comps[k], 0.0)
        inertial.append(value)
        inertial_ref[k] = value
    lane = lax.broadcasted_iota(jnp.int32, (8, 512), 1)
    from_left = left_ref[...]
    extended = []
    for k, channel, offset in ((3, 0, 1), (4, 2, 2)):
        head = pltpu.roll(from_left, 126 - 2 * k, 1)
        weight = jnp.concatenate([head, stiff_ref[channel], jnp.zeros((8, 128), F32)], axis=1)
        low = jnp.where(y == 0, 128, 128 - offset)
        high = jnp.where(y == 3, 384 - offset, 384)
        weight = jnp.where((lane >= low) & (lane < high), weight, 0.0)
        extended.append(weight)
        ext_ref[k - 3] = weight
    near, cross = near_ref[0:4, :], cross_ref[...]
    above = jnp.where(core == 0, cross, near)
    below = jnp.where(core == 0, near, cross)
    above_weight = jnp.where(strip == 0, 0.0, above[3:4])
    above_ref[...] = jnp.broadcast_to(above_weight, (8, CB))
    vertical = jnp.where((row == 7) & (strip == 127), 0.0, stiff_ref[1])
    offset_ref[...] = solve_right_side(
        comps, inertial, from_left, right_ref[...], [below[k : k + 1] for k in range(3)],
        [above[k : k + 1] for k in range(3)], above_weight, extended[0], extended[1], vertical,
        stiff_ref, inv_ref, base_ref,
    )


def second_side_kernel(
    u_ref, stiff_ref, left_ref, right_ref, row_ref, inv_ref, sends_ref, inertial_ref, ext_ref,
    above_ref, base_ref, msg_ref,
):
    core = lax.axis_index("c")
    y = lax.axis_index("y")
    strip = (lax.axis_index("zh") * 4 + lax.axis_index("zl")) * 8 + lax.axis_index("x") * 2 + core
    comps = [u_ref[k] for k in range(3)]
    row = lax.broadcasted_iota(jnp.int32, (8, CB), 0)
    above_weight = above_ref[0:1, :]
    divisor = jnp.where(strip == 0, 1.0, above_weight)
    above_rows = [u_ref[3, k : k + 1, :] / divisor for k in range(3)]
    vertical = jnp.where((row == 7) & (strip == 127), 0.0, stiff_ref[1])
    offset = solve_right_side(
        comps, [inertial_ref[k] for k in range(3)], left_ref[...], right_ref[...],
        [row_ref[k : k + 1, :] for k in range(3)], above_rows, above_weight, ext_ref[0], ext_ref[1],
        vertical, stiff_ref, inv_ref, base_ref,
    )
    write_offsets(offset, sends_ref, msg_ref)


def plane_vectors(got_ref, wh_ref, wl_ref, vec_ref):
    x = lax.axis_index("x")
    sib = x + 1 - 2 * low_bit("x")
    far = 4 - 4 * high_bit("x")
    vec_ref[...] = jnp.zeros(vec_ref.shape, F32)
    put_vector(vec_ref, 0, got_ref[2 * x])
    put_vector(vec_ref, 1, got_ref[2 * x + 1])
    put_vector(vec_ref, 2, got_ref[2 * sib] + got_ref[2 * sib + 1])
    others = (got_ref[far] + got_ref[far + 1]) + (got_ref[far + 2] + got_ref[far + 3])
    put_vector(vec_ref, 3, others)
    return apply_map(vec_ref[...].astype(BF16), wh_ref[...], wl_ref[...])


def send_vectors(total, maps_ref, joint_ref, msg_ref):
    zh = lax.axis_index("zh")
    vec = stacked(total)
    pairs = apply_map(vec, maps_ref[0], maps_ref[1])[0:3]
    near = apply_map(vec, maps_ref[2], maps_ref[3])[0:3]
    far = apply_map(vec, joint_ref[0], joint_ref[1])[0:3]
    far = jnp.where(zh == 0, far, near)
    raw = total[0:3]
    for g in range(4):
        for h in range(2):
            inner = jnp.where(high_bit() == h, raw, pairs)
            value = jnp.where(zh == g, inner, near if g < 2 else far)
            msg_ref[4 * g + 2 * h] = value
            msg_ref[4 * g + 2 * h + 1] = value


def plane_kernel(got_ref, wh_ref, wl_ref, both_ref, vec_ref):
    both_ref[...] = plane_vectors(got_ref, wh_ref, wl_ref, vec_ref)


def plane_send_kernel(got_ref, wh_ref, wl_ref, maps_ref, joint_ref, both_ref, msg_ref, vec_ref):
    both = plane_vectors(got_ref, wh_ref, wl_ref, vec_ref)
    both_ref[...] = both
    send_vectors(both[:, :CB], maps_ref, joint_ref, msg_ref)


def finish(
    got_ref, both_ref, maps_ref, joint_ref, eh_ref, el_ref, stiff_ref, base_ref, inv_ref, vec_ref
):
    zh = lax.axis_index("zh")
    row = lax.broadcasted_iota(jnp.int32, (8, CB), 0)
    none = jnp.zeros((3, CB), F32)
    vec_ref[...] = jnp.zeros(vec_ref.shape, F32)
    first_two = got_ref[4 * zh] + got_ref[4 * zh + 1]
    put_vector(vec_ref, 0, jnp.where(high_bit() == 1, first_two, none))
    sums = [
        (got_ref[4 * g] + got_ref[4 * g + 1]) + (got_ref[4 * g + 2] + got_ref[4 * g + 3])
        for g in range(3)
    ]
    lower = jnp.where(zh >= 1, sums[0], none) + jnp.where(zh >= 2, sums[1], none)
    put_vector(vec_ref, 1, jnp.where(zh == 3, sums[2], lower))
    put_vector(vec_ref, 2, jnp.where(zh == 3, lower, none))
    vec = vec_ref[...].astype(BF16)
    arrived = apply_map(vec[:, :CB], maps_ref[4], maps_ref[5])
    arrived = arrived + apply_map(vec[:, CB : 2 * CB], maps_ref[6], maps_ref[7])
    arrived = arrived + apply_map(vec[:, 2 * CB :], joint_ref[0], joint_ref[1])
    beside = jnp.where(low_bit() == 1, got_ref[4 * zh + 2 * high_bit()], none)
    arrived = arrived + jnp.concatenate([beside, jnp.zeros((5, CB), F32)], axis=0)
    came = both_ref[:, CB:] + apply_map(stacked(arrived), eh_ref[...], el_ref[...])
    weights = stiff_ref[1]
    state = [base_ref[k] for k in range(3)]
    blank = jnp.zeros((8, CB), F32)
    for k in range(4):
        if k == 0:
            source = [jnp.broadcast_to(came[j : j + 1], (8, CB)) for j in range(3)]
        else:
            source = [weights * state[j] for j in range(3)]
        moved = halves_sum(dot_t(stacked(jnp.concatenate(source + [blank], axis=0)), inv_ref[k, :, :CB]))
        for j in range(3):
            part = moved[8 * j : 8 * j + 8]
            state[j] = state[j] + jnp.where(
                row == 2 * k,
                pltpu.roll(part[:, :CB], 1, 0),
                jnp.where(row == 2 * k + 1, pltpu.roll(part[:, CB:], 2, 0), 0.0),
            )
    return state, came


def middle_kernel(
    got_ref, both_ref, maps_ref, joint_ref, eh_ref, el_ref, stiff_ref, base_ref, inv_ref,
    u_ref, left_ref, right_ref, row_ref, vec_ref,
):
    state, came = finish(
        got_ref, both_ref, maps_ref, joint_ref, eh_ref, el_ref, stiff_ref, base_ref, inv_ref, vec_ref
    )
    for k in range(3):
        u_ref[k] = state[k]
    u_ref[3] = came
    left, right = edge_tiles(state, [])
    left_ref[...] = left
    right_ref[...] = right
    row_ref[...] = jnp.concatenate([state[0][0:1], state[1][0:1], state[2][0:1], state[0][0:1]], axis=0)


def final_kernel(
    got_ref, both_ref, maps_ref, joint_ref, eh_ref, el_ref, stiff_ref, base_ref, inv_ref,
    u_ref, vec_ref,
):
    state, came = finish(
        got_ref, both_ref, maps_ref, joint_ref, eh_ref, el_ref, stiff_ref, base_ref, inv_ref, vec_ref
    )
    for k in range(3):
        u_ref[k] = state[k]


def swap(value, axes):
    return lax.all_to_all(value, axes, 0, 0)


def shards(positions, target, inertia, stiffness, pin_columns, inverses):
    smem = pl.BlockSpec(memory_space=pltpu.SMEM)
    anywhere = pl.BlockSpec(memory_space=pl.ANY)

    hbm = pl.BlockSpec(memory_space=pltpu.HBM)
    own_map = call(
        local_map_kernel,
        sds((CB + 8, CB)),
        (inverses, stiffness, positions),
        specs=[hbm] * 3,
        scratch=[
            pltpu.VMEM((4, CB, CB), BF16),
            pltpu.VMEM((3, 8, CB), F32),
            pltpu.VMEM((3, 8, CB), F32),
            pltpu.SemaphoreType.DMA((6,)),
        ],
        flops=10**8,
        limit=WHOLE_VMEM,
    )
    core_maps = lax.all_gather(own_map, "c")
    square = sds((CB, CB))
    chip, near = call(chip_map_kernel, [square, sds((8, CB))], (core_maps,))
    sib_chip = lax.ppermute(chip, "x", [(k, k ^ 1) for k in range(4)])

    tile = sds((8, 128))
    rows = sds((4, CB))
    left, right, cross = call(
        halo_kernel, [tile, tile, rows], (positions, stiffness, chip), specs=[None, None, anywhere]
    )
    to_left = [(1, 0), (2, 1), (3, 2)]
    to_right = [(0, 1), (1, 2), (2, 3)]
    cores = [(0, 1), (1, 0)]
    from_right = lax.ppermute(left, "y", to_left)
    two_chips, cross = call(
        two_chips_kernel,
        [square, rows],
        (chip, sib_chip, cross, from_right),
        specs=[None] * 3 + [anywhere],
    )
    far_chips = lax.ppermute(two_chips, "x", [(k, 3 - k) for k in range(4)])
    pairs = [(2 * k + 1, 2 * k + 2) for k in range(63)]
    cross = lax.ppermute(cross, STRIP, pairs + [(b, a) for a, b in pairs])
    plane, right = call(
        four_chips_kernel,
        [square, tile],
        (two_chips, far_chips, right, cross),
        specs=[None] * 3 + [anywhere],
    )
    beside = lax.ppermute(plane, ZAX, [(k, k ^ 1) for k in range(16)])

    from_left = lax.ppermute(right, "y", to_right)
    half = sds((CB, 128))
    two, two_half = call(
        two_planes_kernel, [square, half], (plane, beside, from_left), specs=[None, None, anywhere]
    )
    two_mine = lax.ppermute(two_half, ZAX, [(k, k ^ 2) for k in range(16)])

    halos = (from_left, from_right, near, cross)
    field = sds((3, 8, CB))
    vector = sds((8, CB))
    base, offset, inertial, ext, above = call(
        first_side_kernel,
        [field, vector, field, sds((2, 8, 512)), vector],
        (positions, target, inertia, stiffness, pin_columns) + halos + (inverses, two),
        specs=[None] * 4 + [smem] + [None] * 5 + [anywhere],
        flops=10**8,
        size=3 * 10**6,
    )
    wide = sds((4 * CB, 2 * CB), BF16)
    narrow = sds((CB, CB), BF16)
    xh, xl, eh, el, sends = call(
        plane_maps_kernel,
        [wide, wide, narrow, narrow, sds((4, CB, CB), BF16)],
        (chip, sib_chip, two_chips, far_chips, core_maps, base),
        specs=[None] * 5 + [anywhere],
        flops=10**9,
    )
    group_half = call(
        four_planes_kernel, half, (two, two_mine, sends), specs=[None, None, anywhere]
    )
    steps = [(4 + k, k) for k in range(4)] + [(8 + k, 12 + k) for k in range(4)]
    far_mine = lax.ppermute(group_half, ZAX, steps)

    msg = call(offsets_kernel, sds((8, 3, CB)), (offset, sends))
    got = swap(msg, PLANE)
    both = call(
        plane_kernel,
        sds((8, 2 * CB)),
        (got, xh, xl),
        scratch=[pltpu.VMEM((16, 4 * CB), F32)],
        size=3 * 10**6,
    )
    mine = call(
        bundle_kernel, sds((2, CB, 128)), (two_mine, far_mine, both), specs=[None, None, anywhere]
    )
    halves = lax.all_gather(mine, "c")
    maps, joint, msg = call(
        group_maps_kernel,
        [sds((8, CB, CB), BF16), sds((2, CB, CB), BF16), sds((16, 3, CB))],
        (both, beside, halves),
        flops=5 * 10**8,
    )
    got = swap(msg, ZAX)
    middle, left, right, low_row = call(
        middle_kernel,
        [sds((4, 8, CB)), tile, tile, rows],
        (got, both, maps, joint, eh, el, stiffness, base, inverses),
        scratch=[pltpu.VMEM((16, 3 * CB), F32)],
        flops=10**8,
    )

    low_row = lax.ppermute(low_row, STRIP, [(k + 1, k) for k in range(127)])
    from_right = lax.ppermute(left, "y", to_left)
    from_left = lax.ppermute(right, "y", to_right)
    base, msg = call(
        second_side_kernel,
        [field, sds((8, 3, CB))],
        (middle, stiffness, from_left, from_right, low_row, inverses, sends)
        + (inertial, ext, above),
        flops=10**8,
        size=3 * 10**6,
    )
    got = swap(msg, PLANE)
    both, msg = call(
        plane_send_kernel,
        [sds((8, 2 * CB)), sds((16, 3, CB))],
        (got, xh, xl, maps, joint),
        scratch=[pltpu.VMEM((16, 4 * CB), F32)],
        size=3 * 10**6,
    )
    got = swap(msg, ZAX)
    return call(
        final_kernel,
        field,
        (got, both, maps, joint, eh, el, stiffness, base, inverses),
        scratch=[pltpu.VMEM((16, 3 * CB), F32)],
        flops=10**8,
    )


def solution(mesh):
    split = Mesh(mesh.devices.reshape(4, 4, 4, 2, 4), ("zh", "zl", "x", "c", "y"))
    return jax.shard_map(
        shards,
        mesh=split,
        in_specs=(
            P(None, STRIP, "y"),
            P(None, STRIP, "y"),
            P(STRIP, "y"),
            P(None, STRIP, "y"),
            P(),
            P(STRIP, None, None),
        ),
        out_specs=P(None, STRIP, "y"),
        check_vma=False,
    )
```

```python
import jax
import jax.numpy as jnp
from jax import lax
from jax.experimental import pallas as pl
from jax.experimental.pallas import tpu as pltpu
from jax.sharding import Mesh
from jax.sharding import PartitionSpec as P

F32 = jnp.float32
BF16 = jnp.bfloat16
STRIP = ("zh", "zl", "x", "c")
ZAX = ("zh", "zl")
PLANE = ("x", "c")
CB = 256
PIN = 20.0
VMEM_LIMIT = 14 * 1024 * 1024
WHOLE_VMEM = 64 * 1024 * 1024 - (64 + 280) * 1024


def dot(a, b):
    return lax.dot_general(a, b, (((1,), (0,)), ((), ())), preferred_element_type=F32)


def dot_t(a, b):
    return lax.dot_general(a, b, (((1,), (1,)), ((), ())), preferred_element_type=F32)


def pair(value):
    high = value.astype(BF16)
    low = (value - high.astype(F32)).astype(BF16)
    return high, low


def mm(a, b):
    return dot(a[0], b[0]) + (dot(a[0], b[1]) + dot(a[1], b[0]))


def eye():
    rows = lax.broadcasted_iota(jnp.int32, (CB, CB), 0)
    cols = lax.broadcasted_iota(jnp.int32, (CB, CB), 1)
    return jnp.where(rows == cols, 1.0, 0.0).astype(F32)


def stacked(value):
    high = value.astype(BF16)
    low = value - high.astype(F32)
    return jnp.concatenate([high.astype(F32), low], axis=0).astype(BF16)


def halves_sum(value):
    half = value.shape[0] // 2
    return value[:half] + value[half:]


def put_vector(vec_ref, slot, value):
    high = value.astype(BF16).astype(F32)
    vec_ref[0:3, slot * CB : (slot + 1) * CB] = high
    vec_ref[8:11, slot * CB : (slot + 1) * CB] = value - high


def apply_map(vec, high, low):
    return halves_sum(dot(vec, high) + dot(vec, low))


def call(kernel, outs, args, specs=None, scratch=(), flops=10**7, size=10**6, limit=VMEM_LIMIT):
    vmem = pl.BlockSpec(memory_space=pltpu.VMEM)
    in_specs = [vmem] * len(args) if specs is None else [vmem if s is None else s for s in specs]
    many = isinstance(outs, (list, tuple))
    out_specs = [vmem] * len(outs) if many else vmem
    return pl.pallas_call(
        kernel,
        out_shape=outs,
        in_specs=in_specs,
        out_specs=out_specs,
        scratch_shapes=list(scratch),
        compiler_params=pltpu.CompilerParams(vmem_limit_bytes=limit),
        cost_estimate=pl.CostEstimate(flops=flops, bytes_accessed=size, transcendentals=0),
    )(*args)


def sds(shape, dtype=F32):
    return jax.ShapeDtypeStruct(shape, dtype)


def local_map_kernel(inv_hbm, stiff_hbm, u_hbm, out_ref, inv_ref, stiff_ref, u_ref, sems):
    copies = [
        pltpu.make_async_copy(stiff_hbm, stiff_ref, sems.at[4]),
        pltpu.make_async_copy(u_hbm, u_ref, sems.at[5]),
    ]
    copies += [
        pltpu.make_async_copy(inv_hbm.at[k, CB : 2 * CB, 0:CB], inv_ref.at[k], sems.at[k])
        for k in range(4)
    ]
    for copy in copies:
        copy.start()
    core = lax.axis_index("c")
    copies[0].wait()
    copies[2].wait()
    first = dot_t(eye().astype(BF16), inv_ref[0]) * stiff_ref[1, 1:2, :]
    for k in range(1, 4):
        copies[2 + k].wait()
        high, low = pair(first)
        first = (dot_t(high, inv_ref[k]) + dot_t(low, inv_ref[k])) * stiff_ref[
            1, 2 * k + 1 : 2 * k + 2, :
        ]
    out_ref[0:CB, :] = first
    copies[1].wait()
    rows = [u_ref[k] for k in range(3)] + [stiff_ref[1]]
    rows = [jnp.where(core == 0, r[7:8], r[0:1]) for r in rows]
    out_ref[CB : CB + 8, :] = jnp.concatenate(rows + rows, axis=0)


def chip_map_kernel(both_ref, out_ref, near_ref):
    core = lax.axis_index("c")
    out_ref[...] = mm(pair(both_ref[0, 0:CB, :]), pair(both_ref[1, 0:CB, :]))
    tails = [both_ref[k, CB : CB + 8, :] for k in range(2)]
    near_ref[...] = jnp.where(core == 0, tails[1], tails[0])


def low_bit(axis="zl"):
    return lax.rem(lax.axis_index(axis), 2)


def high_bit(axis="zl"):
    return lax.div(lax.axis_index(axis), 2)


def in_order(own, other, right):
    return jnp.where(right, other, own), jnp.where(right, own, other)


def two_chips_kernel(own_ref, other_ref, cross_ref, after_ref, out_ref, row_ref):
    left_map, right_map = in_order(own_ref[...], other_ref[...], low_bit("x") == 1)
    out_ref[...] = mm(pair(left_map), pair(right_map))
    row_ref[...] = cross_ref[...]


def four_chips_kernel(own_ref, other_ref, edge_ref, after_ref, out_ref, tile_ref):
    tile_ref[...] = edge_ref[...]
    left_map, right_map = in_order(own_ref[...], other_ref[...], high_bit("x") == 1)
    out_ref[...] = mm(pair(left_map), pair(right_map))


def rows_of_half(half):
    return jnp.concatenate([half[:128], half[128:]], axis=1)


def half_of_rows(rows):
    return jnp.concatenate([rows[:, :128], rows[:, 128:]], axis=0)


def joined(first, second):
    columns = jnp.concatenate([first, second], axis=1)
    rows = jnp.concatenate([rows_of_half(first), rows_of_half(second)], axis=0)
    return jnp.where(high_bit() == 0, columns, rows)


def two_planes_kernel(own_ref, other_ref, *rest):
    out_ref, half_ref = rest[-2:]
    core = lax.axis_index("c")
    left_map, right_map = in_order(own_ref[...], other_ref[...], low_bit() == 1)
    product = mm(pair(left_map), pair(right_map))
    out_ref[...] = product
    columns = jnp.where(core == 0, product[:, :128], product[:, 128:])
    rows = half_of_rows(jnp.where(core == 0, product[:128], product[128:]))
    half_ref[...] = jnp.where(high_bit() == 0, rows, columns)


def four_planes_kernel(own_ref, half_ref, after_ref, out_ref):
    own = pair(own_ref[...])
    half = half_ref[...]
    columns = mm(own, pair(half))
    rows = half_of_rows(mm(pair(rows_of_half(half)), own))
    out_ref[...] = jnp.where(high_bit() == 0, columns, rows)


def plane_maps_kernel(
    own_ref, sib_ref, two_ref, far_ref, cores_ref, after_ref, wh_ref, wl_ref, eh_ref, el_ref, sends_ref
):
    core = lax.axis_index("c")
    one = eye()
    low, high = low_bit("x"), high_bit("x")
    own, sib, two, far = own_ref[...], sib_ref[...], two_ref[...], far_ref[...]
    first, second = cores_ref[0, 0:CB, :], cores_ref[1, 0:CB, :]

    def store(slot, col, value):
        parts = pair(value)
        wh_ref[slot * CB : (slot + 1) * CB, col * CB : (col + 1) * CB] = parts[0]
        wl_ref[slot * CB : (slot + 1) * CB, col * CB : (col + 1) * CB] = parts[1]

    sib_after = jnp.where(low == 0, sib, one)
    rest = pair(jnp.where(high == 0, far, one))
    to_end = mm(pair(sib_after), rest)
    store(0, 0, mm(pair(second), pair(to_end)))
    store(1, 0, to_end)
    store(2, 0, mm(pair(jnp.where(low == 0, one, own)), rest))
    store(3, 0, jnp.where(high == 1, two, one))
    none = jnp.zeros((CB, CB), F32)
    core_before = jnp.where(core == 1, first, one)
    chip_before = mm(pair(jnp.where(low == 1, sib, one)), pair(core_before))
    store(0, 1, jnp.where(core == 1, one, none))
    store(1, 1, none)
    store(2, 1, jnp.where(low == 1, core_before, none))
    store(3, 1, jnp.where(high == 1, chip_before, none))
    parts = pair(mm(pair(jnp.where(high == 1, far, one)), pair(chip_before)))
    eh_ref[...] = parts[0]
    el_ref[...] = parts[1]
    core_after = jnp.where(core == 0, second, one)
    parts = pair(core_after)
    sends_ref[0] = parts[0]
    sends_ref[1] = parts[1]
    parts = pair(mm(parts, pair(sib_after)))
    sends_ref[2] = parts[0]
    sends_ref[3] = parts[1]


def bundle_kernel(two_ref, far_ref, after_ref, out_ref):
    out_ref[0] = two_ref[...]
    out_ref[1] = far_ref[...]


def group_maps_kernel(both_ref, one_ref, halves_ref, out_ref, joint_ref, msg_ref):
    zh = lax.axis_index("zh")
    one = eye()
    sibling = one_ref[...]
    two = pair(joined(halves_ref[0, 0], halves_ref[1, 0]))
    far = joined(halves_ref[0, 1], halves_ref[1, 1])
    send = jnp.where(low_bit() == 0, sibling, one)
    take = jnp.where(low_bit() == 1, sibling, one)
    for k, value in ((0, send), (4, take)):
        parts = pair(value)
        out_ref[k] = parts[0]
        out_ref[k + 1] = parts[1]
    send = jnp.where(high_bit() == 0, mm(pair(send), two), send)
    take = jnp.where(high_bit() == 1, mm(two, pair(take)), take)
    for k, value in ((2, send), (6, take)):
        parts = pair(value)
        out_ref[k] = parts[0]
        out_ref[k + 1] = parts[1]
    left = jnp.where(zh == 0, send, far)
    right = jnp.where(zh == 0, far, take)
    joint = pair(mm(pair(left), pair(right)))
    joint_ref[0] = joint[0]
    joint_ref[1] = joint[1]
    send_vectors(both_ref[:, :CB], out_ref, joint_ref, msg_ref)


def edge_tiles(comps, weights):
    lane = lax.broadcasted_iota(jnp.int32, (8, 128), 1)
    right = jnp.zeros((8, 128), F32)
    left = jnp.zeros((8, 128), F32)
    for k, value in enumerate(comps + weights):
        mask = (lane == 2 * k) | (lane == 2 * k + 1)
        right = jnp.where(mask, pltpu.roll(value[:, 128:], (2 * k - 126) % 128, 1), right)
        if k < 3:
            left = jnp.where(mask, pltpu.roll(value[:, :128], 2 * k, 1), left)
    return left, right


def halo_kernel(u_ref, stiff_ref, after_ref, left_ref, right_ref, cross_ref):
    core = lax.axis_index("c")
    comps = [u_ref[k] for k in range(3)]
    left, right = edge_tiles(comps, [stiff_ref[0], stiff_ref[2]])
    left_ref[...] = left
    right_ref[...] = right
    for k, rows in enumerate(comps + [stiff_ref[1]]):
        cross_ref[k : k + 1, :] = jnp.where(core == 0, rows[0:1], rows[7:8])


def springs(ends, others, weight, rest, length):
    gaps = [o - e for o, e in zip(others, ends)]
    gaps = [g + r if r != 0.0 else g for g, r in zip(gaps, rest)]
    norm = jnp.sqrt(gaps[0] * gaps[0] + gaps[1] * gaps[1] + gaps[2] * gaps[2])
    factor = length / jnp.maximum(norm, 0.5 * length)
    return [weight * (g * factor - r if r != 0.0 else g * factor) for g, r in zip(gaps, rest)]


def solve_right_side(
    comps, inertial, from_left, from_right, below_rows, above_rows, above_weight, h_ext, b_ext,
    vertical, stiff_ref, inv_ref, base_ref,
):
    row = lax.broadcasted_iota(jnp.int32, (8, CB), 0)
    lane = lax.broadcasted_iota(jnp.int32, (8, 512), 1)
    wide = []
    for k in range(3):
        head = pltpu.roll(from_left, 126 - 2 * k, 1)
        tail = pltpu.roll(from_right, (-2 * k) % 128, 1) if k else from_right
        wide.append(jnp.concatenate([head, comps[k], tail], axis=1))
    total = [jnp.zeros((8, 512), F32)] * 3
    for offset, weight in ((1, h_ext), (2, b_ext)):
        shifted = [pltpu.roll(w, 512 - offset, 1) for w in wide]
        rest = (float(offset), 0.0, 0.0)
        pulls = springs(wide, shifted, weight, rest, float(offset))
        crossing = ((lane >= 128 - offset) & (lane < 128)) | (
            (lane >= 384 - offset) & (lane < 384)
        )
        across = jnp.where(crossing, weight, 0.0)
        for k in range(3):
            here = across * shifted[k] - pulls[k]
            there = across * wide[k] + pulls[k]
            total[k] = total[k] + here + pltpu.roll(there, offset, 1)
    lower = [
        jnp.where(row == 7, below_rows[k], pltpu.roll(comps[k], 7, 0)) for k in range(3)
    ]
    down = springs(comps, lower, vertical, (0.0, 1.0, 0.0), 1.0)
    upper = springs(
        above_rows, [c[0:1] for c in comps], above_weight, (0.0, 1.0, 0.0), 1.0
    )
    below_weight = jnp.where(lax.rem(row, 2) == 1, vertical, 0.0)
    rhs = []
    for k in range(3):
        received = jnp.where(row == 0, upper[k], pltpu.roll(down[k], 1, 0))
        rhs.append(
            inertial[k] + total[k][:, 128:384] + received - down[k] + below_weight * lower[k]
        )
    first = jnp.concatenate(rhs + [jnp.zeros((8, CB), F32)], axis=0)
    second = jnp.concatenate(
        [pltpu.roll(r, 7, 0) for r in rhs] + [jnp.zeros((8, CB), F32)], axis=0
    )
    wide_rhs = stacked(jnp.concatenate([first, second], axis=1))
    base = [jnp.zeros((8, CB), F32)] * 3
    for k in range(4):
        solved = halves_sum(dot_t(wide_rhs, inv_ref[k]))
        for j in range(3):
            part = solved[8 * j : 8 * j + 8]
            base[j] = jnp.where(
                row == 2 * k,
                part[:, :CB],
                jnp.where(row == 2 * k + 1, pltpu.roll(part[:, CB:], 1, 0), base[j]),
            )
    for j in range(3):
        base_ref[j] = base[j]
    weights = stiff_ref[1]
    last = base
    for k in range(1, 4):
        carried = jnp.concatenate(
            [weights * last[j] for j in range(3)] + [jnp.zeros((8, CB), F32)], axis=0
        )
        moved = halves_sum(dot_t(stacked(carried), inv_ref[k, CB:, :CB]))
        last = [
            jnp.where(row == 2 * k + 1, base[j] + pltpu.roll(moved[8 * j : 8 * j + 8], 2, 0), last[j])
            for j in range(3)
        ]
    rows = [(weights * last[j])[7:8] for j in range(3)]
    return jnp.concatenate(rows + [jnp.zeros((5, CB), F32)], axis=0)


def write_offsets(offset, sends_ref, msg_ref):
    core = lax.axis_index("c")
    x = lax.axis_index("x")
    vec = stacked(offset)
    raw = offset[0:3]
    beside = jnp.where(core == 0, apply_map(vec, sends_ref[0], sends_ref[1])[0:3], raw)
    far = apply_map(vec, sends_ref[2], sends_ref[3])[0:3]
    for k in range(4):
        value = jnp.where(high_bit("x") == k // 2, beside, far)
        value = jnp.where(x == k, raw, value)
        msg_ref[2 * k] = value
        msg_ref[2 * k + 1] = value


def offsets_kernel(offset_ref, sends_ref, msg_ref):
    write_offsets(offset_ref[...], sends_ref, msg_ref)


def first_side_kernel(
    u_ref, target_ref, inertia_ref, stiff_ref, pin_ref, left_ref, right_ref, near_ref, cross_ref,
    inv_ref, after_ref, base_ref, offset_ref, inertial_ref, ext_ref, above_ref,
):
    core = lax.axis_index("c")
    y = lax.axis_index("y")
    strip = (lax.axis_index("zh") * 4 + lax.axis_index("zl")) * 8 + lax.axis_index("x") * 2 + core
    comps = [u_ref[k] for k in range(3)]
    row = lax.broadcasted_iota(jnp.int32, (8, CB), 0)
    column = lax.broadcasted_iota(jnp.int32, (8, CB), 1) + y * CB
    hit = column < 0
    for k in range(pin_ref.shape[0]):
        hit = hit | (column == pin_ref[k])
    pinned = hit & (row == 0) & (strip == 0)
    inertial = []
    for k in range(3):
        value = inertia_ref[...] * target_ref[k] + PIN * jnp.where(pinned, comps[k], 0.0)
        inertial.append(value)
        inertial_ref[k] = value
    lane = lax.broadcasted_iota(jnp.int32, (8, 512), 1)
    from_left = left_ref[...]
    extended = []
    for k, channel, offset in ((3, 0, 1), (4, 2, 2)):
        head = pltpu.roll(from_left, 126 - 2 * k, 1)
        weight = jnp.concatenate([head, stiff_ref[channel], jnp.zeros((8, 128), F32)], axis=1)
        low = jnp.where(y == 0, 128, 128 - offset)
        high = jnp.where(y == 3, 384 - offset, 384)
        weight = jnp.where((lane >= low) & (lane < high), weight, 0.0)
        extended.append(weight)
        ext_ref[k - 3] = weight
    near, cross = near_ref[0:4, :], cross_ref[...]
    above = jnp.where(core == 0, cross, near)
    below = jnp.where(core == 0, near, cross)
    above_weight = jnp.where(strip == 0, 0.0, above[3:4])
    above_ref[...] = jnp.broadcast_to(above_weight, (8, CB))
    vertical = jnp.where((row == 7) & (strip == 127), 0.0, stiff_ref[1])
    offset_ref[...] = solve_right_side(
        comps, inertial, from_left, right_ref[...], [below[k : k + 1] for k in range(3)],
        [above[k : k + 1] for k in range(3)], above_weight, extended[0], extended[1], vertical,
        stiff_ref, inv_ref, base_ref,
    )


def second_side_kernel(
    u_ref, stiff_ref, row_ref, left_ref, right_ref, inv_ref, sends_ref, inertial_ref, ext_ref,
    above_ref, base_ref, msg_ref,
):
    core = lax.axis_index("c")
    y = lax.axis_index("y")
    strip = (lax.axis_index("zh") * 4 + lax.axis_index("zl")) * 8 + lax.axis_index("x") * 2 + core
    comps = [u_ref[k] for k in range(3)]
    row = lax.broadcasted_iota(jnp.int32, (8, CB), 0)
    above_weight = above_ref[0:1, :]
    divisor = jnp.where(strip == 0, 1.0, above_weight)
    above_rows = [u_ref[3, k : k + 1, :] / divisor for k in range(3)]
    vertical = jnp.where((row == 7) & (strip == 127), 0.0, stiff_ref[1])
    offset = solve_right_side(
        comps, [inertial_ref[k] for k in range(3)], left_ref[...], right_ref[...],
        [row_ref[k : k + 1, :] for k in range(3)], above_rows, above_weight, ext_ref[0], ext_ref[1],
        vertical, stiff_ref, inv_ref, base_ref,
    )
    write_offsets(offset, sends_ref, msg_ref)


def plane_vectors(got_ref, wh_ref, wl_ref, vec_ref):
    x = lax.axis_index("x")
    sib = x + 1 - 2 * low_bit("x")
    far = 4 - 4 * high_bit("x")
    vec_ref[...] = jnp.zeros(vec_ref.shape, F32)
    put_vector(vec_ref, 0, got_ref[2 * x])
    put_vector(vec_ref, 1, got_ref[2 * x + 1])
    put_vector(vec_ref, 2, got_ref[2 * sib] + got_ref[2 * sib + 1])
    others = (got_ref[far] + got_ref[far + 1]) + (got_ref[far + 2] + got_ref[far + 3])
    put_vector(vec_ref, 3, others)
    return apply_map(vec_ref[...].astype(BF16), wh_ref[...], wl_ref[...])


def send_vectors(total, maps_ref, joint_ref, msg_ref):
    zh = lax.axis_index("zh")
    vec = stacked(total)
    pairs = apply_map(vec, maps_ref[0], maps_ref[1])[0:3]
    near = apply_map(vec, maps_ref[2], maps_ref[3])[0:3]
    far = apply_map(vec, joint_ref[0], joint_ref[1])[0:3]
    far = jnp.where(zh == 0, far, near)
    raw = total[0:3]
    for g in range(4):
        for h in range(2):
            inner = jnp.where(high_bit() == h, raw, pairs)
            value = jnp.where(zh == g, inner, near if g < 2 else far)
            msg_ref[4 * g + 2 * h] = value
            msg_ref[4 * g + 2 * h + 1] = value


def plane_kernel(got_ref, wh_ref, wl_ref, both_ref, vec_ref):
    both_ref[...] = plane_vectors(got_ref, wh_ref, wl_ref, vec_ref)


def plane_send_kernel(got_ref, wh_ref, wl_ref, maps_ref, joint_ref, both_ref, msg_ref, vec_ref):
    both = plane_vectors(got_ref, wh_ref, wl_ref, vec_ref)
    both_ref[...] = both
    send_vectors(both[:, :CB], maps_ref, joint_ref, msg_ref)


def finish(
    got_ref, both_ref, maps_ref, joint_ref, eh_ref, el_ref, stiff_ref, base_ref, inv_ref, vec_ref
):
    zh = lax.axis_index("zh")
    row = lax.broadcasted_iota(jnp.int32, (8, CB), 0)
    none = jnp.zeros((3, CB), F32)
    vec_ref[...] = jnp.zeros(vec_ref.shape, F32)
    first_two = got_ref[4 * zh] + got_ref[4 * zh + 1]
    put_vector(vec_ref, 0, jnp.where(high_bit() == 1, first_two, none))
    sums = [
        (got_ref[4 * g] + got_ref[4 * g + 1]) + (got_ref[4 * g + 2] + got_ref[4 * g + 3])
        for g in range(3)
    ]
    lower = jnp.where(zh >= 1, sums[0], none) + jnp.where(zh >= 2, sums[1], none)
    put_vector(vec_ref, 1, jnp.where(zh == 3, sums[2], lower))
    put_vector(vec_ref, 2, jnp.where(zh == 3, lower, none))
    vec = vec_ref[...].astype(BF16)
    arrived = apply_map(vec[:, :CB], maps_ref[4], maps_ref[5])
    arrived = arrived + apply_map(vec[:, CB : 2 * CB], maps_ref[6], maps_ref[7])
    arrived = arrived + apply_map(vec[:, 2 * CB :], joint_ref[0], joint_ref[1])
    beside = jnp.where(low_bit() == 1, got_ref[4 * zh + 2 * high_bit()], none)
    arrived = arrived + jnp.concatenate([beside, jnp.zeros((5, CB), F32)], axis=0)
    came = both_ref[:, CB:] + apply_map(stacked(arrived), eh_ref[...], el_ref[...])
    weights = stiff_ref[1]
    state = [base_ref[k] for k in range(3)]
    blank = jnp.zeros((8, CB), F32)
    for k in range(4):
        if k == 0:
            source = [jnp.broadcast_to(came[j : j + 1], (8, CB)) for j in range(3)]
        else:
            source = [weights * state[j] for j in range(3)]
        moved = halves_sum(dot_t(stacked(jnp.concatenate(source + [blank], axis=0)), inv_ref[k, :, :CB]))
        for j in range(3):
            part = moved[8 * j : 8 * j + 8]
            state[j] = state[j] + jnp.where(
                row == 2 * k,
                pltpu.roll(part[:, :CB], 1, 0),
                jnp.where(row == 2 * k + 1, pltpu.roll(part[:, CB:], 2, 0), 0.0),
            )
    return state, came


def middle_kernel(
    got_ref, both_ref, maps_ref, joint_ref, eh_ref, el_ref, stiff_ref, base_ref, inv_ref,
    u_ref, left_ref, right_ref, row_ref, vec_ref,
):
    state, came = finish(
        got_ref, both_ref, maps_ref, joint_ref, eh_ref, el_ref, stiff_ref, base_ref, inv_ref, vec_ref
    )
    for k in range(3):
        u_ref[k] = state[k]
    u_ref[3] = came
    left, right = edge_tiles(state, [])
    left_ref[...] = left
    right_ref[...] = right
    row_ref[...] = jnp.concatenate([state[0][0:1], state[1][0:1], state[2][0:1], state[0][0:1]], axis=0)


def final_kernel(
    got_ref, both_ref, maps_ref, joint_ref, eh_ref, el_ref, stiff_ref, base_ref, inv_ref,
    u_ref, vec_ref,
):
    state, came = finish(
        got_ref, both_ref, maps_ref, joint_ref, eh_ref, el_ref, stiff_ref, base_ref, inv_ref, vec_ref
    )
    for k in range(3):
        u_ref[k] = state[k]


def swap(value, axes):
    return lax.all_to_all(value, axes, 0, 0)


def shards(positions, target, inertia, stiffness, pin_columns, inverses):
    smem = pl.BlockSpec(memory_space=pltpu.SMEM)
    anywhere = pl.BlockSpec(memory_space=pl.ANY)

    hbm = pl.BlockSpec(memory_space=pltpu.HBM)
    own_map = call(
        local_map_kernel,
        sds((CB + 8, CB)),
        (inverses, stiffness, positions),
        specs=[hbm] * 3,
        scratch=[
            pltpu.VMEM((4, CB, CB), BF16),
            pltpu.VMEM((3, 8, CB), F32),
            pltpu.VMEM((3, 8, CB), F32),
            pltpu.SemaphoreType.DMA((6,)),
        ],
        flops=10**8,
        limit=WHOLE_VMEM,
    )
    core_maps = lax.all_gather(own_map, "c")
    square = sds((CB, CB))
    chip, near = call(chip_map_kernel, [square, sds((8, CB))], (core_maps,))
    sib_chip = lax.ppermute(chip, "x", [(k, k ^ 1) for k in range(4)])

    tile = sds((8, 128))
    rows = sds((4, CB))
    left, right, cross = call(
        halo_kernel, [tile, tile, rows], (positions, stiffness, chip), specs=[None, None, anywhere]
    )
    to_left = [(1, 0), (2, 1), (3, 2)]
    to_right = [(0, 1), (1, 2), (2, 3)]
    cores = [(0, 1), (1, 0)]
    from_right = lax.ppermute(left, "y", to_left)
    two_chips, cross = call(
        two_chips_kernel,
        [square, rows],
        (chip, sib_chip, cross, from_right),
        specs=[None] * 3 + [anywhere],
    )
    far_chips = lax.ppermute(two_chips, "x", [(k, 3 - k) for k in range(4)])
    pairs = [(2 * k + 1, 2 * k + 2) for k in range(63)]
    cross = lax.ppermute(cross, STRIP, pairs + [(b, a) for a, b in pairs])
    plane, right = call(
        four_chips_kernel,
        [square, tile],
        (two_chips, far_chips, right, cross),
        specs=[None] * 3 + [anywhere],
    )
    beside = lax.ppermute(plane, ZAX, [(k, k ^ 1) for k in range(16)])

    from_left = lax.ppermute(right, "y", to_right)
    half = sds((CB, 128))
    two, two_half = call(
        two_planes_kernel, [square, half], (plane, beside, from_left), specs=[None, None, anywhere]
    )
    two_mine = lax.ppermute(two_half, ZAX, [(k, k ^ 2) for k in range(16)])

    halos = (from_left, from_right, near, cross)
    field = sds((3, 8, CB))
    vector = sds((8, CB))
    base, offset, inertial, ext, above = call(
        first_side_kernel,
        [field, vector, field, sds((2, 8, 512)), vector],
        (positions, target, inertia, stiffness, pin_columns) + halos + (inverses, two),
        specs=[None] * 4 + [smem] + [None] * 5 + [anywhere],
        flops=10**8,
        size=3 * 10**6,
    )
    wide = sds((4 * CB, 2 * CB), BF16)
    narrow = sds((CB, CB), BF16)
    xh, xl, eh, el, sends = call(
        plane_maps_kernel,
        [wide, wide, narrow, narrow, sds((4, CB, CB), BF16)],
        (chip, sib_chip, two_chips, far_chips, core_maps, base),
        specs=[None] * 5 + [anywhere],
        flops=10**9,
    )
    group_half = call(
        four_planes_kernel, half, (two, two_mine, sends), specs=[None, None, anywhere]
    )
    steps = [(4 + k, k) for k in range(4)] + [(8 + k, 12 + k) for k in range(4)]
    far_mine = lax.ppermute(group_half, ZAX, steps)

    msg = call(offsets_kernel, sds((8, 3, CB)), (offset, sends))
    got = swap(msg, PLANE)
    both = call(
        plane_kernel,
        sds((8, 2 * CB)),
        (got, xh, xl),
        scratch=[pltpu.VMEM((16, 4 * CB), F32)],
        size=3 * 10**6,
    )
    mine = call(
        bundle_kernel, sds((2, CB, 128)), (two_mine, far_mine, both), specs=[None, None, anywhere]
    )
    halves = lax.all_gather(mine, "c")
    maps, joint, msg = call(
        group_maps_kernel,
        [sds((8, CB, CB), BF16), sds((2, CB, CB), BF16), sds((16, 3, CB))],
        (both, beside, halves),
        flops=5 * 10**8,
    )
    got = swap(msg, ZAX)
    middle, left, right, low_row = call(
        middle_kernel,
        [sds((4, 8, CB)), tile, tile, rows],
        (got, both, maps, joint, eh, el, stiffness, base, inverses),
        scratch=[pltpu.VMEM((16, 3 * CB), F32)],
        flops=10**8,
    )

    low_row = lax.ppermute(low_row, STRIP, [(k + 1, k) for k in range(127)])
    from_right = lax.ppermute(left, "y", to_left)
    from_left = lax.ppermute(right, "y", to_right)
    base, msg = call(
        second_side_kernel,
        [field, sds((8, 3, CB))],
        (middle, stiffness, low_row, from_left, from_right, inverses, sends)
        + (inertial, ext, above),
        flops=10**8,
        size=3 * 10**6,
    )
    got = swap(msg, PLANE)
    both, msg = call(
        plane_send_kernel,
        [sds((8, 2 * CB)), sds((16, 3, CB))],
        (got, xh, xl, maps, joint),
        scratch=[pltpu.VMEM((16, 4 * CB), F32)],
        size=3 * 10**6,
    )
    got = swap(msg, ZAX)
    return call(
        final_kernel,
        field,
        (got, both, maps, joint, eh, el, stiffness, base, inverses),
        scratch=[pltpu.VMEM((16, 3 * CB), F32)],
        flops=10**8,
    )


def solution(mesh):
    split = Mesh(mesh.devices.reshape(4, 4, 4, 2, 4), ("zh", "zl", "x", "c", "y"))
    return jax.shard_map(
        shards,
        mesh=split,
        in_specs=(
            P(None, STRIP, "y"),
            P(None, STRIP, "y"),
            P(STRIP, "y"),
            P(None, STRIP, "y"),
            P(),
            P(STRIP, None, None),
        ),
        out_specs=P(None, STRIP, "y"),
        check_vma=False,
    )
```

```python
import jax
import jax.numpy as jnp
from jax import lax
from jax.experimental import pallas as pl
from jax.experimental.pallas import tpu as pltpu
from jax.sharding import Mesh
from jax.sharding import PartitionSpec as P

F32 = jnp.float32
BF16 = jnp.bfloat16
STRIP = ("zh", "zl", "x", "c")
ZAX = ("zh", "zl")
PLANE = ("x", "c")
CB = 256
PIN = 20.0
VMEM_LIMIT = 14 * 1024 * 1024
WHOLE_VMEM = 64 * 1024 * 1024 - (64 + 280) * 1024


def dot(a, b):
    return lax.dot_general(a, b, (((1,), (0,)), ((), ())), preferred_element_type=F32)


def dot_t(a, b):
    return lax.dot_general(a, b, (((1,), (1,)), ((), ())), preferred_element_type=F32)


def pair(value):
    high = value.astype(BF16)
    low = (value - high.astype(F32)).astype(BF16)
    return high, low


def mm(a, b):
    return dot(a[0], b[0]) + (dot(a[0], b[1]) + dot(a[1], b[0]))


def eye():
    rows = lax.broadcasted_iota(jnp.int32, (CB, CB), 0)
    cols = lax.broadcasted_iota(jnp.int32, (CB, CB), 1)
    return jnp.where(rows == cols, 1.0, 0.0).astype(F32)


def stacked(value):
    high = value.astype(BF16)
    low = value - high.astype(F32)
    return jnp.concatenate([high.astype(F32), low], axis=0).astype(BF16)


def halves_sum(value):
    half = value.shape[0] // 2
    return value[:half] + value[half:]


def put_vector(vec_ref, slot, value):
    high = value.astype(BF16).astype(F32)
    vec_ref[0:3, slot * CB : (slot + 1) * CB] = high
    vec_ref[8:11, slot * CB : (slot + 1) * CB] = value - high


def apply_map(vec, high, low):
    return halves_sum(dot(vec, high) + dot(vec, low))


def call(kernel, outs, args, specs=None, scratch=(), flops=10**7, size=10**6, limit=VMEM_LIMIT):
    vmem = pl.BlockSpec(memory_space=pltpu.VMEM)
    in_specs = [vmem] * len(args) if specs is None else [vmem if s is None else s for s in specs]
    many = isinstance(outs, (list, tuple))
    out_specs = [vmem] * len(outs) if many else vmem
    return pl.pallas_call(
        kernel,
        out_shape=outs,
        in_specs=in_specs,
        out_specs=out_specs,
        scratch_shapes=list(scratch),
        compiler_params=pltpu.CompilerParams(vmem_limit_bytes=limit),
        cost_estimate=pl.CostEstimate(flops=flops, bytes_accessed=size, transcendentals=0),
    )(*args)


def sds(shape, dtype=F32):
    return jax.ShapeDtypeStruct(shape, dtype)


def local_map_kernel(inv_hbm, stiff_hbm, u_hbm, out_ref, inv_ref, stiff_ref, u_ref, sems):
    copies = [
        pltpu.make_async_copy(stiff_hbm, stiff_ref, sems.at[4]),
        pltpu.make_async_copy(u_hbm, u_ref, sems.at[5]),
    ]
    copies += [
        pltpu.make_async_copy(inv_hbm.at[k, CB : 2 * CB, 0:CB], inv_ref.at[k], sems.at[k])
        for k in range(4)
    ]
    for copy in copies:
        copy.start()
    core = lax.axis_index("c")
    copies[0].wait()
    copies[2].wait()
    first = dot_t(eye().astype(BF16), inv_ref[0]) * stiff_ref[1, 1:2, :]
    for k in range(1, 4):
        copies[2 + k].wait()
        high, low = pair(first)
        first = (dot_t(high, inv_ref[k]) + dot_t(low, inv_ref[k])) * stiff_ref[
            1, 2 * k + 1 : 2 * k + 2, :
        ]
    out_ref[0:CB, :] = first
    copies[1].wait()
    rows = [u_ref[k] for k in range(3)] + [stiff_ref[1]]
    rows = [jnp.where(core == 0, r[7:8], r[0:1]) for r in rows]
    out_ref[CB : CB + 8, :] = jnp.concatenate(rows + rows, axis=0)


def chip_map_kernel(both_ref, out_ref, near_ref):
    core = lax.axis_index("c")
    out_ref[...] = mm(pair(both_ref[0, 0:CB, :]), pair(both_ref[1, 0:CB, :]))
    tails = [both_ref[k, CB : CB + 8, :] for k in range(2)]
    near_ref[...] = jnp.where(core == 0, tails[1], tails[0])


def low_bit(axis="zl"):
    return lax.rem(lax.axis_index(axis), 2)


def high_bit(axis="zl"):
    return lax.div(lax.axis_index(axis), 2)


def in_order(own, other, right):
    return jnp.where(right, other, own), jnp.where(right, own, other)


def two_chips_kernel(own_ref, other_ref, cross_ref, after_ref, out_ref, row_ref):
    left_map, right_map = in_order(own_ref[...], other_ref[...], low_bit("x") == 1)
    out_ref[...] = mm(pair(left_map), pair(right_map))
    row_ref[...] = cross_ref[...]


def four_chips_kernel(own_ref, other_ref, edge_ref, after_ref, out_ref, tile_ref):
    tile_ref[...] = edge_ref[...]
    left_map, right_map = in_order(own_ref[...], other_ref[...], high_bit("x") == 1)
    out_ref[...] = mm(pair(left_map), pair(right_map))


def rows_of_half(half):
    return jnp.concatenate([half[:128], half[128:]], axis=1)


def half_of_rows(rows):
    return jnp.concatenate([rows[:, :128], rows[:, 128:]], axis=0)


def joined(first, second):
    columns = jnp.concatenate([first, second], axis=1)
    rows = jnp.concatenate([rows_of_half(first), rows_of_half(second)], axis=0)
    return jnp.where(high_bit() == 0, columns, rows)


def two_planes_kernel(own_ref, other_ref, *rest):
    out_ref, half_ref = rest[-2:]
    core = lax.axis_index("c")
    left_map, right_map = in_order(own_ref[...], other_ref[...], low_bit() == 1)
    product = mm(pair(left_map), pair(right_map))
    out_ref[...] = product
    columns = jnp.where(core == 0, product[:, :128], product[:, 128:])
    rows = half_of_rows(jnp.where(core == 0, product[:128], product[128:]))
    half_ref[...] = jnp.where(high_bit() == 0, rows, columns)


def four_planes_kernel(own_ref, half_ref, after_ref, out_ref):
    own = pair(own_ref[...])
    half = half_ref[...]
    columns = mm(own, pair(half))
    rows = half_of_rows(mm(pair(rows_of_half(half)), own))
    out_ref[...] = jnp.where(high_bit() == 0, columns, rows)


def plane_maps_kernel(
    own_ref, sib_ref, two_ref, far_ref, cores_ref, after_ref, wh_ref, wl_ref, eh_ref, el_ref, sends_ref
):
    core = lax.axis_index("c")
    one = eye()
    low, high = low_bit("x"), high_bit("x")
    own, sib, two, far = own_ref[...], sib_ref[...], two_ref[...], far_ref[...]
    first, second = cores_ref[0, 0:CB, :], cores_ref[1, 0:CB, :]

    def store(slot, col, value):
        parts = pair(value)
        wh_ref[slot * CB : (slot + 1) * CB, col * CB : (col + 1) * CB] = parts[0]
        wl_ref[slot * CB : (slot + 1) * CB, col * CB : (col + 1) * CB] = parts[1]

    sib_after = jnp.where(low == 0, sib, one)
    rest = pair(jnp.where(high == 0, far, one))
    to_end = mm(pair(sib_after), rest)
    store(0, 0, mm(pair(second), pair(to_end)))
    store(1, 0, to_end)
    store(2, 0, mm(pair(jnp.where(low == 0, one, own)), rest))
    store(3, 0, jnp.where(high == 1, two, one))
    none = jnp.zeros((CB, CB), F32)
    core_before = jnp.where(core == 1, first, one)
    chip_before = mm(pair(jnp.where(low == 1, sib, one)), pair(core_before))
    store(0, 1, jnp.where(core == 1, one, none))
    store(1, 1, none)
    store(2, 1, jnp.where(low == 1, core_before, none))
    store(3, 1, jnp.where(high == 1, chip_before, none))
    parts = pair(mm(pair(jnp.where(high == 1, far, one)), pair(chip_before)))
    eh_ref[...] = parts[0]
    el_ref[...] = parts[1]
    core_after = jnp.where(core == 0, second, one)
    parts = pair(core_after)
    sends_ref[0] = parts[0]
    sends_ref[1] = parts[1]
    parts = pair(mm(parts, pair(sib_after)))
    sends_ref[2] = parts[0]
    sends_ref[3] = parts[1]


def bundle_kernel(two_ref, far_ref, after_ref, out_ref):
    out_ref[0] = two_ref[...]
    out_ref[1] = far_ref[...]


def group_maps_kernel(both_ref, one_ref, halves_ref, out_ref, joint_ref, msg_ref):
    zh = lax.axis_index("zh")
    one = eye()
    sibling = one_ref[...]
    two = pair(joined(halves_ref[0, 0], halves_ref[1, 0]))
    far = joined(halves_ref[0, 1], halves_ref[1, 1])
    send = jnp.where(low_bit() == 0, sibling, one)
    take = jnp.where(low_bit() == 1, sibling, one)
    for k, value in ((0, send), (4, take)):
        parts = pair(value)
        out_ref[k] = parts[0]
        out_ref[k + 1] = parts[1]
    send = jnp.where(high_bit() == 0, mm(pair(send), two), send)
    take = jnp.where(high_bit() == 1, mm(two, pair(take)), take)
    for k, value in ((2, send), (6, take)):
        parts = pair(value)
        out_ref[k] = parts[0]
        out_ref[k + 1] = parts[1]
    left = jnp.where(zh == 0, send, far)
    right = jnp.where(zh == 0, far, take)
    joint = pair(mm(pair(left), pair(right)))
    joint_ref[0] = joint[0]
    joint_ref[1] = joint[1]
    send_vectors(both_ref[:, :CB], out_ref, joint_ref, msg_ref)


def edge_tiles(comps, weights):
    lane = lax.broadcasted_iota(jnp.int32, (8, 128), 1)
    right = jnp.zeros((8, 128), F32)
    left = jnp.zeros((8, 128), F32)
    for k, value in enumerate(comps + weights):
        mask = (lane == 2 * k) | (lane == 2 * k + 1)
        right = jnp.where(mask, pltpu.roll(value[:, 128:], (2 * k - 126) % 128, 1), right)
        if k < 3:
            left = jnp.where(mask, pltpu.roll(value[:, :128], 2 * k, 1), left)
    return left, right


def halo_kernel(u_ref, stiff_ref, after_ref, left_ref, right_ref, cross_ref):
    core = lax.axis_index("c")
    comps = [u_ref[k] for k in range(3)]
    left, right = edge_tiles(comps, [stiff_ref[0], stiff_ref[2]])
    left_ref[...] = left
    right_ref[...] = right
    for k, rows in enumerate(comps + [stiff_ref[1]]):
        cross_ref[k : k + 1, :] = jnp.where(core == 0, rows[0:1], rows[7:8])


def springs(ends, others, weight, rest, length):
    gaps = [o - e for o, e in zip(others, ends)]
    gaps = [g + r if r != 0.0 else g for g, r in zip(gaps, rest)]
    norm = jnp.sqrt(gaps[0] * gaps[0] + gaps[1] * gaps[1] + gaps[2] * gaps[2])
    factor = length / jnp.maximum(norm, 0.5 * length)
    return [weight * (g * factor - r if r != 0.0 else g * factor) for g, r in zip(gaps, rest)]


def solve_right_side(
    comps, inertial, from_left, from_right, below_rows, above_rows, above_weight, h_ext, b_ext,
    vertical, stiff_ref, inv_ref, base_ref,
):
    row = lax.broadcasted_iota(jnp.int32, (8, CB), 0)
    lane = lax.broadcasted_iota(jnp.int32, (8, 512), 1)
    wide = []
    for k in range(3):
        head = pltpu.roll(from_left, 126 - 2 * k, 1)
        tail = pltpu.roll(from_right, (-2 * k) % 128, 1) if k else from_right
        wide.append(jnp.concatenate([head, comps[k], tail], axis=1))
    total = [jnp.zeros((8, 512), F32)] * 3
    for offset, weight in ((1, h_ext), (2, b_ext)):
        shifted = [pltpu.roll(w, 512 - offset, 1) for w in wide]
        rest = (float(offset), 0.0, 0.0)
        pulls = springs(wide, shifted, weight, rest, float(offset))
        crossing = ((lane >= 128 - offset) & (lane < 128)) | (
            (lane >= 384 - offset) & (lane < 384)
        )
        across = jnp.where(crossing, weight, 0.0)
        for k in range(3):
            here = across * shifted[k] - pulls[k]
            there = across * wide[k] + pulls[k]
            total[k] = total[k] + here + pltpu.roll(there, offset, 1)
    lower = [
        jnp.where(row == 7, below_rows[k], pltpu.roll(comps[k], 7, 0)) for k in range(3)
    ]
    down = springs(comps, lower, vertical, (0.0, 1.0, 0.0), 1.0)
    upper = springs(
        above_rows, [c[0:1] for c in comps], above_weight, (0.0, 1.0, 0.0), 1.0
    )
    below_weight = jnp.where(lax.rem(row, 2) == 1, vertical, 0.0)
    rhs = []
    for k in range(3):
        received = jnp.where(row == 0, upper[k], pltpu.roll(down[k], 1, 0))
        rhs.append(
            inertial[k] + total[k][:, 128:384] + received - down[k] + below_weight * lower[k]
        )
    first = jnp.concatenate(rhs + [jnp.zeros((8, CB), F32)], axis=0)
    second = jnp.concatenate(
        [pltpu.roll(r, 7, 0) for r in rhs] + [jnp.zeros((8, CB), F32)], axis=0
    )
    wide_rhs = stacked(jnp.concatenate([first, second], axis=1))
    base = [jnp.zeros((8, CB), F32)] * 3
    for k in range(4):
        solved = halves_sum(dot_t(wide_rhs, inv_ref[k]))
        for j in range(3):
            part = solved[8 * j : 8 * j + 8]
            base[j] = jnp.where(
                row == 2 * k,
                part[:, :CB],
                jnp.where(row == 2 * k + 1, pltpu.roll(part[:, CB:], 1, 0), base[j]),
            )
    for j in range(3):
        base_ref[j] = base[j]
    weights = stiff_ref[1]
    last = base
    for k in range(1, 4):
        carried = jnp.concatenate(
            [weights * last[j] for j in range(3)] + [jnp.zeros((8, CB), F32)], axis=0
        )
        moved = halves_sum(dot_t(stacked(carried), inv_ref[k, CB:, :CB]))
        last = [
            jnp.where(row == 2 * k + 1, base[j] + pltpu.roll(moved[8 * j : 8 * j + 8], 2, 0), last[j])
            for j in range(3)
        ]
    rows = [(weights * last[j])[7:8] for j in range(3)]
    return jnp.concatenate(rows + [jnp.zeros((5, CB), F32)], axis=0)


def write_offsets(offset, sends_ref, msg_ref):
    core = lax.axis_index("c")
    x = lax.axis_index("x")
    vec = stacked(offset)
    raw = offset[0:3]
    beside = jnp.where(core == 0, apply_map(vec, sends_ref[0], sends_ref[1])[0:3], raw)
    far = apply_map(vec, sends_ref[2], sends_ref[3])[0:3]
    for k in range(4):
        value = jnp.where(high_bit("x") == k // 2, beside, far)
        value = jnp.where(x == k, raw, value)
        msg_ref[2 * k] = value
        msg_ref[2 * k + 1] = value


def offsets_kernel(offset_ref, sends_ref, msg_ref):
    write_offsets(offset_ref[...], sends_ref, msg_ref)


def first_side_kernel(
    u_ref, target_ref, inertia_ref, stiff_ref, pin_ref, left_ref, right_ref, near_ref, cross_ref,
    inv_ref, after_ref, base_ref, offset_ref, inertial_ref, ext_ref, above_ref,
):
    core = lax.axis_index("c")
    y = lax.axis_index("y")
    strip = (lax.axis_index("zh") * 4 + lax.axis_index("zl")) * 8 + lax.axis_index("x") * 2 + core
    comps = [u_ref[k] for k in range(3)]
    row = lax.broadcasted_iota(jnp.int32, (8, CB), 0)
    column = lax.broadcasted_iota(jnp.int32, (8, CB), 1) + y * CB
    hit = column < 0
    for k in range(pin_ref.shape[0]):
        hit = hit | (column == pin_ref[k])
    pinned = hit & (row == 0) & (strip == 0)
    inertial = []
    for k in range(3):
        value = inertia_ref[...] * target_ref[k] + PIN * jnp.where(pinned, comps[k], 0.0)
        inertial.append(value)
        inertial_ref[k] = value
    lane = lax.broadcasted_iota(jnp.int32, (8, 512), 1)
    from_left = left_ref[...]
    extended = []
    for k, channel, offset in ((3, 0, 1), (4, 2, 2)):
        head = pltpu.roll(from_left, 126 - 2 * k, 1)
        weight = jnp.concatenate([head, stiff_ref[channel], jnp.zeros((8, 128), F32)], axis=1)
        low = jnp.where(y == 0, 128, 128 - offset)
        high = jnp.where(y == 3, 384 - offset, 384)
        weight = jnp.where((lane >= low) & (lane < high), weight, 0.0)
        extended.append(weight)
        ext_ref[k - 3] = weight
    near, cross = near_ref[0:4, :], cross_ref[...]
    above = jnp.where(core == 0, cross, near)
    below = jnp.where(core == 0, near, cross)
    above_weight = jnp.where(strip == 0, 0.0, above[3:4])
    above_ref[...] = jnp.broadcast_to(above_weight, (8, CB))
    vertical = jnp.where((row == 7) & (strip == 127), 0.0, stiff_ref[1])
    offset_ref[...] = solve_right_side(
        comps, inertial, from_left, right_ref[...], [below[k : k + 1] for k in range(3)],
        [above[k : k + 1] for k in range(3)], above_weight, extended[0], extended[1], vertical,
        stiff_ref, inv_ref, base_ref,
    )


def second_side_kernel(
    u_ref, stiff_ref, left_ref, right_ref, row_ref, inv_ref, sends_ref, inertial_ref, ext_ref,
    above_ref, base_ref, msg_ref,
):
    core = lax.axis_index("c")
    y = lax.axis_index("y")
    strip = (lax.axis_index("zh") * 4 + lax.axis_index("zl")) * 8 + lax.axis_index("x") * 2 + core
    comps = [u_ref[k] for k in range(3)]
    row = lax.broadcasted_iota(jnp.int32, (8, CB), 0)
    above_weight = above_ref[0:1, :]
    divisor = jnp.where(strip == 0, 1.0, above_weight)
    above_rows = [u_ref[3, k : k + 1, :] / divisor for k in range(3)]
    vertical = jnp.where((row == 7) & (strip == 127), 0.0, stiff_ref[1])
    offset = solve_right_side(
        comps, [inertial_ref[k] for k in range(3)], left_ref[...], right_ref[...],
        [row_ref[k : k + 1, :] for k in range(3)], above_rows, above_weight, ext_ref[0], ext_ref[1],
        vertical, stiff_ref, inv_ref, base_ref,
    )
    write_offsets(offset, sends_ref, msg_ref)


def plane_vectors(got_ref, wh_ref, wl_ref, vec_ref):
    x = lax.axis_index("x")
    sib = x + 1 - 2 * low_bit("x")
    far = 4 - 4 * high_bit("x")
    vec_ref[...] = jnp.zeros(vec_ref.shape, F32)
    put_vector(vec_ref, 0, got_ref[2 * x])
    put_vector(vec_ref, 1, got_ref[2 * x + 1])
    put_vector(vec_ref, 2, got_ref[2 * sib] + got_ref[2 * sib + 1])
    others = (got_ref[far] + got_ref[far + 1]) + (got_ref[far + 2] + got_ref[far + 3])
    put_vector(vec_ref, 3, others)
    return apply_map(vec_ref[...].astype(BF16), wh_ref[...], wl_ref[...])


def send_vectors(total, maps_ref, joint_ref, msg_ref):
    zh = lax.axis_index("zh")
    vec = stacked(total)
    pairs = apply_map(vec, maps_ref[0], maps_ref[1])[0:3]
    near = apply_map(vec, maps_ref[2], maps_ref[3])[0:3]
    far = apply_map(vec, joint_ref[0], joint_ref[1])[0:3]
    far = jnp.where(zh == 0, far, near)
    raw = total[0:3]
    for g in range(4):
        for h in range(2):
            inner = jnp.where(high_bit() == h, raw, pairs)
            value = jnp.where(zh == g, inner, near if g < 2 else far)
            msg_ref[4 * g + 2 * h] = value
            msg_ref[4 * g + 2 * h + 1] = value


def plane_kernel(got_ref, wh_ref, wl_ref, both_ref, vec_ref):
    both_ref[...] = plane_vectors(got_ref, wh_ref, wl_ref, vec_ref)


def plane_send_kernel(got_ref, wh_ref, wl_ref, maps_ref, joint_ref, both_ref, msg_ref, vec_ref):
    both = plane_vectors(got_ref, wh_ref, wl_ref, vec_ref)
    both_ref[...] = both
    send_vectors(both[:, :CB], maps_ref, joint_ref, msg_ref)


def finish(
    got_ref, both_ref, maps_ref, joint_ref, eh_ref, el_ref, stiff_ref, base_ref, inv_ref, vec_ref
):
    zh = lax.axis_index("zh")
    row = lax.broadcasted_iota(jnp.int32, (8, CB), 0)
    none = jnp.zeros((3, CB), F32)
    vec_ref[...] = jnp.zeros(vec_ref.shape, F32)
    first_two = got_ref[4 * zh] + got_ref[4 * zh + 1]
    put_vector(vec_ref, 0, jnp.where(high_bit() == 1, first_two, none))
    sums = [
        (got_ref[4 * g] + got_ref[4 * g + 1]) + (got_ref[4 * g + 2] + got_ref[4 * g + 3])
        for g in range(3)
    ]
    lower = jnp.where(zh >= 1, sums[0], none) + jnp.where(zh >= 2, sums[1], none)
    put_vector(vec_ref, 1, jnp.where(zh == 3, sums[2], lower))
    put_vector(vec_ref, 2, jnp.where(zh == 3, lower, none))
    vec = vec_ref[...].astype(BF16)
    arrived = apply_map(vec[:, :CB], maps_ref[4], maps_ref[5])
    arrived = arrived + apply_map(vec[:, CB : 2 * CB], maps_ref[6], maps_ref[7])
    arrived = arrived + apply_map(vec[:, 2 * CB :], joint_ref[0], joint_ref[1])
    beside = jnp.where(low_bit() == 1, got_ref[4 * zh + 2 * high_bit()], none)
    arrived = arrived + jnp.concatenate([beside, jnp.zeros((5, CB), F32)], axis=0)
    came = both_ref[:, CB:] + apply_map(stacked(arrived), eh_ref[...], el_ref[...])
    weights = stiff_ref[1]
    state = [base_ref[k] for k in range(3)]
    blank = jnp.zeros((8, CB), F32)
    for k in range(4):
        if k == 0:
            source = [jnp.broadcast_to(came[j : j + 1], (8, CB)) for j in range(3)]
        else:
            source = [weights * state[j] for j in range(3)]
        moved = halves_sum(dot_t(stacked(jnp.concatenate(source + [blank], axis=0)), inv_ref[k, :, :CB]))
        for j in range(3):
            part = moved[8 * j : 8 * j + 8]
            state[j] = state[j] + jnp.where(
                row == 2 * k,
                pltpu.roll(part[:, :CB], 1, 0),
                jnp.where(row == 2 * k + 1, pltpu.roll(part[:, CB:], 2, 0), 0.0),
            )
    return state, came


def middle_kernel(
    got_ref, both_ref, maps_ref, joint_ref, eh_ref, el_ref, stiff_ref, base_ref, inv_ref,
    u_ref, row_ref, vec_ref,
):
    state, came = finish(
        got_ref, both_ref, maps_ref, joint_ref, eh_ref, el_ref, stiff_ref, base_ref, inv_ref, vec_ref
    )
    for k in range(3):
        u_ref[k] = state[k]
    u_ref[3] = came
    row_ref[...] = jnp.concatenate([state[0][0:1], state[1][0:1], state[2][0:1], state[0][0:1]], axis=0)


def edges_kernel(u_ref, left_ref, right_ref):
    left, right = edge_tiles([u_ref[k] for k in range(3)], [])
    left_ref[...] = left
    right_ref[...] = right


def final_kernel(
    got_ref, both_ref, maps_ref, joint_ref, eh_ref, el_ref, stiff_ref, base_ref, inv_ref,
    u_ref, vec_ref,
):
    state, came = finish(
        got_ref, both_ref, maps_ref, joint_ref, eh_ref, el_ref, stiff_ref, base_ref, inv_ref, vec_ref
    )
    for k in range(3):
        u_ref[k] = state[k]


def swap(value, axes):
    return lax.all_to_all(value, axes, 0, 0)


def shards(positions, target, inertia, stiffness, pin_columns, inverses):
    smem = pl.BlockSpec(memory_space=pltpu.SMEM)
    anywhere = pl.BlockSpec(memory_space=pl.ANY)

    hbm = pl.BlockSpec(memory_space=pltpu.HBM)
    own_map = call(
        local_map_kernel,
        sds((CB + 8, CB)),
        (inverses, stiffness, positions),
        specs=[hbm] * 3,
        scratch=[
            pltpu.VMEM((4, CB, CB), BF16),
            pltpu.VMEM((3, 8, CB), F32),
            pltpu.VMEM((3, 8, CB), F32),
            pltpu.SemaphoreType.DMA((6,)),
        ],
        flops=10**8,
        limit=WHOLE_VMEM,
    )
    core_maps = lax.all_gather(own_map, "c")
    square = sds((CB, CB))
    chip, near = call(chip_map_kernel, [square, sds((8, CB))], (core_maps,))
    sib_chip = lax.ppermute(chip, "x", [(k, k ^ 1) for k in range(4)])

    tile = sds((8, 128))
    rows = sds((4, CB))
    left, right, cross = call(
        halo_kernel, [tile, tile, rows], (positions, stiffness, chip), specs=[None, None, anywhere]
    )
    to_left = [(1, 0), (2, 1), (3, 2)]
    to_right = [(0, 1), (1, 2), (2, 3)]
    cores = [(0, 1), (1, 0)]
    from_right = lax.ppermute(left, "y", to_left)
    two_chips, cross = call(
        two_chips_kernel,
        [square, rows],
        (chip, sib_chip, cross, from_right),
        specs=[None] * 3 + [anywhere],
    )
    far_chips = lax.ppermute(two_chips, "x", [(k, 3 - k) for k in range(4)])
    pairs = [(2 * k + 1, 2 * k + 2) for k in range(63)]
    cross = lax.ppermute(cross, STRIP, pairs + [(b, a) for a, b in pairs])
    plane, right = call(
        four_chips_kernel,
        [square, tile],
        (two_chips, far_chips, right, cross),
        specs=[None] * 3 + [anywhere],
    )
    beside = lax.ppermute(plane, ZAX, [(k, k ^ 1) for k in range(16)])

    from_left = lax.ppermute(right, "y", to_right)
    half = sds((CB, 128))
    two, two_half = call(
        two_planes_kernel, [square, half], (plane, beside, from_left), specs=[None, None, anywhere]
    )
    two_mine = lax.ppermute(two_half, ZAX, [(k, k ^ 2) for k in range(16)])

    halos = (from_left, from_right, near, cross)
    field = sds((3, 8, CB))
    vector = sds((8, CB))
    base, offset, inertial, ext, above = call(
        first_side_kernel,
        [field, vector, field, sds((2, 8, 512)), vector],
        (positions, target, inertia, stiffness, pin_columns) + halos + (inverses, two),
        specs=[None] * 4 + [smem] + [None] * 5 + [anywhere],
        flops=10**8,
        size=3 * 10**6,
    )
    wide = sds((4 * CB, 2 * CB), BF16)
    narrow = sds((CB, CB), BF16)
    xh, xl, eh, el, sends = call(
        plane_maps_kernel,
        [wide, wide, narrow, narrow, sds((4, CB, CB), BF16)],
        (chip, sib_chip, two_chips, far_chips, core_maps, base),
        specs=[None] * 5 + [anywhere],
        flops=10**9,
    )
    group_half = call(
        four_planes_kernel, half, (two, two_mine, sends), specs=[None, None, anywhere]
    )
    steps = [(4 + k, k) for k in range(4)] + [(8 + k, 12 + k) for k in range(4)]
    far_mine = lax.ppermute(group_half, ZAX, steps)

    msg = call(offsets_kernel, sds((8, 3, CB)), (offset, sends))
    got = swap(msg, PLANE)
    both = call(
        plane_kernel,
        sds((8, 2 * CB)),
        (got, xh, xl),
        scratch=[pltpu.VMEM((16, 4 * CB), F32)],
        size=3 * 10**6,
    )
    mine = call(
        bundle_kernel, sds((2, CB, 128)), (two_mine, far_mine, both), specs=[None, None, anywhere]
    )
    halves = lax.all_gather(mine, "c")
    maps, joint, msg = call(
        group_maps_kernel,
        [sds((8, CB, CB), BF16), sds((2, CB, CB), BF16), sds((16, 3, CB))],
        (both, beside, halves),
        flops=5 * 10**8,
    )
    got = swap(msg, ZAX)
    middle, low_row = call(
        middle_kernel,
        [sds((4, 8, CB)), rows],
        (got, both, maps, joint, eh, el, stiffness, base, inverses),
        scratch=[pltpu.VMEM((16, 3 * CB), F32)],
        flops=10**8,
    )

    low_row = lax.ppermute(low_row, STRIP, [(k + 1, k) for k in range(127)])
    left, right = call(edges_kernel, [tile, tile], (middle,))
    from_right = lax.ppermute(left, "y", to_left)
    from_left = lax.ppermute(right, "y", to_right)
    base, msg = call(
        second_side_kernel,
        [field, sds((8, 3, CB))],
        (middle, stiffness, from_left, from_right, low_row, inverses, sends)
        + (inertial, ext, above),
        flops=10**8,
        size=3 * 10**6,
    )
    got = swap(msg, PLANE)
    both, msg = call(
        plane_send_kernel,
        [sds((8, 2 * CB)), sds((16, 3, CB))],
        (got, xh, xl, maps, joint),
        scratch=[pltpu.VMEM((16, 4 * CB), F32)],
        size=3 * 10**6,
    )
    got = swap(msg, ZAX)
    return call(
        final_kernel,
        field,
        (got, both, maps, joint, eh, el, stiffness, base, inverses),
        scratch=[pltpu.VMEM((16, 3 * CB), F32)],
        flops=10**8,
    )


def solution(mesh):
    split = Mesh(mesh.devices.reshape(4, 4, 4, 2, 4), ("zh", "zl", "x", "c", "y"))
    return jax.shard_map(
        shards,
        mesh=split,
        in_specs=(
            P(None, STRIP, "y"),
            P(None, STRIP, "y"),
            P(STRIP, "y"),
            P(None, STRIP, "y"),
            P(),
            P(STRIP, None, None),
        ),
        out_specs=P(None, STRIP, "y"),
        check_vma=False,
    )
```
